32 devices in a mesh: group: 2 (over y), expert: 8 (over z, x), dp: 2 (over core).
Axes of the slice: x: 2, y: 2, z: 4, core: 2. Of those that a mesh axis runs over, the one named last changes fastest.
Arguments:
- tokens: bfloat16 [2048, 2048], P(('group', 'expert', 'dp')), parts along dimension 0, may hold values from -6 to 6
- out_grad: bfloat16 [2048, 2048], P(('group', 'expert', 'dp')), parts along dimension 0, may hold values from -6 to 6
- expert_ids: int32 [2048, 8], P(('group', 'expert', 'dp')), parts along dimension 0, may hold values from 0 to 15, all different within a row; in each aligned block of 64 rows (0 to 63, 64 to 127, ...) at most 40 rows name the same one
- route_weight: bfloat16 [2048, 8], P(('group', 'expert', 'dp')), parts along dimension 0, may hold values from 0.019897461 to 0.3984375
- gate_weight: bfloat16 [16, 2048, 384], P('expert', 'dp'), may hold values from -0.125 to 0.125
- up_weight: bfloat16 [16, 2048, 384], P('expert', 'dp'), may hold values from -0.125 to 0.125
- down_weight: bfloat16 [16, 2048, 384], P('expert', 'dp'), may hold values from -0.3125 to 0.3125
- adapter_in: bfloat16 [16, 16, 384], P('expert'), may hold values from -0.3125 to 0.3125
- adapter_out: bfloat16 [16, 16, 2048], P('expert'), may hold values from -0.125 to 0.125
Outputs:
- grad_tokens: bfloat16 [2048, 2048], P(('group', 'expert', 'dp')), parts along dimension 0
- grad_adapter_in: float32 [32, 16, 384], P(('group', 'expert'), None, 'dp'), parts along dimension 0
- grad_adapter_out: float32 [32, 16, 2048], P(('group', 'expert'), None, 'dp'), parts along dimension 0
The draws below stay inside these ranges and needn't reach their ends.
There are 2 independent parts, one for each index of `group`. The reference program is written for one: setup_inputs(seed, part) draws one part's arguments, and reference() takes and returns one part's arrays. A program takes and returns all parts, laid end to end along the dimension named above; an argument that names none is the same for every part. Nothing has to cross between parts.
Inputs may be any that keep to these rules, and one draw needn't show every extreme that they name: `expert_ids`: each token names 8 different experts. Within each aligned block of 64 tokens (the tokens of one device) no expert is named more than 40 times, and some block reaches 40.
All inputs are finite; a program needn't handle non-finite values.
Results may differ from the reference program's by a relative error of at most 0.006.
Values may be sent and summed in bfloat16 or wider, within the bound.
No kernel may reach another device: no remote copies, remote signals or barrier semaphores. Data moves between devices by JAX's collectives and lax.ppermute only.
A program may use at most 128 MiB of HBM per device.

```python
import math
import jax
import jax.numpy as jnp
import numpy as np
from jax import lax

D = 2048
H = 384
R = 16
TOP = 8
TOK_DEV = 64
EXPERTS = 16
MOST = 40
TOKENS = 1024


def levels(own_key, shape, shards, low, top_value):
    gain = 1.0
    for axis_at, shards_of in shards:
        steps = jax.random.uniform(jax.random.fold_in(jax.random.fold_in(own_key, 6), axis_at), (shards_of,), jnp.float32, low / len(shards), top_value / len(shards))
        gain = gain * jnp.repeat(jnp.exp(steps), shape[axis_at] // shards_of).reshape((-1,) + (1,) * (len(shape) - 1 - axis_at))
    return gain


def shared_out(key, own, number, rows, number_of, top, most, slope):
    ranking = jax.random.permutation(key, number_of)
    heavy_load, usual = portions_of(number_of, rows * top, most, slope, True), portions_of(number_of, rows * top, most, slope, False)
    places = jnp.arange(number_of)

    def named(tallies, offset_by):
        used = int((tallies > 0).sum())
        fixed = max(1, used // 4)
        moved = fixed + (places - fixed + offset_by * (used - fixed)) % max(1, number_of - fixed)
        return jnp.zeros((number_of,), jnp.int32).at[ranking[jnp.where(places < fixed, places, moved)]].set(jnp.asarray(tallies, jnp.int32))

    tallies = jnp.where(number % 4 == 0, named(heavy_load, number // 4), named(usual, number - number // 4 - 1))
    mixed = jax.random.permutation(jax.random.fold_in(own, 3), number_of)
    donor, sink = mixed[0:number_of // 2 * 2:2], mixed[1:number_of // 2 * 2:2]
    margin = jnp.minimum(tallies[donor] - 1, most - tallies[sink]) // 2
    margin = jnp.where((donor == ranking[0]) | (sink == ranking[0]) | (tallies[sink] == 0), 0, jnp.maximum(margin, 0))
    moved = jax.random.randint(jax.random.fold_in(own, 4), (number_of // 2,), 0, 1 << 20) % (margin + 1)
    tallies = tallies.at[donor].add(-moved).at[sink].add(moved)
    members = jnp.searchsorted(jnp.cumsum(tallies), jnp.arange(rows * top), side="right").astype(jnp.int32)
    grid = members.reshape(top, rows).T
    grid = grid[jax.random.permutation(jax.random.fold_in(own, 1), rows)]
    offset_by = jax.random.randint(jax.random.fold_in(own, 2), (rows, 1), 0, top)
    return jnp.take_along_axis(grid, (jnp.arange(top)[None, :] + offset_by) % top, axis=1)


def portions_of(count, total, bound, lean, full):
    portions = [(1 << 20) // math.isqrt(grade ** lean) + 1 for grade in range(1, count + 1)]
    largest = bound if full else min(bound, max(-(-total // count), total * portions[0] // sum(portions)))
    least = 1 if total - largest >= count - 1 else 0
    holding, rest = [largest] + [least] * (count - 1), total - largest - least * (count - 1)
    while rest > 0:
        free = [i for i in range(1, count) if holding[i] < largest] or [i for i in range(1, count) if holding[i] < bound]
        pool, left = sum([portions[i] for i in free]), rest
        for i in free:
            extra = min(bound - holding[i], max(1, left * portions[i] // pool), rest)
            holding[i] = holding[i] + extra
            rest = rest - extra
    return np.array(holding)


def bell_draw(own_key, shape, deviation, most, pieces=(), kind=jnp.bfloat16):
    level = levels(own_key, shape, pieces, -0.22, 0.18) if pieces else 1.0
    entries = jax.random.normal(own_key, shape, jnp.float32) * deviation * level
    return jnp.minimum(jnp.maximum(entries, -most), most).astype(kind)


def setup_inputs(seed: int = 0, part: int = 0) -> dict:
    splits = jax.random.split(jax.random.key(seed), 10)
    own_keys = jax.random.split(jax.random.fold_in(splits[9], part), 10)
    tokens = bell_draw(own_keys[0], (TOKENS, D), 1.0, 6.0, ((0, 16),))
    out_grad = bell_draw(own_keys[1], (TOKENS, D), 1.0, 6.0, ((0, 16),))
    expert_ids_keys = jax.random.split(jax.random.fold_in(own_keys[2], 1), TOKENS // TOK_DEV)
    expert_ids_turns = jax.random.permutation(jax.random.fold_in(own_keys[2], 3), TOKENS // TOK_DEV)
    expert_ids = jax.vmap(lambda own, number: shared_out(jax.random.fold_in(own_keys[2], 2), own, number, TOK_DEV, EXPERTS, TOP, MOST, 2))(expert_ids_keys, expert_ids_turns).reshape((TOKENS, TOP))
    route_weight = jnp.clip(jnp.exp(math.log(0.3984375) - 2.9969585 * jax.random.uniform(own_keys[3], (TOKENS, TOP), jnp.float32) ** levels(own_keys[3], (TOKENS, TOP), ((0, 16),), -0.2, 0.2)), 0.019897461, 0.3984375).astype(jnp.bfloat16)
    gate_weight = bell_draw(splits[4], (EXPERTS, D, H), D ** -0.5, 0.125, ((0, 8), (1, 2)))
    up_weight = bell_draw(splits[5], (EXPERTS, D, H), D ** -0.5, 0.125, ((0, 8), (1, 2)))
    down_weight = bell_draw(splits[6], (EXPERTS, D, H), H ** -0.5, 0.3125, ((0, 8), (1, 2)))
    adapter_in = bell_draw(splits[7], (EXPERTS, R, H), H ** -0.5, 0.3125, ((0, 8),))
    adapter_out = bell_draw(splits[8], (EXPERTS, R, D), D ** -0.5, 0.125, ((0, 8),))
    return {"tokens": tokens, "out_grad": out_grad, "expert_ids": expert_ids, "route_weight": route_weight, "gate_weight": gate_weight, "up_weight": up_weight, "down_weight": down_weight, "adapter_in": adapter_in, "adapter_out": adapter_out}


adapter_scale = 2.0


def silu_parts(gate_pre):
    logistic = jax.nn.sigmoid(gate_pre)
    return gate_pre * logistic, logistic * (1.0 + gate_pre * (1.0 - logistic))


def backward_rows(tokens_in, grad_in, weight_in, w_gate, w_up, w_down, factor_in, factor_out):
    gate_pre = jnp.dot(tokens_in, w_gate, preferred_element_type=jnp.float32)
    up_pre = jnp.dot(tokens_in, w_up, preferred_element_type=jnp.float32)
    activation, derivative = silu_parts(gate_pre)
    hidden = (activation * up_pre).astype(jnp.bfloat16)
    route_scale = weight_in.astype(jnp.float32)[:, None]
    low_rank = jnp.dot(hidden, factor_in.T, preferred_element_type=jnp.float32)
    low_scaled = (route_scale * low_rank).astype(jnp.bfloat16)
    adapter_back = jnp.dot(grad_in, factor_out.T, preferred_element_type=jnp.float32).astype(jnp.bfloat16)
    back_scaled = (route_scale * adapter_back.astype(jnp.float32)).astype(jnp.bfloat16)
    grad_hidden = route_scale * (jnp.dot(grad_in, w_down, preferred_element_type=jnp.float32)
                                 + adapter_scale * jnp.dot(adapter_back, factor_in, preferred_element_type=jnp.float32))
    grad_gate = (grad_hidden * up_pre * derivative).astype(jnp.bfloat16)
    grad_up = (grad_hidden * activation).astype(jnp.bfloat16)
    rows_out = (jnp.dot(grad_gate, w_gate.T, preferred_element_type=jnp.float32)
                + jnp.dot(grad_up, w_up.T, preferred_element_type=jnp.float32)).astype(jnp.bfloat16)
    grad_factor_in = adapter_scale * jnp.dot(back_scaled.T, hidden, preferred_element_type=jnp.float32)
    grad_factor_out = adapter_scale * jnp.dot(low_scaled.T, grad_in, preferred_element_type=jnp.float32)
    return rows_out, grad_factor_in, grad_factor_out


def reference(tokens, out_grad, expert_ids, route_weight, gate_weight, up_weight, down_weight, adapter_in, adapter_out):
    token_total = tokens.shape[0]
    flat_ids = expert_ids.reshape(-1)
    flat_weight = route_weight.reshape(-1)
    capacity = (token_total // TOK_DEV) * MOST
    positions = jnp.arange(capacity, dtype=jnp.int32)

    def per_expert(grad_total, inputs):
        expert, w_gate, w_up, w_down, factor_in, factor_out = inputs
        matched = flat_ids == expert
        routes = jnp.nonzero(matched, size=capacity, fill_value=0)[0].astype(jnp.int32)
        is_valid = positions < jnp.sum(matched.astype(jnp.int32))
        owners = routes // TOP
        tokens_in = jnp.where(is_valid[:, None], tokens[owners], jnp.zeros((), jnp.bfloat16))
        grad_in = jnp.where(is_valid[:, None], out_grad[owners], jnp.zeros((), jnp.bfloat16))
        weight_in = jnp.where(is_valid, flat_weight[routes], jnp.zeros((), jnp.bfloat16))
        rows_out, grad_factor_in, grad_factor_out = backward_rows(
            tokens_in, grad_in, weight_in, w_gate, w_up, w_down, factor_in, factor_out)
        grad_total = grad_total.at[owners].add(rows_out.astype(jnp.float32))
        return grad_total, (grad_factor_in, grad_factor_out)

    zero_grads = jnp.zeros((token_total, tokens.shape[1]), jnp.float32)
    grad_total, (grads_in, grads_out) = lax.scan(
        per_expert, zero_grads,
        (jnp.arange(EXPERTS, dtype=jnp.int32), gate_weight, up_weight, down_weight, adapter_in, adapter_out))
    return grad_total.astype(jnp.bfloat16), grads_in, grads_out
```

```python
import jax
import jax.numpy as jnp
from jax import lax
from jax.sharding import PartitionSpec as P

adapter_scale = 2.0


def silu_parts(gate_pre):
    logistic = jax.nn.sigmoid(gate_pre)
    return (gate_pre * logistic, logistic * (1.0 + gate_pre * (1.0 - logistic)))


def expert_grads(tokens_in, grad_in, route_scale, weights):
    w_gate, w_up, w_down, factor_in, factor_out = weights
    gate_pre = jnp.dot(tokens_in, w_gate, preferred_element_type=jnp.float32)
    up_pre = jnp.dot(tokens_in, w_up, preferred_element_type=jnp.float32)
    activation, derivative = silu_parts(gate_pre)
    hidden = (activation * up_pre).astype(jnp.bfloat16)
    low_rank = jnp.dot(hidden, factor_in.T, preferred_element_type=jnp.float32)
    low_scaled = (route_scale * low_rank).astype(jnp.bfloat16)
    adapter_back = jnp.dot(grad_in, factor_out.T, preferred_element_type=jnp.float32).astype(
        jnp.bfloat16
    )
    back_scaled = (route_scale * adapter_back.astype(jnp.float32)).astype(jnp.bfloat16)
    grad_hidden = route_scale * (
        jnp.dot(grad_in, w_down, preferred_element_type=jnp.float32)
        + adapter_scale * jnp.dot(adapter_back, factor_in, preferred_element_type=jnp.float32)
    )
    grad_gate = (grad_hidden * up_pre * derivative).astype(jnp.bfloat16)
    grad_up = (grad_hidden * activation).astype(jnp.bfloat16)
    rows_out = jnp.dot(grad_gate, w_gate.T, preferred_element_type=jnp.float32) + jnp.dot(
        grad_up, w_up.T, preferred_element_type=jnp.float32
    )
    grad_factor_in = adapter_scale * jnp.dot(
        back_scaled.T, hidden, preferred_element_type=jnp.float32
    )
    grad_factor_out = adapter_scale * jnp.dot(
        low_scaled.T, grad_in, preferred_element_type=jnp.float32
    )
    return (rows_out, grad_factor_in, grad_factor_out)


def per_device(
    tokens,
    out_grad,
    expert_ids,
    route_weight,
    gate_weight,
    up_weight,
    down_weight,
    adapter_in,
    adapter_out,
):
    peer_count = lax.axis_size("expert")
    local_count = gate_weight.shape[0]
    expert_total = local_count * peer_count
    named = expert_ids[:, :, None] == jnp.arange(expert_total, dtype=jnp.int32)[None, None, :]
    dense_weight = jnp.sum(
        jnp.where(named, route_weight.astype(jnp.float32)[:, :, None], 0.0), axis=1
    ).astype(jnp.bfloat16)
    all_weight = lax.all_gather(dense_weight, "expert", axis=0, tiled=True)
    all_tokens = lax.all_gather(tokens, "expert", axis=0, tiled=True)
    all_grads = lax.all_gather(out_grad, "expert", axis=0, tiled=True)
    w_gate_all, w_up_all, w_down_all = (
        lax.all_gather(gate_weight, "dp", axis=1, tiled=True),
        lax.all_gather(up_weight, "dp", axis=1, tiled=True),
        lax.all_gather(down_weight, "dp", axis=1, tiled=True),
    )
    first = lax.axis_index("expert") * local_count
    own_weight = lax.dynamic_slice_in_dim(all_weight, first, local_count, axis=1).astype(
        jnp.float32
    )
    rows = 0.0
    results_in = []
    results_out = []
    for expert in range(local_count):
        weights = (
            w_gate_all[expert],
            w_up_all[expert],
            w_down_all[expert],
            adapter_in[expert],
            adapter_out[expert],
        )
        rows_out, grad_factor_in, grad_factor_out = expert_grads(
            all_tokens, all_grads, own_weight[:, expert : expert + 1], weights
        )
        rows = rows + rows_out
        results_in.append(grad_factor_in)
        results_out.append(grad_factor_out)
    grad_tokens = lax.psum_scatter(
        rows.astype(jnp.bfloat16), "expert", scatter_dimension=0, tiled=True
    )
    grad_in_all, grad_out_all = (
        lax.psum_scatter(jnp.stack(results_in), "dp", scatter_dimension=2, tiled=True),
        lax.psum_scatter(jnp.stack(results_out), "dp", scatter_dimension=2, tiled=True),
    )
    return (grad_tokens, grad_in_all, grad_out_all)


def solution(mesh):
    return jax.shard_map(
        per_device,
        mesh=mesh,
        in_specs=(
            P(("group", "expert", "dp"), None),
            P(("group", "expert", "dp"), None),
            P(("group", "expert", "dp"), None),
            P(("group", "expert", "dp"), None),
            P("expert", "dp", None),
            P("expert", "dp", None),
            P("expert", "dp", None),
            P("expert", None, None),
            P("expert", None, None),
        ),
        out_specs=(
            P(("group", "expert", "dp"), None),
            P(("group", "expert"), None, "dp"),
            P(("group", "expert"), None, "dp"),
        ),
        check_vma=False,
    )
```

```python
import functools

import jax
import jax.numpy as jnp
from jax import lax
from jax.experimental import pallas as pl
from jax.experimental.pallas import tpu as pltpu
from jax.sharding import PartitionSpec as P

adapter_scale = 2.0
f32 = jnp.float32
bf16 = jnp.bfloat16


def ring_order(count, snake):
    if snake and count % 2 == 0:
        return list(range(0, count, 2)) + list(range(count - 1, 0, -2))
    return list(range(count))


def matmul(a, b):
    return jnp.dot(a, b, preferred_element_type=f32)


def matmul_bt(a, b):
    return lax.dot_general(a, b, (((1,), (1,)), ((), ())), preferred_element_type=f32)


def matmul_at(a, b):
    return lax.dot_general(a, b, (((0,), (0,)), ((), ())), preferred_element_type=f32)


def stage_kernel(pieces, parts, hidden_width, rank, *refs):
    offset_ref, refs = refs[0], refs[1:]
    token_refs, refs = refs[:pieces], refs[pieces:]
    grad_refs, refs = refs[:pieces], refs[pieces:]
    scale_ref, factor_in_ref, factor_out_ref, refs = refs[0], refs[1], refs[2], refs[3:]
    weight_refs, refs = refs[:parts], refs[parts:]
    rows_ref, grad_in_ref, grad_out_ref = refs
    depth = weight_refs[0].shape[0]
    wide = weight_refs[0].shape[1] // 3
    spans = [
        pl.ds(pl.multiple_of(offset_ref[part], depth), depth) if parts > 1 else slice(None)
        for part in range(parts)
    ]

    def columns(piece_refs, span):
        return jnp.concatenate([ref[:, span] for ref in piece_refs], axis=0)

    gate_pre, up_pre, grad_down = 0.0, 0.0, 0.0
    for span, weight in zip(spans, weight_refs):
        tokens_in = columns(token_refs, span)
        gate_pre += matmul(tokens_in, weight[:, :wide])
        up_pre += matmul(tokens_in, weight[:, wide : 2 * wide])
    for span, weight in zip(spans, weight_refs):
        grad_down += matmul(columns(grad_refs, span), weight[:, 2 * wide :])
    grad_all = columns(grad_refs, slice(None))
    logistic = 1.0 / (1.0 + jnp.exp(-gate_pre))
    activation = gate_pre * logistic
    derivative = logistic * (1.0 + gate_pre * (1.0 - logistic))
    hidden = (activation * up_pre).astype(bf16)
    rows = hidden.shape[0]
    experts = wide // hidden_width
    scale = scale_ref[...]

    def spread(width):
        return jnp.concatenate(
            [jnp.broadcast_to(scale[:, j : j + 1], (rows, width)) for j in range(experts)], axis=1
        )

    rank_at = lax.broadcasted_iota(jnp.int32, (rows, experts * rank), 1) // rank
    rank_scale = jnp.zeros((rows, experts * rank), f32)
    for j in range(experts):
        rank_scale = jnp.where(rank_at == j, scale[:, j : j + 1], rank_scale)
    low_rank = matmul_bt(hidden, factor_in_ref[...])
    low_scaled = (rank_scale * low_rank).astype(bf16)
    adapter_back = matmul_bt(grad_all, factor_out_ref[...]).astype(bf16)
    back_scaled = (rank_scale * adapter_back.astype(f32)).astype(bf16)
    grad_hidden = spread(hidden_width) * (
        grad_down + adapter_scale * matmul(adapter_back, factor_in_ref[...])
    )
    grad_gate = (grad_hidden * up_pre * derivative).astype(bf16)
    grad_up = (grad_hidden * activation).astype(bf16)
    for span, weight in zip(spans, weight_refs):
        rows_ref[:, span] = matmul_bt(grad_gate, weight[:, :wide]) + matmul_bt(
            grad_up, weight[:, wide : 2 * wide]
        )
    grad_in_ref[...] = adapter_scale * matmul_at(back_scaled, hidden)
    grad_out_ref[...] = adapter_scale * matmul_at(low_scaled, grad_all)


def stage(offsets, token_pieces, grad_pieces, scale, factor_in, factor_out, weights, hidden_width, rank):
    rows = sum(piece.shape[0] for piece in token_pieces)
    model_width = token_pieces[0].shape[1]
    wide = weights[0].shape[1] // 3
    ranks = factor_in.shape[0]
    operands = [*token_pieces, *grad_pieces, scale, factor_in, factor_out, *weights]
    return pl.pallas_call(
        functools.partial(stage_kernel, len(token_pieces), len(weights), hidden_width, rank),
        out_shape=(
            jax.ShapeDtypeStruct((rows, model_width), f32),
            jax.ShapeDtypeStruct((ranks, wide), f32),
            jax.ShapeDtypeStruct((ranks, model_width), f32),
        ),
        in_specs=[pl.BlockSpec(memory_space=pltpu.SMEM)]
        + [pl.BlockSpec(memory_space=pltpu.VMEM)] * len(operands),
        out_specs=(pl.BlockSpec(memory_space=pltpu.VMEM),) * 3,
        compiler_params=pltpu.CompilerParams(vmem_limit_bytes=40 * 1024 * 1024),
        cost_estimate=pl.CostEstimate(
            flops=10 * rows * model_width * wide,
            bytes_accessed=sum(op.size * op.dtype.itemsize for op in operands)
            + 4 * rows * model_width,
            transcendentals=rows * wide,
        ),
    )(offsets, *operands)


def per_device(
    snake,
    tokens,
    out_grad,
    expert_ids,
    route_weight,
    gate_weight,
    up_weight,
    down_weight,
    adapter_in,
    adapter_out,
):
    peer_count = lax.axis_size("expert")
    dp_count = lax.axis_size("dp")
    token_count, model_width = tokens.shape
    local_count, depth, hidden_width = gate_weight.shape
    rank = adapter_in.shape[1]
    ranks = local_count * rank
    wide = local_count * hidden_width
    expert_total = local_count * peer_count
    order = ring_order(peer_count, snake)
    forward = [(order[i], order[(i + 1) % peer_count]) for i in range(peer_count)]
    backward = [(b, a) for a, b in forward]
    me = lax.axis_index("expert")
    dp_me = lax.axis_index("dp")

    mine = jnp.concatenate(
        [w.transpose(1, 0, 2).reshape(depth, wide) for w in (gate_weight, up_weight, down_weight)],
        axis=1,
    )
    if dp_count == 2:
        weights = (mine, lax.ppermute(mine, "dp", [(0, 1), (1, 0)]))
        offsets = jnp.stack([dp_me, 1 - dp_me]).astype(jnp.int32) * depth
    else:
        weights = (lax.all_gather(mine, "dp", axis=0, tiled=True),)
        offsets = jnp.zeros((1,), jnp.int32)

    named = expert_ids[:, :, None] == jnp.arange(expert_total, dtype=jnp.int32)[None, None, :]
    dense_weight = jnp.sum(
        jnp.where(named, route_weight.astype(f32)[:, :, None], 0.0), axis=1
    ).astype(bf16)
    all_weight = lax.all_gather(dense_weight, "expert", axis=0, tiled=False)
    order_array = jnp.asarray(order, jnp.int32)
    place = jnp.argmax(order_array == me).astype(jnp.int32)
    own_weight = lax.dynamic_slice_in_dim(all_weight, me * local_count, local_count, axis=2)
    behind = order_array[(place - jnp.arange(peer_count)) % peer_count]
    scales = own_weight[behind].astype(f32)

    eye = jnp.eye(local_count, dtype=bf16)
    factor_in = (adapter_in[:, :, None, :] * eye[:, None, :, None]).reshape(ranks, wide)
    factor_out = adapter_out.reshape(ranks, model_width)

    full = (peer_count - 1) // 2
    split = peer_count % 2 == 0
    half = token_count // 2
    tokens_behind, tokens_ahead, grads_behind, grads_ahead = [tokens], [tokens], [out_grad], [out_grad]
    for _ in range(full):
        tokens_behind.append(lax.ppermute(tokens_behind[-1], "expert", forward))
        tokens_ahead.append(lax.ppermute(tokens_ahead[-1], "expert", backward))
        grads_behind.append(lax.ppermute(grads_behind[-1], "expert", forward))
        grads_ahead.append(lax.ppermute(grads_ahead[-1], "expert", backward))
    if split:
        tokens_far = (
            lax.ppermute(tokens_behind[-1][:half], "expert", forward),
            lax.ppermute(tokens_ahead[-1][half:], "expert", backward),
        )
        grads_far = (
            lax.ppermute(grads_behind[-1][:half], "expert", forward),
            lax.ppermute(grads_ahead[-1][half:], "expert", backward),
        )

    run = functools.partial(
        stage,
        offsets,
        factor_in=factor_in,
        factor_out=factor_out,
        weights=weights,
        hidden_width=hidden_width,
        rank=rank,
    )
    total_in, total_out = [], []
    rows_own, grad_in, grad_out = run([tokens], [out_grad], scales[0])
    total_in.append(grad_in)
    total_out.append(grad_out)
    rows_at = [None]
    for d in range(1, full + 1):
        rows_d, grad_in, grad_out = run(
            [tokens_behind[d], tokens_ahead[d]],
            [grads_behind[d], grads_ahead[d]],
            jnp.concatenate([scales[d], scales[peer_count - d]]),
        )
        rows_at.append(rows_d)
        total_in.append(grad_in)
        total_out.append(grad_out)
    if split:
        rows_far, grad_in, grad_out = run(tokens_far, grads_far, scales[peer_count // 2])
        total_in.append(grad_in)
        total_out.append(grad_out)
        moving_back = lax.ppermute(rows_far[:half].astype(bf16), "expert", backward)
        moving_ahead = lax.ppermute(rows_far[half:].astype(bf16), "expert", forward)

    for d in range(full, 0, -1):
        back = rows_at[d][:token_count]
        ahead = rows_at[d][token_count:]
        if d < full:
            back = back + moving_back.astype(f32)
            ahead = ahead + moving_ahead.astype(f32)
        elif split:
            back = jnp.concatenate([back[:half] + moving_back.astype(f32), back[half:]])
            ahead = jnp.concatenate([ahead[:half], ahead[half:] + moving_ahead.astype(f32)])
        moving_back = lax.ppermute(back.astype(bf16), "expert", backward)
        moving_ahead = lax.ppermute(ahead.astype(bf16), "expert", forward)
    grad_tokens = (rows_own + moving_back.astype(f32) + moving_ahead.astype(f32)).astype(bf16)

    sum_in = sum(total_in)
    grad_in = jnp.stack(
        [
            sum_in[j * rank : (j + 1) * rank, j * hidden_width : (j + 1) * hidden_width]
            for j in range(local_count)
        ]
    )
    grad_out = sum(total_out).reshape(local_count, rank, model_width)
    grad_in_all = lax.psum_scatter(grad_in, "dp", scatter_dimension=2, tiled=True)
    grad_out_all = lax.psum_scatter(grad_out, "dp", scatter_dimension=2, tiled=True)
    return (grad_tokens, grad_in_all, grad_out_all)


def solution(mesh):
    snake = mesh.shape["dp"] == 2
    return jax.shard_map(
        functools.partial(per_device, snake),
        mesh=mesh,
        in_specs=(
            P(("group", "expert", "dp"), None),
            P(("group", "expert", "dp"), None),
            P(("group", "expert", "dp"), None),
            P(("group", "expert", "dp"), None),
            P("expert", "dp", None),
            P("expert", "dp", None),
            P("expert", "dp", None),
            P("expert", None, None),
            P("expert", None, None),
        ),
        out_specs=(
            P(("group", "expert", "dp"), None),
            P(("group", "expert"), None, "dp"),
            P(("group", "expert"), None, "dp"),
        ),
        check_vma=False,
    )
```

```python
import functools

import jax
import jax.numpy as jnp
from jax import lax
from jax.experimental import pallas as pl
from jax.experimental.pallas import tpu as pltpu
from jax.sharding import PartitionSpec as P

adapter_scale = 2.0
f32 = jnp.float32
bf16 = jnp.bfloat16
lane_count = 128


def ring_order(count, snake):
    if snake and count % 2 == 0:
        return list(range(0, count, 2)) + list(range(count - 1, 0, -2))
    return list(range(count))


def matmul(a, b):
    return jnp.dot(a, b, preferred_element_type=f32)


def matmul_bt(a, b):
    return lax.dot_general(a, b, (((1,), (1,)), ((), ())), preferred_element_type=f32)


def matmul_at(a, b):
    return lax.dot_general(a, b, (((0,), (0,)), ((), ())), preferred_element_type=f32)


def stacked(piece_refs, span):
    return jnp.concatenate([ref[:, span] for ref in piece_refs], axis=0)


class Plan:
    def __init__(self, parts, depth, model_width, hidden_width, rank, experts):
        self.parts = parts
        self.depth = depth
        self.model_width = model_width
        self.hidden_width = hidden_width
        self.rank = rank
        self.experts = experts
        self.wide = experts * hidden_width
        self.ranks = experts * rank

    def spans(self, position_ref):
        if self.parts == 1:
            return [slice(0, self.model_width)]
        return [
            pl.ds(pl.multiple_of(position_ref[part], self.depth), self.depth)
            for part in range(self.parts)
        ]

    def forward(self, position_ref, token_refs, factor_in_ref, weight_refs):
        gate_pre, up_pre = 0.0, 0.0
        for span, weight in zip(self.spans(position_ref), weight_refs):
            tokens_in = stacked(token_refs, span)
            gate_pre += matmul(tokens_in, weight[:, : self.wide])
            up_pre += matmul(tokens_in, weight[:, self.wide : 2 * self.wide])
        logistic = 1.0 / (1.0 + jnp.exp(-gate_pre))
        activation = gate_pre * logistic
        derivative = logistic * (1.0 + gate_pre * (1.0 - logistic))
        hidden = (activation * up_pre).astype(bf16)
        low_rank = matmul_bt(hidden, factor_in_ref[...])
        return activation, up_pre * derivative, hidden, low_rank

    def scales(self, position_ref, grad_refs):
        columns = stacked(grad_refs, slice(self.model_width, None)).astype(f32)
        lane = lax.broadcasted_iota(jnp.int32, columns.shape, 1)
        first = position_ref[self.parts]
        return [
            jnp.sum(jnp.where(lane == first + j, columns, 0.0), axis=1, keepdims=True)
            for j in range(self.experts)
        ]

    def spread(self, scales, width):
        rows = scales[0].shape[0]
        at = lax.broadcasted_iota(jnp.int32, (rows, self.experts * width), 1)
        out = jnp.broadcast_to(scales[0], at.shape)
        for j in range(1, self.experts):
            out = jnp.where(at >= j * width, scales[j], out)
        return out

    def backward(
        self, position_ref, grad_refs, activation, slope, factor_in_ref, factor_out_ref, weight_refs, rows_ref
    ):
        scales = self.scales(position_ref, grad_refs)
        adapter_back, grad_down = 0.0, 0.0
        spans = self.spans(position_ref)
        for span, weight in zip(spans, weight_refs):
            grad_in = stacked(grad_refs, span)
            adapter_back += matmul_bt(grad_in, factor_out_ref[:, span])
            grad_down += matmul(grad_in, weight[:, 2 * self.wide :])
        adapter_back = adapter_back.astype(bf16)
        grad_hidden = self.spread(scales, self.hidden_width) * (
            grad_down + adapter_scale * matmul(adapter_back, factor_in_ref[...])
        )
        grad_gate = (grad_hidden * slope).astype(bf16)
        grad_up = (grad_hidden * activation).astype(bf16)
        for span, weight in zip(spans, weight_refs):
            rows_ref[:, span] = matmul_bt(grad_gate, weight[:, : self.wide]) + matmul_bt(
                grad_up, weight[:, self.wide : 2 * self.wide]
            )
        rank_scale = self.spread(scales, self.rank)
        return rank_scale, (rank_scale * adapter_back.astype(f32)).astype(bf16)

    def adapters(self, grad_refs, hidden, low_scaled, back_scaled, total_refs, out_refs):
        grad_all = stacked(grad_refs, slice(0, self.model_width))
        for total, out, value in zip(
            total_refs, out_refs, (matmul_at(back_scaled, hidden), matmul_at(low_scaled, grad_all))
        ):
            out[...] = total[...] + adapter_scale * value


def whole_kernel(plan, pieces, *refs):
    position_ref, refs = refs[0], refs[1:]
    token_refs, grad_refs, refs = refs[:pieces], refs[pieces : 2 * pieces], refs[2 * pieces :]
    factor_in_ref, factor_out_ref, refs = refs[0], refs[1], refs[2:]
    weight_refs, refs = refs[: plan.parts], refs[plan.parts :]
    total_refs, rows_ref, out_refs = refs[:2], refs[2], refs[3:]
    activation, slope, hidden, low_rank = plan.forward(
        position_ref, token_refs, factor_in_ref, weight_refs
    )
    rank_scale, back_scaled = plan.backward(
        position_ref, grad_refs, activation, slope, factor_in_ref, factor_out_ref, weight_refs, rows_ref
    )
    low_scaled = (rank_scale * low_rank).astype(bf16)
    plan.adapters(grad_refs, hidden, low_scaled, back_scaled, total_refs, out_refs)


def prepare_kernel(plan, *refs):
    raw_refs, refs = refs[:3], refs[3:]
    out_grad_ref, ids_ref, route_ref, factor_ref = refs[:4]
    packed_ref, grads_ref, factor_in_ref, sems = refs[4:]
    copies = []
    for kind in range(3):
        for expert in range(plan.experts):
            at = kind * plan.wide + expert * plan.hidden_width
            copies.append(
                pltpu.make_async_copy(
                    raw_refs[kind].at[expert],
                    packed_ref.at[:, at : at + plan.hidden_width],
                    sems.at[kind * plan.experts + expert],
                )
            )
    for copy in copies:
        copy.start()
    rows, lanes = grads_ref.shape[0], grads_ref.shape[1] - plan.model_width
    lane = lax.broadcasted_iota(jnp.int32, (rows, lanes), 1)
    ids, route = ids_ref[...], route_ref[...].astype(f32)
    dense = jnp.zeros((rows, lanes), f32)
    for k in range(ids.shape[1]):
        dense = jnp.where(ids[:, k : k + 1] == lane, route[:, k : k + 1], dense)
    grads_ref[:, : plan.model_width] = out_grad_ref[...]
    grads_ref[:, plan.model_width :] = dense.astype(bf16)
    factor_in_ref[...] = jnp.zeros(factor_in_ref.shape, bf16)
    for expert in range(plan.experts):
        factor_in_ref[
            expert * plan.rank : (expert + 1) * plan.rank,
            expert * plan.hidden_width : (expert + 1) * plan.hidden_width,
        ] = factor_ref[expert]
    for copy in copies:
        copy.wait()


def forward_kernel(plan, pieces, *refs):
    position_ref, refs = refs[0], refs[1:]
    token_refs, refs = refs[:pieces], refs[pieces:]
    factor_in_ref, refs = refs[0], refs[1:]
    weight_refs, out_refs = refs[: plan.parts], refs[plan.parts :]
    for out, value in zip(
        out_refs, plan.forward(position_ref, token_refs, factor_in_ref, weight_refs)
    ):
        out[...] = value


def backward_kernel(plan, pieces, *refs):
    position_ref, refs = refs[0], refs[1:]
    grad_refs, refs = refs[:pieces], refs[pieces:]
    activation_ref, slope_ref, low_rank_ref, refs = refs[0], refs[1], refs[2], refs[3:]
    factor_in_ref, factor_out_ref, refs = refs[0], refs[1], refs[2:]
    weight_refs, refs = refs[: plan.parts], refs[plan.parts :]
    rows_ref, low_scaled_ref, back_scaled_ref = refs
    rank_scale, back_scaled = plan.backward(
        position_ref,
        grad_refs,
        activation_ref[...],
        slope_ref[...],
        factor_in_ref,
        factor_out_ref,
        weight_refs,
        rows_ref,
    )
    low_scaled_ref[...] = (rank_scale * low_rank_ref[...]).astype(bf16)
    back_scaled_ref[...] = back_scaled


def adapters_kernel(plan, pieces, *refs):
    grad_refs, refs = refs[1 : 1 + pieces], refs[1 + pieces :]
    hidden_ref, low_scaled_ref, back_scaled_ref, refs = refs[0], refs[1], refs[2], refs[3:]
    plan.adapters(
        grad_refs, hidden_ref[...], low_scaled_ref[...], back_scaled_ref[...], refs[:2], refs[2:]
    )


def call(kernel, plan, pieces, position, operands, outs, flops):
    return pl.pallas_call(
        functools.partial(kernel, plan, pieces),
        out_shape=tuple(jax.ShapeDtypeStruct(shape, dtype) for shape, dtype in outs),
        in_specs=[pl.BlockSpec(memory_space=pltpu.SMEM)]
        + [pl.BlockSpec(memory_space=pltpu.VMEM)] * len(operands),
        out_specs=(pl.BlockSpec(memory_space=pltpu.VMEM),) * len(outs),
        compiler_params=pltpu.CompilerParams(vmem_limit_bytes=16 * 1024 * 1024),
        cost_estimate=pl.CostEstimate(
            flops=flops,
            bytes_accessed=sum(op.size * op.dtype.itemsize for op in operands),
            transcendentals=0,
        ),
    )(position, *operands)


def per_device(
    snake,
    tokens,
    out_grad,
    expert_ids,
    route_weight,
    gate_weight,
    up_weight,
    down_weight,
    adapter_in,
    adapter_out,
):
    peer_count = lax.axis_size("expert")
    dp_count = lax.axis_size("dp")
    token_count, model_width = tokens.shape
    local_count, depth, hidden_width = gate_weight.shape
    rank = adapter_in.shape[1]
    expert_total = local_count * peer_count
    order = ring_order(peer_count, snake)
    forward = [(order[i], order[(i + 1) % peer_count]) for i in range(peer_count)]
    backward = [(b, a) for a, b in forward]
    me = lax.axis_index("expert")
    dp_me = lax.axis_index("dp")
    parts = 2 if dp_count == 2 else 1
    plan = Plan(parts, depth, model_width, hidden_width, rank, local_count)
    wide, ranks = plan.wide, plan.ranks

    lanes = -(-expert_total // lane_count) * lane_count
    mine, grads, factor_in = pl.pallas_call(
        functools.partial(prepare_kernel, plan),
        out_shape=(
            jax.ShapeDtypeStruct((depth, 3 * wide), bf16),
            jax.ShapeDtypeStruct((token_count, model_width + lanes), bf16),
            jax.ShapeDtypeStruct((ranks, wide), bf16),
        ),
        in_specs=[pl.BlockSpec(memory_space=pltpu.HBM)] * 3 + [pl.BlockSpec(memory_space=pltpu.VMEM)] * 4,
        out_specs=(pl.BlockSpec(memory_space=pltpu.VMEM),) * 3,
        scratch_shapes=[pltpu.SemaphoreType.DMA((3 * local_count,))],
        compiler_params=pltpu.CompilerParams(vmem_limit_bytes=16 * 1024 * 1024),
    )(gate_weight, up_weight, down_weight, out_grad, expert_ids, route_weight, adapter_in)
    first_expert = me * local_count
    if parts == 2:
        weights = [mine, lax.ppermute(mine, "dp", [(0, 1), (1, 0)])]
        position = jnp.stack([dp_me * depth, (1 - dp_me) * depth, first_expert]).astype(jnp.int32)
    else:
        weights = [lax.all_gather(mine, "dp", axis=0, tiled=True)]
        position = jnp.stack([0 * first_expert, first_expert]).astype(jnp.int32)
    factor_out = adapter_out.reshape(ranks, model_width)

    full = (peer_count - 1) // 2
    split = peer_count % 2 == 0
    half = token_count // 2
    matmul_flops = 2 * model_width * wide
    totals = (jnp.zeros((ranks, wide), f32), jnp.zeros((ranks, model_width), f32))
    total_shapes = [((ranks, wide), f32), ((ranks, model_width), f32)]
    behind, ahead = [(tokens, grads)], [(tokens, grads)]
    rows_at = [None]

    def run(d):
        pieces = [behind[d], ahead[d]] + ([behind[0]] if d == 1 else [])
        rows = len(pieces) * token_count
        rows_d, *outs = call(
            whole_kernel,
            plan,
            len(pieces),
            position,
            [p[0] for p in pieces] + [p[1] for p in pieces] + [factor_in, factor_out, *weights, *totals],
            [((rows, model_width), f32)] + total_shapes,
            5 * rows * matmul_flops,
        )
        rows_at.append(rows_d)
        return outs

    def after(value, *arrays):
        held = []
        for x in arrays:
            x, value = lax.optimization_barrier((x, value))
            held.append(x)
        return value, held

    for d in range(full):
        if d > 1:
            totals, (tokens_b, tokens_a, grads_b, grads_a) = after(
                totals, behind[d][0], ahead[d][0], behind[d][1], ahead[d][1]
            )
            behind[d], ahead[d] = (tokens_b, grads_b), (tokens_a, grads_a)
        behind.append(tuple(lax.ppermute(x, "expert", forward) for x in behind[d]))
        ahead.append(tuple(lax.ppermute(x, "expert", backward) for x in ahead[d]))
        if d > 0:
            totals = run(d)
    if split:
        totals, (tokens_b, tokens_a, grads_b, grads_a) = after(
            totals, behind[full][0], ahead[full][0], behind[full][1], ahead[full][1]
        )
        far_behind = [lax.ppermute(x[:half], "expert", forward) for x in (tokens_b, grads_b)]
        far_ahead = [lax.ppermute(x[half:], "expert", backward) for x in (tokens_a, grads_a)]
        far_tokens = [far_behind[0], far_ahead[0]]
        far_grads = [far_behind[1], far_ahead[1]]
        activation, slope, hidden, low_rank = call(
            forward_kernel,
            plan,
            2,
            position,
            far_tokens + [factor_in, *weights],
            [((token_count, wide), f32)] * 2 + [((token_count, wide), bf16), ((token_count, ranks), f32)],
            2 * token_count * matmul_flops,
        )
        rows_far, low_scaled, back_scaled = call(
            backward_kernel,
            plan,
            2,
            position,
            far_grads + [activation, slope, low_rank, factor_in, factor_out, *weights],
            [((token_count, model_width), f32)] + [((token_count, ranks), bf16)] * 2,
            3 * token_count * matmul_flops,
        )
        moving_back = lax.ppermute(rows_far[:half].astype(bf16), "expert", backward)
        moving_ahead = lax.ppermute(rows_far[half:].astype(bf16), "expert", forward)
        totals, low_scaled = lax.optimization_barrier((totals, low_scaled))
    if full > 1:
        totals = run(full)
    if split:
        totals = call(
            adapters_kernel,
            plan,
            2,
            position,
            far_grads + [hidden, low_scaled, back_scaled, *totals],
            total_shapes,
            4 * token_count * ranks * (model_width + wide),
        )

    for d in range(full, 0, -1):
        back = rows_at[d][:token_count]
        front = rows_at[d][token_count : 2 * token_count]
        if d < full:
            back = back + moving_back.astype(f32)
            front = front + moving_ahead.astype(f32)
        elif split:
            back = jnp.concatenate([back[:half] + moving_back.astype(f32), back[half:]])
            front = jnp.concatenate([front[:half], front[half:] + moving_ahead.astype(f32)])
        moving_back = lax.ppermute(back.astype(bf16), "expert", backward)
        moving_ahead = lax.ppermute(front.astype(bf16), "expert", forward)
    rows_own = rows_at[1][2 * token_count :]
    grad_tokens = (rows_own + moving_back.astype(f32) + moving_ahead.astype(f32)).astype(bf16)

    grad_in = jnp.stack(
        [
            totals[0][j * rank : (j + 1) * rank, j * hidden_width : (j + 1) * hidden_width]
            for j in range(local_count)
        ]
    )
    narrow = hidden_width // dp_count
    both = jnp.concatenate(
        [
            grad_in.reshape(ranks, dp_count, narrow),
            totals[1].reshape(ranks, dp_count, model_width // dp_count),
        ],
        axis=2,
    ).transpose(1, 0, 2)
    summed = lax.psum_scatter(both, "dp", scatter_dimension=0, tiled=False)
    grad_in_all = summed[:, :narrow].reshape(local_count, rank, narrow)
    grad_out_all = summed[:, narrow:].reshape(local_count, rank, model_width // dp_count)
    return (grad_tokens, grad_in_all, grad_out_all)


def solution(mesh):
    snake = mesh.shape["dp"] == 2
    return jax.shard_map(
        functools.partial(per_device, snake),
        mesh=mesh,
        in_specs=(
            P(("group", "expert", "dp"), None),
            P(("group", "expert", "dp"), None),
            P(("group", "expert", "dp"), None),
            P(("group", "expert", "dp"), None),
            P("expert", "dp", None),
            P("expert", "dp", None),
            P("expert", "dp", None),
            P("expert", None, None),
            P("expert", None, None),
        ),
        out_specs=(
            P(("group", "expert", "dp"), None),
            P(("group", "expert"), None, "dp"),
            P(("group", "expert"), None, "dp"),
        ),
        check_vma=False,
    )
```

```python
import functools

import jax
import jax.numpy as jnp
from jax import lax
from jax.experimental import pallas as pl
from jax.experimental.pallas import tpu as pltpu
from jax.sharding import PartitionSpec as P

adapter_scale = 2.0
f32 = jnp.float32
bf16 = jnp.bfloat16
lane_count = 128


def ring_order(count, snake):
    if snake and count % 2 == 0:
        return list(range(0, count, 2)) + list(range(count - 1, 0, -2))
    return list(range(count))


def matmul(a, b):
    return jnp.dot(a, b, preferred_element_type=f32)


def matmul_bt(a, b):
    return lax.dot_general(a, b, (((1,), (1,)), ((), ())), preferred_element_type=f32)


def matmul_at(a, b):
    return lax.dot_general(a, b, (((0,), (0,)), ((), ())), preferred_element_type=f32)


def stacked(piece_refs, span):
    return jnp.concatenate([ref[:, span] for ref in piece_refs], axis=0)


class Plan:
    def __init__(self, parts, depth, model_width, hidden_width, rank, experts):
        self.parts = parts
        self.depth = depth
        self.model_width = model_width
        self.hidden_width = hidden_width
        self.rank = rank
        self.experts = experts
        self.wide = experts * hidden_width
        self.ranks = experts * rank

    def spans(self):
        if self.parts == 1:
            return [slice(0, self.model_width)]
        core = lax.axis_index("dp")
        return [
            pl.ds(pl.multiple_of(at * self.depth, self.depth), self.depth) for at in (core, 1 - core)
        ]

    def forward(self, token_refs, factor_in_ref, weight_refs):
        gate_pre, up_pre = 0.0, 0.0
        for span, weight in zip(self.spans(), weight_refs):
            tokens_in = stacked(token_refs, span)
            gate_pre += matmul(tokens_in, weight[:, : self.wide])
            up_pre += matmul(tokens_in, weight[:, self.wide : 2 * self.wide])
        logistic = 1.0 / (1.0 + jnp.exp(-gate_pre))
        activation = gate_pre * logistic
        derivative = logistic * (1.0 + gate_pre * (1.0 - logistic))
        hidden = (activation * up_pre).astype(bf16)
        low_rank = matmul_bt(hidden, factor_in_ref[...])
        return activation, up_pre * derivative, hidden, low_rank

    def scales(self, grad_refs):
        columns = stacked(grad_refs, slice(self.model_width, None)).astype(f32)
        lane = lax.broadcasted_iota(jnp.int32, columns.shape, 1)
        first = lax.axis_index("expert") * self.experts
        return [
            jnp.sum(jnp.where(lane == first + j, columns, 0.0), axis=1, keepdims=True)
            for j in range(self.experts)
        ]

    def spread(self, scales, width):
        rows = scales[0].shape[0]
        at = lax.broadcasted_iota(jnp.int32, (rows, self.experts * width), 1)
        out = jnp.broadcast_to(scales[0], at.shape)
        for j in range(1, self.experts):
            out = jnp.where(at >= j * width, scales[j], out)
        return out

    def backward(
        self, grad_refs, activation, slope, factor_in_ref, factor_out_ref, weight_refs, rows_ref
    ):
        scales = self.scales(grad_refs)
        adapter_back, grad_down = 0.0, 0.0
        spans = self.spans()
        for span, weight in zip(spans, weight_refs):
            grad_in = stacked(grad_refs, span)
            adapter_back += matmul_bt(grad_in, factor_out_ref[:, span])
            grad_down += matmul(grad_in, weight[:, 2 * self.wide :])
        adapter_back = adapter_back.astype(bf16)
        grad_hidden = self.spread(scales, self.hidden_width) * (
            grad_down + adapter_scale * matmul(adapter_back, factor_in_ref[...])
        )
        grad_gate = (grad_hidden * slope).astype(bf16)
        grad_up = (grad_hidden * activation).astype(bf16)
        for span, weight in zip(spans, weight_refs):
            rows_ref[:, span] = matmul_bt(grad_gate, weight[:, : self.wide]) + matmul_bt(
                grad_up, weight[:, self.wide : 2 * self.wide]
            )
        rank_scale = self.spread(scales, self.rank)
        return rank_scale, (rank_scale * adapter_back.astype(f32)).astype(bf16)

    def adapters(self, grad_refs, hidden, low_scaled, back_scaled, total_refs, out_refs):
        grad_all = stacked(grad_refs, slice(0, self.model_width))
        for total, out, value in zip(
            total_refs, out_refs, (matmul_at(back_scaled, hidden), matmul_at(low_scaled, grad_all))
        ):
            out[...] = total[...] + adapter_scale * value


def whole_kernel(plan, pieces, *refs):
    token_refs, grad_refs, refs = refs[:pieces], refs[pieces : 2 * pieces], refs[2 * pieces :]
    factor_in_ref, factor_out_ref, refs = refs[0], refs[1], refs[2:]
    weight_refs, refs = refs[: plan.parts], refs[plan.parts :]
    total_refs, rows_ref, out_refs = refs[:2], refs[2], refs[3:]
    activation, slope, hidden, low_rank = plan.forward(
        token_refs, factor_in_ref, weight_refs
    )
    rank_scale, back_scaled = plan.backward(
        grad_refs, activation, slope, factor_in_ref, factor_out_ref, weight_refs, rows_ref
    )
    low_scaled = (rank_scale * low_rank).astype(bf16)
    plan.adapters(grad_refs, hidden, low_scaled, back_scaled, total_refs, out_refs)


def prepare_kernel(plan, *refs):
    raw_refs, refs = refs[:3], refs[3:]
    out_grad_ref, ids_ref, route_ref, factor_ref = refs[:4]
    packed_ref, grads_ref, factor_in_ref, sems = refs[4:]
    copies = []
    for kind in range(3):
        for expert in range(plan.experts):
            at = kind * plan.wide + expert * plan.hidden_width
            copies.append(
                pltpu.make_async_copy(
                    raw_refs[kind].at[expert],
                    packed_ref.at[:, at : at + plan.hidden_width],
                    sems.at[kind * plan.experts + expert],
                )
            )
    for copy in copies:
        copy.start()
    rows, lanes = grads_ref.shape[0], grads_ref.shape[1] - plan.model_width
    expert_at = lax.broadcasted_iota(jnp.int32, (lanes, rows), 0)
    ids, route = ids_ref[...], route_ref[...].astype(f32)
    dense = jnp.zeros((lanes, rows), f32)
    for k in range(ids.shape[0]):
        dense = jnp.where(ids[k : k + 1, :] == expert_at, route[k : k + 1, :], dense)
    grads_ref[:, : plan.model_width] = out_grad_ref[...]
    grads_ref[:, plan.model_width :] = dense.T.astype(bf16)
    factor_in_ref[...] = jnp.zeros(factor_in_ref.shape, bf16)
    for expert in range(plan.experts):
        factor_in_ref[
            expert * plan.rank : (expert + 1) * plan.rank,
            expert * plan.hidden_width : (expert + 1) * plan.hidden_width,
        ] = factor_ref[expert]
    for copy in copies:
        copy.wait()


def forward_kernel(plan, pieces, *refs):
    token_refs, refs = refs[:pieces], refs[pieces:]
    factor_in_ref, refs = refs[0], refs[1:]
    weight_refs, out_refs = refs[: plan.parts], refs[plan.parts :]
    for out, value in zip(
        out_refs, plan.forward(token_refs, factor_in_ref, weight_refs)
    ):
        out[...] = value


def backward_kernel(plan, pieces, *refs):
    grad_refs, refs = refs[:pieces], refs[pieces:]
    activation_ref, slope_ref, low_rank_ref, refs = refs[0], refs[1], refs[2], refs[3:]
    factor_in_ref, factor_out_ref, refs = refs[0], refs[1], refs[2:]
    weight_refs, refs = refs[: plan.parts], refs[plan.parts :]
    rows_ref, low_scaled_ref, back_scaled_ref = refs
    rank_scale, back_scaled = plan.backward(
        grad_refs,
        activation_ref[...],
        slope_ref[...],
        factor_in_ref,
        factor_out_ref,
        weight_refs,
        rows_ref,
    )
    low_scaled_ref[...] = (rank_scale * low_rank_ref[...]).astype(bf16)
    back_scaled_ref[...] = back_scaled


def adapters_kernel(plan, pieces, *refs):
    grad_refs, refs = refs[:pieces], refs[pieces:]
    hidden_ref, low_scaled_ref, back_scaled_ref, refs = refs[0], refs[1], refs[2], refs[3:]
    plan.adapters(
        grad_refs, hidden_ref[...], low_scaled_ref[...], back_scaled_ref[...], refs[:2], refs[2:]
    )


def add_kernel(row_count, span, *refs):
    rows_ref, refs = refs[0], refs[1:]
    ways = len(refs) // 2
    for way in range(ways):
        rows = rows_ref[way * row_count : (way + 1) * row_count, span]
        refs[ways + way][...] = (rows + refs[way][...].astype(f32)).astype(bf16)


def add_sums(rows, span, incoming):
    shape = incoming[0].shape
    return pl.pallas_call(
        functools.partial(add_kernel, shape[0], span),
        out_shape=tuple(jax.ShapeDtypeStruct(shape, bf16) for _ in incoming),
        in_specs=[pl.BlockSpec(memory_space=pltpu.VMEM)] * (1 + len(incoming)),
        out_specs=(pl.BlockSpec(memory_space=pltpu.VMEM),) * len(incoming),
        compiler_params=pltpu.CompilerParams(vmem_limit_bytes=16 * 1024 * 1024),
    )(rows, *incoming)


def last_kernel(first_row, spans, *refs):
    rows_ref, out_ref = refs[0], refs[-1]
    for at, span in enumerate(spans):
        total = rows_ref[first_row : first_row + out_ref.shape[0], span]
        for incoming in refs[1 + 2 * at : 3 + 2 * at]:
            total = total + incoming[...].astype(f32)
        out_ref[:, span] = total.astype(bf16)


def call(kernel, plan, pieces, operands, outs, flops):
    return pl.pallas_call(
        functools.partial(kernel, plan, pieces),
        out_shape=tuple(jax.ShapeDtypeStruct(shape, dtype) for shape, dtype in outs),
        in_specs=[pl.BlockSpec(memory_space=pltpu.VMEM)] * len(operands),
        out_specs=(pl.BlockSpec(memory_space=pltpu.VMEM),) * len(outs),
        compiler_params=pltpu.CompilerParams(vmem_limit_bytes=16 * 1024 * 1024),
        cost_estimate=pl.CostEstimate(
            flops=flops,
            bytes_accessed=sum(op.size * op.dtype.itemsize for op in operands),
            transcendentals=0,
        ),
    )(*operands)


def per_device(
    snake,
    tokens,
    out_grad,
    expert_ids,
    route_weight,
    gate_weight,
    up_weight,
    down_weight,
    adapter_in,
    adapter_out,
):
    peer_count = lax.axis_size("expert")
    dp_count = lax.axis_size("dp")
    token_count, model_width = tokens.shape
    local_count, depth, hidden_width = gate_weight.shape
    rank = adapter_in.shape[1]
    expert_total = local_count * peer_count
    order = ring_order(peer_count, snake)
    forward = [(order[i], order[(i + 1) % peer_count]) for i in range(peer_count)]
    backward = [(b, a) for a, b in forward]
    swap = [(0, 1), (1, 0)]
    parts = 2 if dp_count == 2 else 1
    plan = Plan(parts, depth, model_width, hidden_width, rank, local_count)
    wide, ranks = plan.wide, plan.ranks

    lanes = -(-expert_total // lane_count) * lane_count
    mine, grads, factor_in = pl.pallas_call(
        functools.partial(prepare_kernel, plan),
        out_shape=(
            jax.ShapeDtypeStruct((depth, 3 * wide), bf16),
            jax.ShapeDtypeStruct((token_count, model_width + lanes), bf16),
            jax.ShapeDtypeStruct((ranks, wide), bf16),
        ),
        in_specs=[pl.BlockSpec(memory_space=pltpu.HBM)] * 3 + [pl.BlockSpec(memory_space=pltpu.VMEM)] * 4,
        out_specs=(pl.BlockSpec(memory_space=pltpu.VMEM),) * 3,
        scratch_shapes=[pltpu.SemaphoreType.DMA((3 * local_count,))],
        compiler_params=pltpu.CompilerParams(vmem_limit_bytes=16 * 1024 * 1024),
    )(
        *(pltpu.with_memory_space_constraint(w, pltpu.HBM) for w in (gate_weight, up_weight, down_weight)),
        out_grad,
        expert_ids.T,
        route_weight.T,
        adapter_in,
    )
    factor_out = adapter_out.reshape(ranks, model_width)

    full = (peer_count - 1) // 2
    split = peer_count % 2 == 0
    half = token_count // 2
    matmul_flops = 2 * model_width * wide
    totals = (jnp.zeros((ranks, wide), f32), jnp.zeros((ranks, model_width), f32))
    total_shapes = [((ranks, wide), f32), ((ranks, model_width), f32)]
    behind, ahead = [(tokens, grads)], [(tokens, grads)]
    rows_at = [None]

    def run(d):
        pieces = [behind[d], ahead[d]] + ([behind[0]] if d == 1 else [])
        rows = len(pieces) * token_count
        rows_d, *outs = call(
            whole_kernel,
            plan,
            len(pieces),
            [p[0] for p in pieces] + [p[1] for p in pieces] + [factor_in, factor_out, *weights, *totals],
            [((rows, model_width), f32)] + total_shapes,
            5 * rows * matmul_flops,
        )
        rows_at.append(rows_d)
        return outs

    def after(value, *arrays):
        held = []
        for x in arrays:
            x, value = lax.optimization_barrier((x, value))
            held.append(x)
        return value, held

    middle = model_width // 2
    columns = {"left": slice(0, middle), "right": slice(middle, None)}
    moving = {}

    def send(value, way):
        return lax.ppermute(value.astype(bf16), "expert", forward if way == "ahead" else backward)

    for d in range(full):
        if d > 1:
            totals, (tokens_b, tokens_a, grads_b, grads_a) = after(
                totals, behind[d][0], ahead[d][0], behind[d][1], ahead[d][1]
            )
            behind[d], ahead[d] = (tokens_b, grads_b), (tokens_a, grads_a)
        behind.append(tuple(lax.ppermute(x, "expert", forward) for x in behind[d]))
        ahead.append(tuple(lax.ppermute(x, "expert", backward) for x in ahead[d]))
        if d == 0:
            sent, (mine,) = after(behind[1][0], mine)
            behind[1] = (sent, behind[1][1])
            sent, (mine,) = after(ahead[1][0], mine)
            ahead[1] = (sent, ahead[1][1])
            if parts == 2:
                weights = [mine, lax.ppermute(mine, "dp", swap)]
            else:
                weights = [lax.all_gather(mine, "dp", axis=0, tiled=True)]
            weights = [pltpu.with_memory_space_constraint(w, pltpu.VMEM) for w in weights]
        else:
            totals = run(d)
    if split:
        totals, (tokens_b, tokens_a, grads_b, grads_a) = after(
            totals, behind[full][0], ahead[full][0], behind[full][1], ahead[full][1]
        )
        far_behind = [lax.ppermute(x[:half], "expert", forward) for x in (tokens_b, grads_b)]
        far_ahead = [lax.ppermute(x[half:], "expert", backward) for x in (tokens_a, grads_a)]
        far_tokens = [far_behind[0], far_ahead[0]]
        far_grads = [far_behind[1], far_ahead[1]]
        activation, slope, hidden, low_rank = call(
            forward_kernel,
            plan,
            2,
            far_tokens + [factor_in, *weights],
            [((token_count, wide), f32)] * 2 + [((token_count, wide), bf16), ((token_count, ranks), f32)],
            2 * token_count * matmul_flops,
        )
        rows_far, low_scaled, back_scaled = call(
            backward_kernel,
            plan,
            2,
            far_grads + [activation, slope, low_rank, factor_in, factor_out, *weights],
            [((token_count, model_width), f32)] + [((token_count, ranks), bf16)] * 2,
            3 * token_count * matmul_flops,
        )
        moving["left", "back"] = send(rows_far[:, :middle], "back")
        moving["right", "ahead"] = send(rows_far[:, middle:], "ahead")
        totals, low_scaled = lax.optimization_barrier((totals, low_scaled))
    if full > 1:
        totals = run(full)
    if split:
        totals = call(
            adapters_kernel,
            plan,
            2,
            far_grads + [hidden, low_scaled, back_scaled, *totals],
            total_shapes,
            4 * token_count * ranks * (model_width + wide),
        )

    ways = ("back", "ahead")
    for d in range(full, 0, -1):
        for side, span in columns.items():
            blocks = {
                way: rows_at[d][at * token_count : (at + 1) * token_count, span]
                for at, way in enumerate(ways)
            }
            if all((side, way) in moving for way in ways):
                blocks = dict(zip(ways, add_sums(rows_at[d], span, [moving[side, way] for way in ways])))
            for way in ways:
                if d == full and (side, way) in moving:
                    blocks[way] = blocks[way] + moving[side, way].astype(f32)
                moving[side, way] = send(blocks[way], way)
    grad_tokens = pl.pallas_call(
        functools.partial(last_kernel, 2 * token_count, list(columns.values())),
        out_shape=jax.ShapeDtypeStruct((token_count, model_width), bf16),
        in_specs=[pl.BlockSpec(memory_space=pltpu.VMEM)] * 5,
        out_specs=pl.BlockSpec(memory_space=pltpu.VMEM),
        compiler_params=pltpu.CompilerParams(vmem_limit_bytes=16 * 1024 * 1024),
    )(rows_at[1], *(moving[side, way] for side in columns for way in ways))

    grad_in = jnp.stack(
        [
            totals[0][j * rank : (j + 1) * rank, j * hidden_width : (j + 1) * hidden_width]
            for j in range(local_count)
        ]
    )
    narrow = hidden_width // dp_count
    both = jnp.concatenate(
        [
            grad_in.reshape(ranks, dp_count, narrow),
            totals[1].reshape(ranks, dp_count, model_width // dp_count),
        ],
        axis=2,
    ).transpose(1, 0, 2)
    if dp_count == 2:
        core = lax.axis_index("dp")
        summed = both[core] + lax.ppermute(both[1 - core], "dp", swap)
    else:
        summed = lax.psum_scatter(both, "dp", scatter_dimension=0, tiled=False)
    grad_in_all = summed[:, :narrow].reshape(local_count, rank, narrow)
    grad_out_all = summed[:, narrow:].reshape(local_count, rank, model_width // dp_count)
    return (grad_tokens, grad_in_all, grad_out_all)


def solution(mesh):
    snake = mesh.shape["dp"] == 2
    return jax.shard_map(
        functools.partial(per_device, snake),
        mesh=mesh,
        in_specs=(
            P(("group", "expert", "dp"), None),
            P(("group", "expert", "dp"), None),
            P(("group", "expert", "dp"), None),
            P(("group", "expert", "dp"), None),
            P("expert", "dp", None),
            P("expert", "dp", None),
            P("expert", "dp", None),
            P("expert", None, None),
            P("expert", None, None),
        ),
        out_specs=(
            P(("group", "expert", "dp"), None),
            P(("group", "expert"), None, "dp"),
            P(("group", "expert"), None, "dp"),
        ),
        check_vma=False,
    )
```

```python
import functools

import jax
import jax.numpy as jnp
from jax import lax
from jax.experimental import pallas as pl
from jax.experimental.pallas import tpu as pltpu
from jax.sharding import PartitionSpec as P

adapter_scale = 2.0
f32 = jnp.float32
bf16 = jnp.bfloat16
lane_count = 128


def ring_order(count, snake):
    if snake and count % 2 == 0:
        return list(range(0, count, 2)) + list(range(count - 1, 0, -2))
    return list(range(count))


def matmul(a, b):
    return jnp.dot(a, b, preferred_element_type=f32)


def matmul_bt(a, b):
    return lax.dot_general(a, b, (((1,), (1,)), ((), ())), preferred_element_type=f32)


def matmul_at(a, b):
    return lax.dot_general(a, b, (((0,), (0,)), ((), ())), preferred_element_type=f32)


def stacked(piece_refs, span):
    return jnp.concatenate([ref[:, span] for ref in piece_refs], axis=0)


class Plan:
    def __init__(self, parts, depth, model_width, hidden_width, rank, experts):
        self.parts = parts
        self.depth = depth
        self.model_width = model_width
        self.hidden_width = hidden_width
        self.rank = rank
        self.experts = experts
        self.wide = experts * hidden_width
        self.ranks = experts * rank

    def spans(self):
        if self.parts == 1:
            return [slice(0, self.model_width)]
        core = lax.axis_index("dp")
        return [
            pl.ds(pl.multiple_of(at * self.depth, self.depth), self.depth) for at in (core, 1 - core)
        ]

    def forward(self, token_refs, factor_in_ref, weight_refs):
        gate_pre, up_pre = 0.0, 0.0
        for span, weight in zip(self.spans(), weight_refs):
            tokens_in = stacked(token_refs, span)
            gate_pre += matmul(tokens_in, weight[:, : self.wide])
            up_pre += matmul(tokens_in, weight[:, self.wide : 2 * self.wide])
        logistic = 1.0 / (1.0 + jnp.exp(-gate_pre))
        activation = gate_pre * logistic
        derivative = logistic * (1.0 + gate_pre * (1.0 - logistic))
        hidden = (activation * up_pre).astype(bf16)
        low_rank = matmul_bt(hidden, factor_in_ref[...])
        return activation, up_pre * derivative, hidden, low_rank

    def scales(self, grad_refs):
        columns = stacked(grad_refs, slice(self.model_width, None)).astype(f32)
        lane = lax.broadcasted_iota(jnp.int32, columns.shape, 1)
        first = lax.axis_index("expert") * self.experts
        return [
            jnp.sum(jnp.where(lane == first + j, columns, 0.0), axis=1, keepdims=True)
            for j in range(self.experts)
        ]

    def spread(self, scales, width):
        rows = scales[0].shape[0]
        at = lax.broadcasted_iota(jnp.int32, (rows, self.experts * width), 1)
        out = jnp.broadcast_to(scales[0], at.shape)
        for j in range(1, self.experts):
            out = jnp.where(at >= j * width, scales[j], out)
        return out

    def backward(
        self, grad_refs, activation, slope, factor_in_ref, factor_out_ref, weight_refs, rows_ref
    ):
        scales = self.scales(grad_refs)
        adapter_back, grad_down = 0.0, 0.0
        spans = self.spans()
        for span, weight in zip(spans, weight_refs):
            grad_in = stacked(grad_refs, span)
            adapter_back += matmul_bt(grad_in, factor_out_ref[:, span])
            grad_down += matmul(grad_in, weight[:, 2 * self.wide :])
        adapter_back = adapter_back.astype(bf16)
        grad_hidden = self.spread(scales, self.hidden_width) * (
            grad_down + adapter_scale * matmul(adapter_back, factor_in_ref[...])
        )
        grad_gate = (grad_hidden * slope).astype(bf16)
        grad_up = (grad_hidden * activation).astype(bf16)
        for span, weight in zip(spans, weight_refs):
            rows_ref[:, span] = matmul_bt(grad_gate, weight[:, : self.wide]) + matmul_bt(
                grad_up, weight[:, self.wide : 2 * self.wide]
            )
        rank_scale = self.spread(scales, self.rank)
        return rank_scale, (rank_scale * adapter_back.astype(f32)).astype(bf16)

    def adapters(self, grad_refs, hidden, low_scaled, back_scaled, total_refs, out_refs):
        grad_all = stacked(grad_refs, slice(0, self.model_width))
        for total, out, value in zip(
            total_refs, out_refs, (matmul_at(back_scaled, hidden), matmul_at(low_scaled, grad_all))
        ):
            out[...] = total[...] + adapter_scale * value


def whole_kernel(plan, pieces, blocks, *refs):
    token_refs, grad_refs, refs = refs[:pieces], refs[pieces : 2 * pieces], refs[2 * pieces :]
    factor_in_ref, factor_out_ref, refs = refs[0], refs[1], refs[2:]
    weight_refs, refs = refs[: plan.parts], refs[plan.parts :]
    total_refs, rows_ref, out_refs, send_refs = refs[:2], refs[2], refs[3:5], refs[5:]
    activation, slope, hidden, low_rank = plan.forward(token_refs, factor_in_ref, weight_refs)
    rank_scale, back_scaled = plan.backward(
        grad_refs, activation, slope, factor_in_ref, factor_out_ref, weight_refs, rows_ref
    )
    for (first_row, span), send_ref in zip(blocks, send_refs):
        send_ref[...] = rows_ref[first_row : first_row + send_ref.shape[0], span].astype(bf16)
    low_scaled = (rank_scale * low_rank).astype(bf16)
    plan.adapters(grad_refs, hidden, low_scaled, back_scaled, total_refs, out_refs)


def prepare_kernel(plan, *refs):
    raw_refs, refs = refs[:3], refs[3:]
    out_grad_ref, ids_ref, route_ref, factor_ref = refs[:4]
    packed_ref, grads_ref, factor_in_ref, ids_held, route_held, sems = refs[4:]
    width, rank = plan.hidden_width, plan.rank
    pairs = [(ids_ref, ids_held), (route_ref, route_held)]
    pairs.append((out_grad_ref, grads_ref.at[:, : plan.model_width]))
    for kind in range(3):
        for expert in range(plan.experts):
            at = kind * plan.wide + expert * width
            pairs.append((raw_refs[kind].at[expert], packed_ref.at[:, at : at + width]))
    for expert in range(plan.experts):
        block = factor_in_ref.at[
            expert * rank : (expert + 1) * rank, expert * width : (expert + 1) * width
        ]
        pairs.append((factor_ref.at[expert], block))
    copies = [
        pltpu.make_async_copy(source, target, sems.at[at])
        for at, (source, target) in enumerate(pairs)
    ]
    for copy in copies:
        copy.start()
    for expert in range(plan.experts):
        for other in range(plan.experts):
            if other != expert:
                factor_in_ref[
                    expert * rank : (expert + 1) * rank, other * width : (other + 1) * width
                ] = jnp.zeros((rank, width), bf16)
    copies[0].wait()
    copies[1].wait()
    rows, lanes = grads_ref.shape[0], grads_ref.shape[1] - plan.model_width
    expert_at = lax.broadcasted_iota(jnp.int32, (lanes, rows), 0)
    ids, route = ids_held[...], route_held[...].astype(f32)
    dense = jnp.zeros((lanes, rows), f32)
    for k in range(ids.shape[0]):
        dense = jnp.where(ids[k : k + 1, :] == expert_at, route[k : k + 1, :], dense)
    grads_ref[:, plan.model_width :] = dense.T.astype(bf16)
    for copy in copies[2:]:
        copy.wait()


def add_kernel(blocks, *refs):
    rows_ref, refs = refs[0], refs[1:]
    for (first_row, span), incoming, out in zip(blocks, refs, refs[len(blocks) :]):
        rows = rows_ref[first_row : first_row + out.shape[0], span]
        out[...] = (rows + incoming[...].astype(f32)).astype(bf16)


def add_sums(rows, blocks, incoming):
    return pl.pallas_call(
        functools.partial(add_kernel, blocks),
        out_shape=tuple(jax.ShapeDtypeStruct(x.shape, bf16) for x in incoming),
        in_specs=[pl.BlockSpec(memory_space=pltpu.VMEM)] * (1 + len(incoming)),
        out_specs=(pl.BlockSpec(memory_space=pltpu.VMEM),) * len(incoming),
        compiler_params=pltpu.CompilerParams(vmem_limit_bytes=16 * 1024 * 1024),
    )(rows, *incoming)


def halves_kernel(plan, total_in_ref, total_out_ref, keep_ref, send_ref):
    first = lax.axis_index("dp") == 0
    middle, narrow = plan.model_width // 2, plan.hidden_width // 2
    low, high = total_out_ref[:, :middle], total_out_ref[:, middle:]
    keep_ref[:, :middle] = jnp.where(first, low, high)
    send_ref[:, :middle] = jnp.where(first, high, low)
    for expert in range(plan.experts):
        rows = slice(expert * plan.rank, (expert + 1) * plan.rank)
        block = total_in_ref[rows, expert * plan.hidden_width : (expert + 1) * plan.hidden_width]
        low, high = block[:, :narrow], block[:, narrow:]
        keep_ref[rows, middle:] = jnp.where(first, low, high)
        send_ref[rows, middle:] = jnp.where(first, high, low)


def joined_kernel(plan, keep_ref, other_ref, in_ref, out_ref):
    middle = plan.model_width // 2
    for expert in range(plan.experts):
        rows = slice(expert * plan.rank, (expert + 1) * plan.rank)
        out_ref[expert] = keep_ref[rows, :middle] + other_ref[rows, :middle]
        in_ref[expert] = keep_ref[rows, middle:] + other_ref[rows, middle:]


def last_kernel(first_row, spans, *refs):
    rows_ref, out_ref = refs[0], refs[-1]
    for at, span in enumerate(spans):
        total = rows_ref[first_row : first_row + out_ref.shape[0], span]
        for incoming in refs[1 + 2 * at : 3 + 2 * at]:
            total = total + incoming[...].astype(f32)
        out_ref[:, span] = total.astype(bf16)


def simple_call(kernel, operands, outs):
    return pl.pallas_call(
        kernel,
        out_shape=tuple(jax.ShapeDtypeStruct(shape, dtype) for shape, dtype in outs),
        in_specs=[pl.BlockSpec(memory_space=pltpu.VMEM)] * len(operands),
        out_specs=(pl.BlockSpec(memory_space=pltpu.VMEM),) * len(outs),
        compiler_params=pltpu.CompilerParams(vmem_limit_bytes=16 * 1024 * 1024),
    )(*operands)


def expert_call(plan, pieces, blocks, block_rows, operands, totals):
    rows = sum(piece[0].shape[0] for piece in pieces)
    operands = [p[0] for p in pieces] + [p[1] for p in pieces] + [*operands, *totals]
    outs = [((rows, plan.model_width), f32)] + [(total.shape, f32) for total in totals]
    outs += [((block_rows, plan.model_width // 2), bf16)] * len(blocks)
    return pl.pallas_call(
        functools.partial(whole_kernel, plan, len(pieces), blocks),
        out_shape=tuple(jax.ShapeDtypeStruct(shape, dtype) for shape, dtype in outs),
        in_specs=[pl.BlockSpec(memory_space=pltpu.VMEM)] * len(operands),
        out_specs=(pl.BlockSpec(memory_space=pltpu.VMEM),) * len(outs),
        compiler_params=pltpu.CompilerParams(vmem_limit_bytes=16 * 1024 * 1024),
        cost_estimate=pl.CostEstimate(
            flops=10 * rows * plan.model_width * plan.wide,
            bytes_accessed=sum(op.size * op.dtype.itemsize for op in operands),
            transcendentals=0,
        ),
    )(*operands)


def per_device(
    snake,
    tokens,
    out_grad,
    expert_ids,
    route_weight,
    gate_weight,
    up_weight,
    down_weight,
    adapter_in,
    adapter_out,
):
    peer_count = lax.axis_size("expert")
    dp_count = lax.axis_size("dp")
    token_count, model_width = tokens.shape
    local_count, depth, hidden_width = gate_weight.shape
    rank = adapter_in.shape[1]
    expert_total = local_count * peer_count
    order = ring_order(peer_count, snake)
    forward = [(order[i], order[(i + 1) % peer_count]) for i in range(peer_count)]
    backward = [(b, a) for a, b in forward]
    swap = [(0, 1), (1, 0)]
    parts = 2 if dp_count == 2 else 1
    plan = Plan(parts, depth, model_width, hidden_width, rank, local_count)
    wide, ranks = plan.wide, plan.ranks

    lanes = -(-expert_total // lane_count) * lane_count
    mine, grads, factor_in = pl.pallas_call(
        functools.partial(prepare_kernel, plan),
        out_shape=(
            jax.ShapeDtypeStruct((depth, 3 * wide), bf16),
            jax.ShapeDtypeStruct((token_count, model_width + lanes), bf16),
            jax.ShapeDtypeStruct((ranks, wide), bf16),
        ),
        in_specs=[pl.BlockSpec(memory_space=pltpu.HBM)] * 7,
        out_specs=(pl.BlockSpec(memory_space=pltpu.VMEM),) * 3,
        scratch_shapes=[
            pltpu.VMEM(expert_ids.shape[::-1], jnp.int32),
            pltpu.VMEM(route_weight.shape[::-1], bf16),
            pltpu.SemaphoreType.DMA((3 + 4 * local_count,)),
        ],
        compiler_params=pltpu.CompilerParams(vmem_limit_bytes=16 * 1024 * 1024),
    )(
        *(
            pltpu.with_memory_space_constraint(x, pltpu.HBM)
            for x in (
                gate_weight,
                up_weight,
                down_weight,
                out_grad,
                expert_ids.T,
                route_weight.T,
                adapter_in,
            )
        )
    )
    if parts == 2:
        weights = [mine, lax.ppermute(mine, "dp", swap)]
    else:
        weights = [lax.all_gather(mine, "dp", axis=0, tiled=True)]
    weights = [pltpu.with_memory_space_constraint(w, pltpu.VMEM) for w in weights]
    factor_out = adapter_out.reshape(ranks, model_width)

    full = (peer_count - 1) // 2
    split = peer_count % 2 == 0
    totals = (jnp.zeros((ranks, wide), f32), jnp.zeros((ranks, model_width), f32))
    behind, ahead = [(tokens, grads)], [(tokens, grads)]
    rows_at = [None]

    middle = model_width // 2
    columns = {"left": slice(0, middle), "right": slice(middle, None)}
    ways = {"back": (0, backward), "ahead": (token_count, forward)}
    moving = {}

    def send(value, way):
        return lax.ppermute(value, "expert", ways[way][1])

    def run(pieces, blocks, totals):
        return expert_call(
            plan, pieces, blocks, token_count, [factor_in, factor_out, *weights], totals
        )

    def after(value, *arrays):
        held = []
        for x in arrays:
            x, value = lax.optimization_barrier((x, value))
            held.append(x)
        return value, held

    for d in range(full):
        if d > 1:
            totals, (tokens_b, grads_a) = after(totals, behind[d][0], ahead[d][1])
            tokens_a, grads_b = ahead[d][0], behind[d][1]
            behind[d], ahead[d] = (tokens_b, grads_b), (tokens_a, grads_a)
        behind.append(tuple(lax.ppermute(x, "expert", forward) for x in behind[d]))
        ahead.append(tuple(lax.ppermute(x, "expert", backward) for x in ahead[d]))
        if d > 0:
            pieces = [behind[d], ahead[d]] + ([behind[0]] if d == 1 else [])
            rows_d, *totals = run(pieces, [], totals)
            rows_at.append(rows_d)
    first_sends = [("left", "ahead"), ("right", "back")]
    if not split:
        first_sends += [("left", "back"), ("right", "ahead")]
    if split:
        totals, (tokens_b, grads_a) = after(totals, behind[full][0], ahead[full][1])
        far = (lax.ppermute(tokens_b, "expert", forward), lax.ppermute(grads_a, "expert", backward))
    if full > 0:
        pieces = [behind[full], ahead[full]] + ([behind[0]] if full == 1 else [])
        rows_d, *outs = run(pieces, [(ways[way][0], columns[side]) for side, way in first_sends], totals)
        rows_at.append(rows_d)
        totals, ready = outs[:2], outs[2:]
    if split:
        last, ready = after(far[1], *ready)
        far = (far[0], last)
    for (side, way), value in zip(first_sends, ready):
        moving[side, way] = send(value, way)
    if split:
        _, *outs = run([far], [(0, columns["left"]), (0, columns["right"])], totals)
        totals = outs[:2]
        moving["left", "back"] = send(outs[2], "back")
        moving["right", "ahead"] = send(outs[3], "ahead")
        blocks = [(0, columns["left"]), (token_count, columns["right"])]
        for block, key in zip(blocks, [("left", "back"), ("right", "ahead")]):
            (value,) = add_sums(rows_at[full], [block], [moving[key]])
            moving[key] = send(value, key[1])
    for d in range(full - 1, 0, -1):
        for side, span in columns.items():
            blocks = [(first_row, span) for first_row, _ in ways.values()]
            values = add_sums(rows_at[d], blocks, [moving[side, way] for way in ways])
            for way, value in zip(ways, values):
                moving[side, way] = send(value, way)
    grad_tokens = pl.pallas_call(
        functools.partial(last_kernel, 2 * token_count, list(columns.values())),
        out_shape=jax.ShapeDtypeStruct((token_count, model_width), bf16),
        in_specs=[pl.BlockSpec(memory_space=pltpu.VMEM)] * 5,
        out_specs=pl.BlockSpec(memory_space=pltpu.VMEM),
        compiler_params=pltpu.CompilerParams(vmem_limit_bytes=16 * 1024 * 1024),
    )(rows_at[1], *(moving[side, way] for side in columns for way in ways))

    narrow = hidden_width // dp_count
    if dp_count == 2:
        half = ((ranks, middle + narrow), f32)
        keep, other = simple_call(functools.partial(halves_kernel, plan), totals, [half, half])
        grad_in_all, grad_out_all = simple_call(
            functools.partial(joined_kernel, plan),
            [keep, lax.ppermute(other, "dp", swap)],
            [((local_count, rank, narrow), f32), ((local_count, rank, middle), f32)],
        )
        return (grad_tokens, grad_in_all, grad_out_all)
    grad_in = jnp.stack(
        [
            totals[0][j * rank : (j + 1) * rank, j * hidden_width : (j + 1) * hidden_width]
            for j in range(local_count)
        ]
    )
    both = jnp.concatenate(
        [
            grad_in.reshape(ranks, dp_count, narrow),
            totals[1].reshape(ranks, dp_count, model_width // dp_count),
        ],
        axis=2,
    ).transpose(1, 0, 2)
    summed = lax.psum_scatter(both, "dp", scatter_dimension=0, tiled=False)
    grad_in_all = summed[:, :narrow].reshape(local_count, rank, narrow)
    grad_out_all = summed[:, narrow:].reshape(local_count, rank, model_width // dp_count)
    return (grad_tokens, grad_in_all, grad_out_all)


def solution(mesh):
    snake = mesh.shape["dp"] == 2
    return jax.shard_map(
        functools.partial(per_device, snake),
        mesh=mesh,
        in_specs=(
            P(("group", "expert", "dp"), None),
            P(("group", "expert", "dp"), None),
            P(("group", "expert", "dp"), None),
            P(("group", "expert", "dp"), None),
            P("expert", "dp", None),
            P("expert", "dp", None),
            P("expert", "dp", None),
            P("expert", None, None),
            P("expert", None, None),
        ),
        out_specs=(
            P(("group", "expert", "dp"), None),
            P(("group", "expert"), None, "dp"),
            P(("group", "expert"), None, "dp"),
        ),
        check_vma=False,
    )
```

```python
import functools

import jax
import jax.numpy as jnp
from jax import lax
from jax.experimental import pallas as pl
from jax.experimental.pallas import tpu as pltpu
from jax.sharding import PartitionSpec as P

adapter_scale = 2.0
f32 = jnp.float32
bf16 = jnp.bfloat16
lane_count = 128


def ring_order(count, snake):
    if snake and count % 2 == 0:
        return list(range(0, count, 2)) + list(range(count - 1, 0, -2))
    return list(range(count))


def matmul(a, b):
    return jnp.dot(a, b, preferred_element_type=f32)


def matmul_bt(a, b):
    return lax.dot_general(a, b, (((1,), (1,)), ((), ())), preferred_element_type=f32)


def matmul_at(a, b):
    return lax.dot_general(a, b, (((0,), (0,)), ((), ())), preferred_element_type=f32)


def stacked(piece_refs, span):
    return jnp.concatenate([ref[:, span] for ref in piece_refs], axis=0)


class Plan:
    def __init__(self, parts, depth, model_width, hidden_width, rank, experts):
        self.parts = parts
        self.depth = depth
        self.model_width = model_width
        self.hidden_width = hidden_width
        self.rank = rank
        self.experts = experts
        self.wide = experts * hidden_width
        self.ranks = experts * rank

    def spans(self):
        if self.parts == 1:
            return [slice(0, self.model_width)]
        core = lax.axis_index("dp")
        return [
            pl.ds(pl.multiple_of(at * self.depth, self.depth), self.depth) for at in (core, 1 - core)
        ]

    def forward(self, token_refs, factor_in_ref, weight_refs):
        gate_pre, up_pre = 0.0, 0.0
        for span, weight in zip(self.spans(), weight_refs):
            tokens_in = stacked(token_refs, span)
            gate_pre += matmul(tokens_in, weight[:, : self.wide])
            up_pre += matmul(tokens_in, weight[:, self.wide : 2 * self.wide])
        logistic = 1.0 / (1.0 + jnp.exp(-gate_pre))
        activation = gate_pre * logistic
        derivative = logistic * (1.0 + gate_pre * (1.0 - logistic))
        hidden = (activation * up_pre).astype(bf16)
        low_rank = matmul_bt(hidden, factor_in_ref[...])
        return activation, up_pre * derivative, hidden, low_rank

    def scales(self, grad_refs):
        columns = stacked(grad_refs, slice(self.model_width, None)).astype(f32)
        lane = lax.broadcasted_iota(jnp.int32, columns.shape, 1)
        first = lax.axis_index("expert") * self.experts
        return [
            jnp.sum(jnp.where(lane == first + j, columns, 0.0), axis=1, keepdims=True)
            for j in range(self.experts)
        ]

    def spread(self, scales, width):
        rows = scales[0].shape[0]
        at = lax.broadcasted_iota(jnp.int32, (rows, self.experts * width), 1)
        out = jnp.broadcast_to(scales[0], at.shape)
        for j in range(1, self.experts):
            out = jnp.where(at >= j * width, scales[j], out)
        return out

    def backward(
        self, grad_refs, activation, slope, factor_in_ref, factor_out_ref, weight_refs, rows_ref
    ):
        scales = self.scales(grad_refs)
        adapter_back, grad_down = 0.0, 0.0
        spans = self.spans()
        for span, weight in zip(spans, weight_refs):
            grad_in = stacked(grad_refs, span)
            adapter_back += matmul_bt(grad_in, factor_out_ref[:, span])
            grad_down += matmul(grad_in, weight[:, 2 * self.wide :])
        adapter_back = adapter_back.astype(bf16)
        grad_hidden = self.spread(scales, self.hidden_width) * (
            grad_down + adapter_scale * matmul(adapter_back, factor_in_ref[...])
        )
        grad_gate = (grad_hidden * slope).astype(bf16)
        grad_up = (grad_hidden * activation).astype(bf16)
        for span, weight in zip(spans, weight_refs):
            rows_ref[:, span] = matmul_bt(grad_gate, weight[:, : self.wide]) + matmul_bt(
                grad_up, weight[:, self.wide : 2 * self.wide]
            )
        rank_scale = self.spread(scales, self.rank)
        return rank_scale, (rank_scale * adapter_back.astype(f32)).astype(bf16)

    def adapters(self, grad_refs, hidden, low_scaled, back_scaled, total_refs, out_refs):
        grad_all = stacked(grad_refs, slice(0, self.model_width))
        for total, out, value in zip(
            total_refs, out_refs, (matmul_at(back_scaled, hidden), matmul_at(low_scaled, grad_all))
        ):
            out[...] = total[...] + adapter_scale * value


def whole_kernel(plan, pieces, blocks, *refs):
    token_refs, grad_refs, refs = refs[:pieces], refs[pieces : 2 * pieces], refs[2 * pieces :]
    factor_in_ref, factor_out_ref, refs = refs[0], refs[1], refs[2:]
    weight_refs, refs = refs[: plan.parts], refs[plan.parts :]
    total_refs, rows_ref, out_refs, send_refs = refs[:2], refs[2], refs[3:5], refs[5:]
    activation, slope, hidden, low_rank = plan.forward(token_refs, factor_in_ref, weight_refs)
    rank_scale, back_scaled = plan.backward(
        grad_refs, activation, slope, factor_in_ref, factor_out_ref, weight_refs, rows_ref
    )
    for (first_row, span), send_ref in zip(blocks, send_refs):
        send_ref[...] = rows_ref[first_row : first_row + send_ref.shape[0], span].astype(bf16)
    low_scaled = (rank_scale * low_rank).astype(bf16)
    plan.adapters(grad_refs, hidden, low_scaled, back_scaled, total_refs, out_refs)


def prepare_kernel(plan, *refs):
    raw_refs, refs = refs[:3], refs[3:]
    out_grad_ref, ids_ref, route_ref, factor_ref = refs[:4]
    tokens_ref, refs = refs[4], refs[5:]
    packed_ref, grads_ref, tokens_held_ref, factor_in_ref, ids_held, route_held, sems = refs
    width, rank = plan.hidden_width, plan.rank
    pairs = [(ids_ref, ids_held), (route_ref, route_held)]
    pairs.append((out_grad_ref, grads_ref.at[:, : plan.model_width]))
    pairs.append((tokens_ref, tokens_held_ref.at[:, : plan.model_width]))
    for kind in range(3):
        for expert in range(plan.experts):
            at = kind * plan.wide + expert * width
            pairs.append((raw_refs[kind].at[expert], packed_ref.at[:, at : at + width]))
    for expert in range(plan.experts):
        block = factor_in_ref.at[
            expert * rank : (expert + 1) * rank, expert * width : (expert + 1) * width
        ]
        pairs.append((factor_ref.at[expert], block))
    copies = [
        pltpu.make_async_copy(source, target, sems.at[at])
        for at, (source, target) in enumerate(pairs)
    ]
    for copy in copies:
        copy.start()
    for expert in range(plan.experts):
        for other in range(plan.experts):
            if other != expert:
                factor_in_ref[
                    expert * rank : (expert + 1) * rank, other * width : (other + 1) * width
                ] = jnp.zeros((rank, width), bf16)
    copies[0].wait()
    copies[1].wait()
    rows, lanes = grads_ref.shape[0], grads_ref.shape[1] - plan.model_width
    expert_at = lax.broadcasted_iota(jnp.int32, (lanes, rows), 0)
    ids, route = ids_held[...], route_held[...].astype(f32)
    dense = jnp.zeros((lanes, rows), f32)
    for k in range(ids.shape[0]):
        dense = jnp.where(ids[k : k + 1, :] == expert_at, route[k : k + 1, :], dense)
    dense = dense.T.astype(bf16)
    grads_ref[:, plan.model_width :] = dense
    tokens_held_ref[:, plan.model_width :] = dense
    for copy in copies[2:]:
        copy.wait()


def add_kernel(blocks, *refs):
    rows_ref, refs = refs[0], refs[1:]
    for (first_row, span), incoming, out in zip(blocks, refs, refs[len(blocks) :]):
        rows = rows_ref[first_row : first_row + out.shape[0], span]
        out[...] = (rows + incoming[...].astype(f32)).astype(bf16)


def add_sums(rows, blocks, incoming):
    return pl.pallas_call(
        functools.partial(add_kernel, blocks),
        out_shape=tuple(jax.ShapeDtypeStruct(x.shape, bf16) for x in incoming),
        in_specs=[pl.BlockSpec(memory_space=pltpu.VMEM)] * (1 + len(incoming)),
        out_specs=(pl.BlockSpec(memory_space=pltpu.VMEM),) * len(incoming),
        compiler_params=pltpu.CompilerParams(vmem_limit_bytes=16 * 1024 * 1024),
    )(rows, *incoming)


def half_rows_kernel(half, first_ref, second_ref, top_ref, bottom_ref):
    top_ref[...] = first_ref[:half]
    bottom_ref[...] = second_ref[half:]


def halves(first, second, half):
    out = ((half, first.shape[1]), first.dtype)
    return simple_call(functools.partial(half_rows_kernel, half), [first, second], [out, out])


def halves_kernel(plan, total_in_ref, total_out_ref, keep_ref, send_ref):
    first = lax.axis_index("dp") == 0
    middle, narrow = plan.model_width // 2, plan.hidden_width // 2
    low, high = total_out_ref[:, :middle], total_out_ref[:, middle:]
    keep_ref[:, :middle] = jnp.where(first, low, high)
    send_ref[:, :middle] = jnp.where(first, high, low)
    for expert in range(plan.experts):
        rows = slice(expert * plan.rank, (expert + 1) * plan.rank)
        block = total_in_ref[rows, expert * plan.hidden_width : (expert + 1) * plan.hidden_width]
        low, high = block[:, :narrow], block[:, narrow:]
        keep_ref[rows, middle:] = jnp.where(first, low, high)
        send_ref[rows, middle:] = jnp.where(first, high, low)


def joined_kernel(plan, keep_ref, other_ref, in_ref, out_ref):
    middle = plan.model_width // 2
    for expert in range(plan.experts):
        rows = slice(expert * plan.rank, (expert + 1) * plan.rank)
        out_ref[expert] = keep_ref[rows, :middle] + other_ref[rows, :middle]
        in_ref[expert] = keep_ref[rows, middle:] + other_ref[rows, middle:]


def last_kernel(first_row, spans, *refs):
    rows_ref, out_ref = refs[0], refs[-1]
    for at, span in enumerate(spans):
        total = rows_ref[first_row : first_row + out_ref.shape[0], span]
        for incoming in refs[1 + 2 * at : 3 + 2 * at]:
            total = total + incoming[...].astype(f32)
        out_ref[:, span] = total.astype(bf16)


def simple_call(kernel, operands, outs):
    return pl.pallas_call(
        kernel,
        out_shape=tuple(jax.ShapeDtypeStruct(shape, dtype) for shape, dtype in outs),
        in_specs=[pl.BlockSpec(memory_space=pltpu.VMEM)] * len(operands),
        out_specs=(pl.BlockSpec(memory_space=pltpu.VMEM),) * len(outs),
        compiler_params=pltpu.CompilerParams(vmem_limit_bytes=16 * 1024 * 1024),
    )(*operands)


def expert_call(plan, pieces, blocks, block_rows, operands, totals):
    rows = sum(piece[0].shape[0] for piece in pieces)
    operands = [p[0] for p in pieces] + [p[1] for p in pieces] + [*operands, *totals]
    outs = [((rows, plan.model_width), f32)] + [(total.shape, f32) for total in totals]
    outs += [((block_rows, plan.model_width // 2), bf16)] * len(blocks)
    return pl.pallas_call(
        functools.partial(whole_kernel, plan, len(pieces), blocks),
        out_shape=tuple(jax.ShapeDtypeStruct(shape, dtype) for shape, dtype in outs),
        in_specs=[pl.BlockSpec(memory_space=pltpu.VMEM)] * len(operands),
        out_specs=(pl.BlockSpec(memory_space=pltpu.VMEM),) * len(outs),
        compiler_params=pltpu.CompilerParams(vmem_limit_bytes=16 * 1024 * 1024),
        cost_estimate=pl.CostEstimate(
            flops=10 * rows * plan.model_width * plan.wide,
            bytes_accessed=sum(op.size * op.dtype.itemsize for op in operands),
            transcendentals=0,
        ),
    )(*operands)


def per_device(
    snake,
    tokens,
    out_grad,
    expert_ids,
    route_weight,
    gate_weight,
    up_weight,
    down_weight,
    adapter_in,
    adapter_out,
):
    peer_count = lax.axis_size("expert")
    dp_count = lax.axis_size("dp")
    token_count, model_width = tokens.shape
    local_count, depth, hidden_width = gate_weight.shape
    rank = adapter_in.shape[1]
    expert_total = local_count * peer_count
    order = ring_order(peer_count, snake)
    forward = [(order[i], order[(i + 1) % peer_count]) for i in range(peer_count)]
    backward = [(b, a) for a, b in forward]
    swap = [(0, 1), (1, 0)]
    parts = 2 if dp_count == 2 else 1
    plan = Plan(parts, depth, model_width, hidden_width, rank, local_count)
    wide, ranks = plan.wide, plan.ranks

    lanes = -(-expert_total // lane_count) * lane_count
    mine, grads, tokens_held, factor_in = pl.pallas_call(
        functools.partial(prepare_kernel, plan),
        out_shape=(
            jax.ShapeDtypeStruct((depth, 3 * wide), bf16),
            jax.ShapeDtypeStruct((token_count, model_width + lanes), bf16),
            jax.ShapeDtypeStruct((token_count, model_width + lanes), bf16),
            jax.ShapeDtypeStruct((ranks, wide), bf16),
        ),
        in_specs=[pl.BlockSpec(memory_space=pltpu.HBM)] * 8,
        out_specs=(pl.BlockSpec(memory_space=pltpu.VMEM),) * 4,
        scratch_shapes=[
            pltpu.VMEM(expert_ids.shape[::-1], jnp.int32),
            pltpu.VMEM(route_weight.shape[::-1], bf16),
            pltpu.SemaphoreType.DMA((4 + 4 * local_count,)),
        ],
        compiler_params=pltpu.CompilerParams(vmem_limit_bytes=16 * 1024 * 1024),
    )(
        *(
            pltpu.with_memory_space_constraint(x, pltpu.HBM)
            for x in (
                gate_weight,
                up_weight,
                down_weight,
                out_grad,
                expert_ids.T,
                route_weight.T,
                adapter_in,
                tokens,
            )
        )
    )
    if parts == 2:
        weights = [mine, lax.ppermute(mine, "dp", swap)]
    else:
        weights = [lax.all_gather(mine, "dp", axis=0, tiled=True)]
    weights = [pltpu.with_memory_space_constraint(w, pltpu.VMEM) for w in weights]
    factor_out = adapter_out.reshape(ranks, model_width)

    full = (peer_count - 1) // 2
    split = peer_count % 2 == 0
    totals = (jnp.zeros((ranks, wide), f32), jnp.zeros((ranks, model_width), f32))
    behind, ahead = [(tokens_held, grads)], [(tokens_held, grads)]
    rows_at = [None]

    middle = model_width // 2
    columns = {"left": slice(0, middle), "right": slice(middle, None)}
    ways = {"back": (0, backward), "ahead": (token_count, forward)}
    moving = {}

    def send(value, way):
        return lax.ppermute(value, "expert", ways[way][1])

    def run(pieces, blocks, totals):
        return expert_call(
            plan, pieces, blocks, token_count, [factor_in, factor_out, *weights], totals
        )

    def after(value, *arrays):
        held = []
        for x in arrays:
            x, value = lax.optimization_barrier((x, value))
            held.append(x)
        return value, held

    for d in range(full):
        if d > 1:
            totals, (tokens_b, tokens_a) = after(totals, behind[d][0], ahead[d][0])
            grads_b, grads_a = behind[d][1], ahead[d][1]
            behind[d], ahead[d] = (tokens_b, grads_b), (tokens_a, grads_a)
        behind.append(tuple(lax.ppermute(x, "expert", forward) for x in behind[d]))
        ahead.append(tuple(lax.ppermute(x, "expert", backward) for x in ahead[d]))
        if d > 0:
            pieces = [behind[d], ahead[d]] + ([behind[0]] if d == 1 else [])
            rows_d, *totals = run(pieces, [], totals)
            rows_at.append(rows_d)
    first_sends = [("left", "ahead"), ("right", "back")]
    if not split:
        first_sends += [("left", "back"), ("right", "ahead")]
    if split:
        half = token_count // 2
        totals, (tokens_b, tokens_a) = after(totals, behind[full][0], ahead[full][0])
        tokens_b, tokens_a = halves(tokens_b, tokens_a, half)
        grads_b, grads_a = halves(behind[full][1], ahead[full][1], half)
        far = [
            tuple(lax.ppermute(x, "expert", forward) for x in (tokens_b, grads_b)),
            tuple(lax.ppermute(x, "expert", backward) for x in (tokens_a, grads_a)),
        ]
    if full > 0:
        pieces = [behind[full], ahead[full]] + ([behind[0]] if full == 1 else [])
        rows_d, *outs = run(pieces, [(ways[way][0], columns[side]) for side, way in first_sends], totals)
        rows_at.append(rows_d)
        totals, ready = outs[:2], outs[2:]
    if split:
        last, ready = after(far[1][1], *ready)
        far[1] = (far[1][0], last)
    for (side, way), value in zip(first_sends, ready):
        moving[side, way] = send(value, way)
    if split:
        _, *outs = run(far, [(0, columns["left"]), (0, columns["right"])], totals)
        totals = outs[:2]
        moving["left", "back"] = send(outs[2], "back")
        moving["right", "ahead"] = send(outs[3], "ahead")
        blocks = [(0, columns["left"]), (token_count, columns["right"])]
        for block, key in zip(blocks, [("left", "back"), ("right", "ahead")]):
            (value,) = add_sums(rows_at[full], [block], [moving[key]])
            moving[key] = send(value, key[1])
    for d in range(full - 1, 0, -1):
        for side, span in columns.items():
            blocks = [(first_row, span) for first_row, _ in ways.values()]
            values = add_sums(rows_at[d], blocks, [moving[side, way] for way in ways])
            for way, value in zip(ways, values):
                moving[side, way] = send(value, way)
    grad_tokens = pl.pallas_call(
        functools.partial(last_kernel, 2 * token_count, list(columns.values())),
        out_shape=jax.ShapeDtypeStruct((token_count, model_width), bf16),
        in_specs=[pl.BlockSpec(memory_space=pltpu.VMEM)] * 5,
        out_specs=pl.BlockSpec(memory_space=pltpu.VMEM),
        compiler_params=pltpu.CompilerParams(vmem_limit_bytes=16 * 1024 * 1024),
    )(rows_at[1], *(moving[side, way] for side in columns for way in ways))

    narrow = hidden_width // dp_count
    if dp_count == 2:
        half = ((ranks, middle + narrow), f32)
        keep, other = simple_call(functools.partial(halves_kernel, plan), totals, [half, half])
        grad_in_all, grad_out_all = simple_call(
            functools.partial(joined_kernel, plan),
            [keep, lax.ppermute(other, "dp", swap)],
            [((local_count, rank, narrow), f32), ((local_count, rank, middle), f32)],
        )
        return (grad_tokens, grad_in_all, grad_out_all)
    grad_in = jnp.stack(
        [
            totals[0][j * rank : (j + 1) * rank, j * hidden_width : (j + 1) * hidden_width]
            for j in range(local_count)
        ]
    )
    both = jnp.concatenate(
        [
            grad_in.reshape(ranks, dp_count, narrow),
            totals[1].reshape(ranks, dp_count, model_width // dp_count),
        ],
        axis=2,
    ).transpose(1, 0, 2)
    summed = lax.psum_scatter(both, "dp", scatter_dimension=0, tiled=False)
    grad_in_all = summed[:, :narrow].reshape(local_count, rank, narrow)
    grad_out_all = summed[:, narrow:].reshape(local_count, rank, model_width // dp_count)
    return (grad_tokens, grad_in_all, grad_out_all)


def solution(mesh):
    snake = mesh.shape["dp"] == 2
    return jax.shard_map(
        functools.partial(per_device, snake),
        mesh=mesh,
        in_specs=(
            P(("group", "expert", "dp"), None),
            P(("group", "expert", "dp"), None),
            P(("group", "expert", "dp"), None),
            P(("group", "expert", "dp"), None),
            P("expert", "dp", None),
            P("expert", "dp", None),
            P("expert", "dp", None),
            P("expert", None, None),
            P("expert", None, None),
        ),
        out_specs=(
            P(("group", "expert", "dp"), None),
            P(("group", "expert"), None, "dp"),
            P(("group", "expert"), None, "dp"),
        ),
        check_vma=False,
    )
```

```python
import functools

import jax
import jax.numpy as jnp
from jax import lax
from jax.experimental import pallas as pl
from jax.experimental.pallas import tpu as pltpu
from jax.sharding import PartitionSpec as P

adapter_scale = 2.0
f32 = jnp.float32
bf16 = jnp.bfloat16
lane_count = 128


def ring_order(count, snake):
    if snake and count % 2 == 0:
        return list(range(0, count, 2)) + list(range(count - 1, 0, -2))
    return list(range(count))


def matmul(a, b):
    return jnp.dot(a, b, preferred_element_type=f32)


def matmul_bt(a, b):
    return lax.dot_general(a, b, (((1,), (1,)), ((), ())), preferred_element_type=f32)


def matmul_at(a, b):
    return lax.dot_general(a, b, (((0,), (0,)), ((), ())), preferred_element_type=f32)


def stacked(piece_refs, span):
    return jnp.concatenate([ref[:, span] for ref in piece_refs], axis=0)


class Plan:
    def __init__(self, parts, depth, model_width, hidden_width, rank, experts):
        self.parts = parts
        self.depth = depth
        self.model_width = model_width
        self.hidden_width = hidden_width
        self.rank = rank
        self.experts = experts
        self.wide = experts * hidden_width
        self.ranks = experts * rank

    def spans(self, first):
        if self.parts == 1:
            return [slice(first, first + self.model_width)]
        core = lax.axis_index("dp")
        return [
            pl.ds(pl.multiple_of(first + at * self.depth, self.depth), self.depth)
            for at in (core, 1 - core)
        ]

    def scales(self, piece_refs):
        columns = stacked(piece_refs, slice(2 * self.model_width, None)).astype(f32)
        lane = lax.broadcasted_iota(jnp.int32, columns.shape, 1)
        first = lax.axis_index("expert") * self.experts
        return [
            jnp.sum(jnp.where(lane == first + j, columns, 0.0), axis=1, keepdims=True)
            for j in range(self.experts)
        ]

    def spread(self, scales, width):
        rows = scales[0].shape[0]
        at = lax.broadcasted_iota(jnp.int32, (rows, self.experts * width), 1)
        out = jnp.broadcast_to(scales[0], at.shape)
        for j in range(1, self.experts):
            out = jnp.where(at >= j * width, scales[j], out)
        return out


def expert_kernel(plan, pieces, blocks, *refs):
    piece_refs, refs = refs[:pieces], refs[pieces:]
    factor_in_ref, factor_out_ref, refs = refs[0], refs[1], refs[2:]
    weight_refs, refs = refs[: plan.parts], refs[plan.parts :]
    total_in_ref, total_out_ref, rows_ref, sum_in_ref, sum_out_ref, *send_refs = refs
    wide = plan.wide

    gate_pre, up_pre = 0.0, 0.0
    for span, weight in zip(plan.spans(0), weight_refs):
        tokens_in = stacked(piece_refs, span)
        gate_pre += matmul(tokens_in, weight[:, :wide])
        up_pre += matmul(tokens_in, weight[:, wide : 2 * wide])
    adapter_back, grad_down = 0.0, 0.0
    for span, at, weight in zip(plan.spans(plan.model_width), plan.spans(0), weight_refs):
        grad_in = stacked(piece_refs, span)
        adapter_back += matmul_bt(grad_in, factor_out_ref[:, at])
        grad_down += matmul(grad_in, weight[:, 2 * wide :])
    adapter_back = adapter_back.astype(bf16)
    scales = plan.scales(piece_refs)
    logistic = 1.0 / (1.0 + jnp.exp(-gate_pre))
    activation = gate_pre * logistic
    derivative = logistic * (1.0 + gate_pre * (1.0 - logistic))
    hidden = (activation * up_pre).astype(bf16)
    grad_hidden = plan.spread(scales, plan.hidden_width) * (
        grad_down + adapter_scale * matmul(adapter_back, factor_in_ref[...])
    )
    grad_gate = (grad_hidden * up_pre * derivative).astype(bf16)
    grad_up = (grad_hidden * activation).astype(bf16)
    for span, weight in zip(plan.spans(0), weight_refs):
        rows_ref[:, span] = matmul_bt(grad_gate, weight[:, :wide]) + matmul_bt(
            grad_up, weight[:, wide : 2 * wide]
        )
    for first_row, send_ref in zip(blocks, send_refs):
        send_ref[...] = rows_ref[first_row : first_row + send_ref.shape[0], :].astype(bf16)

    rank_scale = plan.spread(scales, plan.rank)
    back_scaled = (rank_scale * adapter_back.astype(f32)).astype(bf16)
    low_scaled = (rank_scale * matmul_bt(hidden, factor_in_ref[...])).astype(bf16)
    grad_all = stacked(piece_refs, slice(plan.model_width, 2 * plan.model_width))
    sum_in_ref[...] = total_in_ref[...] + adapter_scale * matmul_at(back_scaled, hidden)
    sum_out_ref[...] = total_out_ref[...] + adapter_scale * matmul_at(low_scaled, grad_all)


def start_all(pairs, sems):
    copies = [
        pltpu.make_async_copy(source, target, sems.at[at])
        for at, (source, target) in enumerate(pairs)
    ]
    for copy in copies:
        copy.start()
    return copies


def piece_kernel(plan, tokens_ref, grads_ref, ids_ref, route_ref, *refs):
    *piece_refs, ids_held, route_held, sems = refs
    rows = piece_refs[0].shape[0]
    pairs = [(ids_ref, ids_held), (route_ref, route_held)]
    for at, piece_ref in enumerate(piece_refs):
        for kind, source in enumerate((tokens_ref, grads_ref)):
            columns = slice(kind * plan.model_width, (kind + 1) * plan.model_width)
            pairs.append((source.at[at * rows : (at + 1) * rows], piece_ref.at[:, columns]))
    copies = start_all(pairs, sems)
    copies[0].wait()
    copies[1].wait()
    lanes = piece_refs[0].shape[1] - 2 * plan.model_width
    ids, route = ids_held[...], route_held[...].astype(f32)
    expert_at = lax.broadcasted_iota(jnp.int32, (lanes, ids.shape[1]), 0)
    dense = jnp.zeros(expert_at.shape, f32)
    for k in range(ids.shape[0]):
        dense = jnp.where(ids[k : k + 1, :] == expert_at, route[k : k + 1, :], dense)
    dense = dense.T.astype(bf16)
    for at, piece_ref in enumerate(piece_refs):
        piece_ref[:, 2 * plan.model_width :] = dense[at * rows : (at + 1) * rows, :]
    for copy in copies[2:]:
        copy.wait()


def weight_kernel(plan, *refs):
    raw_refs, factor_ref = refs[:3], refs[3]
    packed_ref, factor_in_ref, sems = refs[4:]
    width, rank = plan.hidden_width, plan.rank
    pairs = []
    for kind in range(3):
        for expert in range(plan.experts):
            at = kind * plan.wide + expert * width
            pairs.append((raw_refs[kind].at[expert], packed_ref.at[:, at : at + width]))
    for expert in range(plan.experts):
        block = factor_in_ref.at[
            expert * rank : (expert + 1) * rank, expert * width : (expert + 1) * width
        ]
        pairs.append((factor_ref.at[expert], block))
    copies = start_all(pairs, sems)
    for expert in range(plan.experts):
        for other in range(plan.experts):
            if other != expert:
                factor_in_ref[
                    expert * rank : (expert + 1) * rank, other * width : (other + 1) * width
                ] = jnp.zeros((rank, width), bf16)
    for copy in copies:
        copy.wait()


def add_kernel(first_rows, *refs):
    count = len(first_rows)
    for at, first_row in enumerate(first_rows):
        out = refs[2 * count + at]
        rows = refs[at][first_row : first_row + out.shape[0], :]
        out[...] = (rows + refs[count + at][...].astype(f32)).astype(bf16)


def last_kernel(batches, *refs):
    out_ref = refs[-1]
    for at in range(batches):
        rows_ref, back_ref, ahead_ref = refs[3 * at : 3 * at + 3]
        count = back_ref.shape[0]
        total = rows_ref[:count, :] + back_ref[...].astype(f32) + ahead_ref[...].astype(f32)
        out_ref[at * count : (at + 1) * count, :] = total.astype(bf16)


def halves_kernel(plan, total_in_ref, total_out_ref, keep_ref, send_ref):
    first = lax.axis_index("dp") == 0
    middle, narrow = plan.model_width // 2, plan.hidden_width // 2
    low, high = total_out_ref[:, :middle], total_out_ref[:, middle:]
    keep_ref[:, :middle] = jnp.where(first, low, high)
    send_ref[:, :middle] = jnp.where(first, high, low)
    for expert in range(plan.experts):
        rows = slice(expert * plan.rank, (expert + 1) * plan.rank)
        block = total_in_ref[rows, expert * plan.hidden_width : (expert + 1) * plan.hidden_width]
        low, high = block[:, :narrow], block[:, narrow:]
        keep_ref[rows, middle:] = jnp.where(first, low, high)
        send_ref[rows, middle:] = jnp.where(first, high, low)


def joined_kernel(plan, keep_ref, other_ref, in_ref, out_ref):
    middle = plan.model_width // 2
    for expert in range(plan.experts):
        rows = slice(expert * plan.rank, (expert + 1) * plan.rank)
        out_ref[expert] = keep_ref[rows, :middle] + other_ref[rows, :middle]
        in_ref[expert] = keep_ref[rows, middle:] + other_ref[rows, middle:]


def simple_call(kernel, operands, outs, scratch=(), space=pltpu.VMEM, flops=0, limit=16):
    return pl.pallas_call(
        kernel,
        out_shape=tuple(jax.ShapeDtypeStruct(shape, dtype) for shape, dtype in outs),
        in_specs=[pl.BlockSpec(memory_space=space)] * len(operands),
        out_specs=(pl.BlockSpec(memory_space=pltpu.VMEM),) * len(outs),
        scratch_shapes=list(scratch),
        compiler_params=pltpu.CompilerParams(vmem_limit_bytes=limit * 1024 * 1024),
        cost_estimate=pl.CostEstimate(
            flops=flops,
            bytes_accessed=sum(op.size * op.dtype.itemsize for op in operands),
            transcendentals=0,
        ),
    )(*operands)


def held_in(space, arrays):
    return [pltpu.with_memory_space_constraint(x, space) for x in arrays]


def per_device(
    snake,
    tokens,
    out_grad,
    expert_ids,
    route_weight,
    gate_weight,
    up_weight,
    down_weight,
    adapter_in,
    adapter_out,
):
    peer_count = lax.axis_size("expert")
    dp_count = lax.axis_size("dp")
    token_count, model_width = tokens.shape
    local_count, depth, hidden_width = gate_weight.shape
    rank = adapter_in.shape[1]
    expert_total = local_count * peer_count
    order = ring_order(peer_count, snake)
    forward = [(order[i], order[(i + 1) % peer_count]) for i in range(peer_count)]
    backward = [(b, a) for a, b in forward]
    swap = [(0, 1), (1, 0)]
    parts = 2 if dp_count == 2 else 1
    plan = Plan(parts, depth, model_width, hidden_width, rank, local_count)
    wide, ranks = plan.wide, plan.ranks
    batches = 2
    rows = token_count // batches

    lanes = -(-expert_total // lane_count) * lane_count
    own = simple_call(
        functools.partial(piece_kernel, plan),
        held_in(pltpu.HBM, (tokens, out_grad, expert_ids.T, route_weight.T)),
        [((rows, 2 * model_width + lanes), bf16)] * batches,
        [
            pltpu.VMEM(expert_ids.shape[::-1], jnp.int32),
            pltpu.VMEM(route_weight.shape[::-1], bf16),
            pltpu.SemaphoreType.DMA((2 + 2 * batches,)),
        ],
        pltpu.HBM,
    )

    full = (peer_count - 1) // 2
    split = peer_count % 2 == 0
    ways = {"back": backward, "ahead": forward}
    long_way = ["back", "ahead"]
    short_way = ["ahead", "back"]
    pieces = [{(0, "own"): own[at]} for at in range(batches)]
    after_first = {}

    def behind(value, x):
        return lax.optimization_barrier((x, value))[0]

    totals = [jnp.zeros((ranks, wide), f32), jnp.zeros((ranks, model_width), f32)]
    rows_of = [{} for _ in range(batches)]
    moving = [{} for _ in range(batches)]

    def run_many(members, totals):
        for start in range(0, len(members), 12):
            group = members[start : start + 12]
            sent = [
                (at, key)
                for at, key in group
                if key[0] > 0 and key in ((full + split, long_way[at]), (full, short_way[at]))
            ]
            rows_here, *outs = simple_call(
                functools.partial(
                    expert_kernel, plan, len(group), [group.index(member) * rows for member in sent]
                ),
                [pieces[at][key] for at, key in group] + [factor_in, factor_out, *weights, *totals],
                [((len(group) * rows, model_width), f32)]
                + [(total.shape, f32) for total in totals]
                + [((rows, model_width), bf16)] * len(sent),
                flops=10 * len(group) * rows * model_width * wide,
                limit=24,
            )
            totals = outs[:2]
            for (at, key), value in zip(sent, outs[2:]):
                moving[at][key] = value
            for index, (at, key) in enumerate(group):
                rows_of[at][key] = (rows_here, index * rows)
        return totals

    ties = [(0, 1, 1, 'both')]
    early = [[1]]
    done = []
    for d in range(1, full + 1 + split):
        for at in range(batches):
            for way in ways:
                if d <= full or way == long_way[at]:
                    last = pieces[at].get((d - 1, way), own[at])
                    for kernel, hop, batch, side in ties:
                        if hop == d - full and batch == at and side in (way, "both") and kernel < len(done):
                            last = behind(done[kernel][0], last)
                    opposite = forward if way == "back" else backward
                    pieces[at][d, way] = lax.ppermute(last, "expert", opposite)
        if d == 1:
            mine, factor_in = simple_call(
                functools.partial(weight_kernel, plan),
                held_in(pltpu.HBM, (gate_weight, up_weight, down_weight, adapter_in)),
                [((depth, 3 * wide), bf16), ((ranks, wide), bf16)],
                [pltpu.SemaphoreType.DMA((4 * local_count,))],
                pltpu.HBM,
            )
            if parts == 2:
                weights = [mine, lax.ppermute(mine, "dp", swap)]
            else:
                weights = [lax.all_gather(mine, "dp", axis=0, tiled=True)]
            weights = held_in(pltpu.VMEM, weights)
            factor_out = adapter_out.reshape(ranks, model_width)
        if d == full - 1:
            for kernel in early:
                totals = run_many([(at, key) for at in kernel for key in pieces[at]], totals)
                done.append(totals)

    for at in range(batches):
        totals = run_many([(at, key) for key in pieces[at] if key not in rows_of[at]], totals)

    for d in range(full + split, 0, -1):
        for at in range(batches):
            keys = [(d, way) for way in ways if (d, way) in rows_of[at]]
            added = [key for key in keys if key not in moving[at]]
            if added:
                held = [rows_of[at][key] for key in added]
                values = simple_call(
                    functools.partial(add_kernel, [first_row for _, first_row in held]),
                    [rows_here for rows_here, _ in held]
                    + [moving[at].pop((d + 1, way)) for _, way in added],
                    [((rows, model_width), bf16)] * len(added),
                )
                moving[at].update(zip(added, values))
            for key in keys:
                moving[at][key] = lax.ppermute(moving[at][key], "expert", ways[key[1]])
    operands = []
    for at in range(batches):
        operands += [rows_of[at][0, "own"][0], moving[at][1, "back"], moving[at][1, "ahead"]]
    (grad_tokens,) = simple_call(
        functools.partial(last_kernel, batches), operands, [((token_count, model_width), bf16)]
    )

    narrow = hidden_width // dp_count
    if dp_count == 2:
        middle = model_width // 2
        half = ((ranks, middle + narrow), f32)
        keep, other = simple_call(functools.partial(halves_kernel, plan), totals, [half, half])
        grad_in_all, grad_out_all = simple_call(
            functools.partial(joined_kernel, plan),
            [keep, lax.ppermute(other, "dp", swap)],
            [((local_count, rank, narrow), f32), ((local_count, rank, middle), f32)],
        )
        return (grad_tokens, grad_in_all, grad_out_all)
    grad_in = jnp.stack(
        [
            totals[0][j * rank : (j + 1) * rank, j * hidden_width : (j + 1) * hidden_width]
            for j in range(local_count)
        ]
    )
    both = jnp.concatenate(
        [
            grad_in.reshape(ranks, dp_count, narrow),
            totals[1].reshape(ranks, dp_count, model_width // dp_count),
        ],
        axis=2,
    ).transpose(1, 0, 2)
    summed = lax.psum_scatter(both, "dp", scatter_dimension=0, tiled=False)
    grad_in_all = summed[:, :narrow].reshape(local_count, rank, narrow)
    grad_out_all = summed[:, narrow:].reshape(local_count, rank, model_width // dp_count)
    return (grad_tokens, grad_in_all, grad_out_all)


def solution(mesh):
    snake = mesh.shape["dp"] == 2
    return jax.shard_map(
        functools.partial(per_device, snake),
        mesh=mesh,
        in_specs=(
            P(("group", "expert", "dp"), None),
            P(("group", "expert", "dp"), None),
            P(("group", "expert", "dp"), None),
            P(("group", "expert", "dp"), None),
            P("expert", "dp", None),
            P("expert", "dp", None),
            P("expert", "dp", None),
            P("expert", None, None),
            P("expert", None, None),
        ),
        out_specs=(
            P(("group", "expert", "dp"), None),
            P(("group", "expert"), None, "dp"),
            P(("group", "expert"), None, "dp"),
        ),
        check_vma=False,
    )
```

```python
import functools

import jax
import jax.numpy as jnp
from jax import lax
from jax.experimental import pallas as pl
from jax.experimental.pallas import tpu as pltpu
from jax.sharding import PartitionSpec as P

adapter_scale = 2.0
f32 = jnp.float32
bf16 = jnp.bfloat16
lane_count = 128


def ring_order(count, snake):
    if snake and count % 2 == 0:
        return list(range(0, count, 2)) + list(range(count - 1, 0, -2))
    return list(range(count))


def matmul(a, b):
    return jnp.dot(a, b, preferred_element_type=f32)


def matmul_bt(a, b):
    return lax.dot_general(a, b, (((1,), (1,)), ((), ())), preferred_element_type=f32)


def matmul_at(a, b):
    return lax.dot_general(a, b, (((0,), (0,)), ((), ())), preferred_element_type=f32)


def stacked(piece_refs, span):
    return jnp.concatenate([ref[:, span] for ref in piece_refs], axis=0)


class Plan:
    def __init__(self, parts, depth, model_width, hidden_width, rank, experts):
        self.parts = parts
        self.depth = depth
        self.model_width = model_width
        self.hidden_width = hidden_width
        self.rank = rank
        self.experts = experts
        self.wide = experts * hidden_width
        self.ranks = experts * rank

    def spans(self):
        if self.parts == 1:
            return [slice(0, self.model_width)]
        core = lax.axis_index("dp")
        return [
            pl.ds(pl.multiple_of(at * self.depth, self.depth), self.depth) for at in (core, 1 - core)
        ]

    def forward(self, token_refs, factor_in_ref, weight_refs):
        gate_pre, up_pre = 0.0, 0.0
        for span, weight in zip(self.spans(), weight_refs):
            tokens_in = stacked(token_refs, span)
            gate_pre += matmul(tokens_in, weight[:, : self.wide])
            up_pre += matmul(tokens_in, weight[:, self.wide : 2 * self.wide])
        logistic = 1.0 / (1.0 + jnp.exp(-gate_pre))
        activation = gate_pre * logistic
        derivative = logistic * (1.0 + gate_pre * (1.0 - logistic))
        hidden = (activation * up_pre).astype(bf16)
        low_rank = matmul_bt(hidden, factor_in_ref[...])
        return activation, up_pre * derivative, hidden, low_rank

    def scales(self, grad_refs):
        columns = stacked(grad_refs, slice(self.model_width, None)).astype(f32)
        lane = lax.broadcasted_iota(jnp.int32, columns.shape, 1)
        first = lax.axis_index("expert") * self.experts
        return [
            jnp.sum(jnp.where(lane == first + j, columns, 0.0), axis=1, keepdims=True)
            for j in range(self.experts)
        ]

    def spread(self, scales, width):
        rows = scales[0].shape[0]
        at = lax.broadcasted_iota(jnp.int32, (rows, self.experts * width), 1)
        out = jnp.broadcast_to(scales[0], at.shape)
        for j in range(1, self.experts):
            out = jnp.where(at >= j * width, scales[j], out)
        return out

    def backward(
        self, grad_refs, activation, slope, factor_in_ref, factor_out_ref, weight_refs, rows_ref
    ):
        scales = self.scales(grad_refs)
        adapter_back, grad_down = 0.0, 0.0
        spans = self.spans()
        for span, weight in zip(spans, weight_refs):
            grad_in = stacked(grad_refs, span)
            adapter_back += matmul_bt(grad_in, factor_out_ref[:, span])
            grad_down += matmul(grad_in, weight[:, 2 * self.wide :])
        adapter_back = adapter_back.astype(bf16)
        grad_hidden = self.spread(scales, self.hidden_width) * (
            grad_down + adapter_scale * matmul(adapter_back, factor_in_ref[...])
        )
        grad_gate = (grad_hidden * slope).astype(bf16)
        grad_up = (grad_hidden * activation).astype(bf16)
        for span, weight in zip(spans, weight_refs):
            rows_ref[:, span] = matmul_bt(grad_gate, weight[:, : self.wide]) + matmul_bt(
                grad_up, weight[:, self.wide : 2 * self.wide]
            )
        rank_scale = self.spread(scales, self.rank)
        return rank_scale, (rank_scale * adapter_back.astype(f32)).astype(bf16)

    def adapters(self, grad_refs, hidden, low_scaled, back_scaled, total_refs, out_refs):
        grad_all = stacked(grad_refs, slice(0, self.model_width))
        for total, out, value in zip(
            total_refs, out_refs, (matmul_at(back_scaled, hidden), matmul_at(low_scaled, grad_all))
        ):
            out[...] = total[...] + adapter_scale * value


def whole_kernel(plan, pieces, blocks, keep_rows, *refs):
    token_refs, grad_refs, refs = refs[:pieces], refs[pieces : 2 * pieces], refs[2 * pieces :]
    factor_in_ref, factor_out_ref, refs = refs[0], refs[1], refs[2:]
    weight_refs, refs = refs[: plan.parts], refs[plan.parts :]
    total_refs, refs = refs[:2], refs[2:]
    if keep_rows:
        rows_ref, refs = refs[0], refs[1:]
    else:
        *refs, rows_ref = refs
    out_refs, send_refs = refs[:2], refs[2:]
    activation, slope, hidden, low_rank = plan.forward(token_refs, factor_in_ref, weight_refs)
    rank_scale, back_scaled = plan.backward(
        grad_refs, activation, slope, factor_in_ref, factor_out_ref, weight_refs, rows_ref
    )
    for (first_row, span), send_ref in zip(blocks, send_refs):
        send_ref[...] = rows_ref[first_row : first_row + send_ref.shape[0], span].astype(bf16)
    low_scaled = (rank_scale * low_rank).astype(bf16)
    plan.adapters(grad_refs, hidden, low_scaled, back_scaled, total_refs, out_refs)


def prepare_kernel(plan, *refs):
    raw_refs, refs = refs[:3], refs[3:]
    out_grad_ref, ids_ref, route_ref, factor_ref = refs[:4]
    tokens_ref, refs = refs[4], refs[5:]
    packed_ref, grads_ref, tokens_held_ref, factor_in_ref, ids_held, route_held, sems = refs
    width, rank = plan.hidden_width, plan.rank
    pairs = [(ids_ref, ids_held), (route_ref, route_held)]
    pairs.append((out_grad_ref, grads_ref.at[:, : plan.model_width]))
    pairs.append((tokens_ref, tokens_held_ref.at[:, : plan.model_width]))
    for kind in range(3):
        for expert in range(plan.experts):
            at = kind * plan.wide + expert * width
            pairs.append((raw_refs[kind].at[expert], packed_ref.at[:, at : at + width]))
    for expert in range(plan.experts):
        block = factor_in_ref.at[
            expert * rank : (expert + 1) * rank, expert * width : (expert + 1) * width
        ]
        pairs.append((factor_ref.at[expert], block))
    copies = [
        pltpu.make_async_copy(source, target, sems.at[at])
        for at, (source, target) in enumerate(pairs)
    ]
    for copy in copies:
        copy.start()
    for expert in range(plan.experts):
        for other in range(plan.experts):
            if other != expert:
                factor_in_ref[
                    expert * rank : (expert + 1) * rank, other * width : (other + 1) * width
                ] = jnp.zeros((rank, width), bf16)
    copies[0].wait()
    copies[1].wait()
    rows, lanes = grads_ref.shape[0], grads_ref.shape[1] - plan.model_width
    expert_at = lax.broadcasted_iota(jnp.int32, (lanes, rows), 0)
    ids, route = ids_held[...], route_held[...].astype(f32)
    dense = jnp.zeros((lanes, rows), f32)
    for k in range(ids.shape[0]):
        dense = jnp.where(ids[k : k + 1, :] == expert_at, route[k : k + 1, :], dense)
    dense = dense.T.astype(bf16)
    grads_ref[:, plan.model_width :] = dense
    tokens_held_ref[:, plan.model_width :] = dense
    for copy in copies[2:]:
        copy.wait()


def add_kernel(blocks, *refs):
    rows_ref, refs = refs[0], list(refs[1:])
    outs = refs[-len(blocks) :]
    for (first_row, span, arrived), out in zip(blocks, outs):
        total = rows_ref[first_row : first_row + out.shape[0], span]
        for columns in arrived:
            total = total + refs.pop(0)[:, columns].astype(f32)
        out[...] = total.astype(bf16)


def add_sums(rows, row_count, blocks, arrived):
    operands = [rows, *arrived]
    return pl.pallas_call(
        functools.partial(add_kernel, blocks),
        out_shape=tuple(
            jax.ShapeDtypeStruct((row_count, len(range(*span.indices(rows.shape[1])))), bf16)
            for _, span, _ in blocks
        ),
        in_specs=[pl.BlockSpec(memory_space=pltpu.VMEM)] * len(operands),
        out_specs=(pl.BlockSpec(memory_space=pltpu.VMEM),) * len(blocks),
        compiler_params=pltpu.CompilerParams(vmem_limit_bytes=16 * 1024 * 1024),
    )(*operands)


def half_rows_kernel(half, first_ref, second_ref, top_ref, bottom_ref):
    top_ref[...] = first_ref[:half]
    bottom_ref[...] = second_ref[half:]


def halves(first, second, half):
    out = ((half, first.shape[1]), first.dtype)
    return simple_call(functools.partial(half_rows_kernel, half), [first, second], [out, out])


def halves_kernel(plan, total_in_ref, total_out_ref, keep_ref, send_ref):
    first = lax.axis_index("dp") == 0
    middle, narrow = plan.model_width // 2, plan.hidden_width // 2
    low, high = total_out_ref[:, :middle], total_out_ref[:, middle:]
    keep_ref[:, :middle] = jnp.where(first, low, high)
    send_ref[:, :middle] = jnp.where(first, high, low)
    for expert in range(plan.experts):
        rows = slice(expert * plan.rank, (expert + 1) * plan.rank)
        block = total_in_ref[rows, expert * plan.hidden_width : (expert + 1) * plan.hidden_width]
        low, high = block[:, :narrow], block[:, narrow:]
        keep_ref[rows, middle:] = jnp.where(first, low, high)
        send_ref[rows, middle:] = jnp.where(first, high, low)


def joined_kernel(plan, keep_ref, other_ref, in_ref, out_ref):
    middle = plan.model_width // 2
    for expert in range(plan.experts):
        rows = slice(expert * plan.rank, (expert + 1) * plan.rank)
        out_ref[expert] = keep_ref[rows, :middle] + other_ref[rows, :middle]
        in_ref[expert] = keep_ref[rows, middle:] + other_ref[rows, middle:]


def last_kernel(first_row, spans, *refs):
    rows_ref, out_ref = refs[0], refs[-1]
    for at, span in enumerate(spans):
        total = rows_ref[first_row : first_row + out_ref.shape[0], span]
        for incoming in refs[1 + 2 * at : 3 + 2 * at]:
            total = total + incoming[...].astype(f32)
        out_ref[:, span] = total.astype(bf16)


def simple_call(kernel, operands, outs):
    return pl.pallas_call(
        kernel,
        out_shape=tuple(jax.ShapeDtypeStruct(shape, dtype) for shape, dtype in outs),
        in_specs=[pl.BlockSpec(memory_space=pltpu.VMEM)] * len(operands),
        out_specs=(pl.BlockSpec(memory_space=pltpu.VMEM),) * len(outs),
        compiler_params=pltpu.CompilerParams(vmem_limit_bytes=16 * 1024 * 1024),
    )(*operands)


def expert_call(plan, pieces, blocks, block_rows, operands, totals, keep_rows):
    rows = sum(piece[0].shape[0] for piece in pieces)
    operands = [p[0] for p in pieces] + [p[1] for p in pieces] + [*operands, *totals]
    shape = (rows, plan.model_width)
    outs = [(shape, f32)] * keep_rows + [(total.shape, f32) for total in totals]
    widths = [len(range(*span.indices(plan.model_width))) for _, span in blocks]
    outs += [((block_rows, width), bf16) for width in widths]
    return pl.pallas_call(
        functools.partial(whole_kernel, plan, len(pieces), blocks, keep_rows),
        scratch_shapes=[] if keep_rows else [pltpu.VMEM(shape, f32)],
        out_shape=tuple(jax.ShapeDtypeStruct(shape, dtype) for shape, dtype in outs),
        in_specs=[pl.BlockSpec(memory_space=pltpu.VMEM)] * len(operands),
        out_specs=(pl.BlockSpec(memory_space=pltpu.VMEM),) * len(outs),
        compiler_params=pltpu.CompilerParams(vmem_limit_bytes=16 * 1024 * 1024),
        cost_estimate=pl.CostEstimate(
            flops=10 * rows * plan.model_width * plan.wide,
            bytes_accessed=sum(op.size * op.dtype.itemsize for op in operands),
            transcendentals=0,
        ),
    )(*operands)


def per_device(
    snake,
    tokens,
    out_grad,
    expert_ids,
    route_weight,
    gate_weight,
    up_weight,
    down_weight,
    adapter_in,
    adapter_out,
):
    peer_count = lax.axis_size("expert")
    dp_count = lax.axis_size("dp")
    token_count, model_width = tokens.shape
    local_count, depth, hidden_width = gate_weight.shape
    rank = adapter_in.shape[1]
    expert_total = local_count * peer_count
    order = ring_order(peer_count, snake)
    forward = [(order[i], order[(i + 1) % peer_count]) for i in range(peer_count)]
    backward = [(b, a) for a, b in forward]
    swap = [(0, 1), (1, 0)]
    parts = 2 if dp_count == 2 else 1
    plan = Plan(parts, depth, model_width, hidden_width, rank, local_count)
    wide, ranks = plan.wide, plan.ranks

    lanes = -(-expert_total // lane_count) * lane_count
    mine, grads, tokens_held, factor_in = pl.pallas_call(
        functools.partial(prepare_kernel, plan),
        out_shape=(
            jax.ShapeDtypeStruct((depth, 3 * wide), bf16),
            jax.ShapeDtypeStruct((token_count, model_width + lanes), bf16),
            jax.ShapeDtypeStruct((token_count, model_width + lanes), bf16),
            jax.ShapeDtypeStruct((ranks, wide), bf16),
        ),
        in_specs=[pl.BlockSpec(memory_space=pltpu.HBM)] * 8,
        out_specs=(pl.BlockSpec(memory_space=pltpu.VMEM),) * 4,
        scratch_shapes=[
            pltpu.VMEM(expert_ids.shape[::-1], jnp.int32),
            pltpu.VMEM(route_weight.shape[::-1], bf16),
            pltpu.SemaphoreType.DMA((4 + 4 * local_count,)),
        ],
        compiler_params=pltpu.CompilerParams(vmem_limit_bytes=16 * 1024 * 1024),
    )(
        *(
            pltpu.with_memory_space_constraint(x, pltpu.HBM)
            for x in (
                gate_weight,
                up_weight,
                down_weight,
                out_grad,
                expert_ids.T,
                route_weight.T,
                adapter_in,
                tokens,
            )
        )
    )
    if parts == 2:
        weights = [mine, lax.ppermute(mine, "dp", swap)]
    else:
        weights = [lax.all_gather(mine, "dp", axis=0, tiled=True)]
    weights = [pltpu.with_memory_space_constraint(w, pltpu.VMEM) for w in weights]
    factor_out = adapter_out.reshape(ranks, model_width)

    full = (peer_count - 1) // 2
    split = peer_count % 2 == 0
    totals = (jnp.zeros((ranks, wide), f32), jnp.zeros((ranks, model_width), f32))
    behind, ahead = [(tokens_held, grads)], [(tokens_held, grads)]
    rows_at = [None]

    middle = model_width // 2
    columns = {"left": slice(0, middle), "right": slice(middle, model_width)}
    everything = slice(0, model_width)
    ways = {"back": (0, backward), "ahead": (token_count, forward)}
    skips = {"left": "back", "right": "ahead"}
    moving = {}

    def send(value, way):
        return lax.ppermute(value, "expert", ways[way][1])

    def run(pieces, blocks, totals, keep_rows=True):
        operands = [factor_in, factor_out, *weights]
        return expert_call(plan, pieces, blocks, token_count, operands, totals, keep_rows)

    def after(value, *arrays):
        held = []
        for x in arrays:
            x, value = lax.optimization_barrier((x, value))
            held.append(x)
        return value, held

    for d in range(full):
        if d > 1:
            totals, (tokens_b, tokens_a) = after(totals, behind[d][0], ahead[d][0])
            grads_b, grads_a = behind[d][1], ahead[d][1]
            behind[d], ahead[d] = (tokens_b, grads_b), (tokens_a, grads_a)
        behind.append(tuple(lax.ppermute(x, "expert", forward) for x in behind[d]))
        ahead.append(tuple(lax.ppermute(x, "expert", backward) for x in ahead[d]))
        if d > 0:
            pieces = [behind[d], ahead[d]] + ([behind[0]] if d == 1 else [])
            rows_d, *totals = run(pieces, [], totals)
            rows_at.append(rows_d)
    if split:
        half = token_count // 2
        totals, (tokens_b, tokens_a) = after(totals, behind[full][0], ahead[full][0])
        tokens_b, tokens_a = halves(tokens_b, tokens_a, half)
        grads_b, grads_a = halves(behind[full][1], ahead[full][1], half)
        far = [
            tuple(lax.ppermute(x, "expert", forward) for x in (tokens_b, grads_b)),
            tuple(lax.ppermute(x, "expert", backward) for x in (tokens_a, grads_a)),
        ]
    pieces = [behind[full], ahead[full]]
    rows_d, *outs = run(pieces, [(first_row, everything) for first_row, _ in ways.values()], totals)
    totals = outs[:2]
    for way, value in zip(ways, outs[2:]):
        for side in columns:
            moving[side, way] = send(value, way) if side == "left" else moving["left", way]
    skipped = {}
    if split:
        outs = run(far, [(0, span) for span in columns.values()], totals, keep_rows=False)
        totals = outs[:2]
        for (side, way), value in zip(skips.items(), outs[2:]):
            step = -full if way == "back" else full
            pairs = [(order[i], order[(i + step) % peer_count]) for i in range(peer_count)]
            skipped[side, way] = lax.ppermute(value, "expert", pairs)
    for d in range(full - 1, 0, -1):
        for side, span in columns.items():
            blocks, arrived = [], []
            for way, (first_row, _) in ways.items():
                taken = [span if d == full - 1 else slice(0, middle)]
                arrived.append(moving[side, way])
                if d == 1 and (side, way) in skipped:
                    taken.append(slice(0, middle))
                    arrived.append(skipped[side, way])
                blocks.append((first_row, span, taken))
            for way, value in zip(ways, add_sums(rows_at[d], token_count, blocks, arrived)):
                moving[side, way] = send(value, way)
    grad_tokens = pl.pallas_call(
        functools.partial(last_kernel, 2 * token_count, list(columns.values())),
        out_shape=jax.ShapeDtypeStruct((token_count, model_width), bf16),
        in_specs=[pl.BlockSpec(memory_space=pltpu.VMEM)] * 5,
        out_specs=pl.BlockSpec(memory_space=pltpu.VMEM),
        compiler_params=pltpu.CompilerParams(vmem_limit_bytes=16 * 1024 * 1024),
    )(rows_at[1], *(moving[side, way] for side in columns for way in ways))

    narrow = hidden_width // dp_count
    if dp_count == 2:
        half = ((ranks, middle + narrow), f32)
        keep, other = simple_call(functools.partial(halves_kernel, plan), totals, [half, half])
        grad_in_all, grad_out_all = simple_call(
            functools.partial(joined_kernel, plan),
            [keep, lax.ppermute(other, "dp", swap)],
            [((local_count, rank, narrow), f32), ((local_count, rank, middle), f32)],
        )
        return (grad_tokens, grad_in_all, grad_out_all)
    grad_in = jnp.stack(
        [
            totals[0][j * rank : (j + 1) * rank, j * hidden_width : (j + 1) * hidden_width]
            for j in range(local_count)
        ]
    )
    both = jnp.concatenate(
        [
            grad_in.reshape(ranks, dp_count, narrow),
            totals[1].reshape(ranks, dp_count, model_width // dp_count),
        ],
        axis=2,
    ).transpose(1, 0, 2)
    summed = lax.psum_scatter(both, "dp", scatter_dimension=0, tiled=False)
    grad_in_all = summed[:, :narrow].reshape(local_count, rank, narrow)
    grad_out_all = summed[:, narrow:].reshape(local_count, rank, model_width // dp_count)
    return (grad_tokens, grad_in_all, grad_out_all)


def solution(mesh):
    snake = mesh.shape["dp"] == 2
    return jax.shard_map(
        functools.partial(per_device, snake),
        mesh=mesh,
        in_specs=(
            P(("group", "expert", "dp"), None),
            P(("group", "expert", "dp"), None),
            P(("group", "expert", "dp"), None),
            P(("group", "expert", "dp"), None),
            P("expert", "dp", None),
            P("expert", "dp", None),
            P("expert", "dp", None),
            P("expert", None, None),
            P("expert", None, None),
        ),
        out_specs=(
            P(("group", "expert", "dp"), None),
            P(("group", "expert"), None, "dp"),
            P(("group", "expert"), None, "dp"),
        ),
        check_vma=False,
    )
```

```python
import functools

import jax
import jax.numpy as jnp
from jax import lax
from jax.experimental import pallas as pl
from jax.experimental.pallas import tpu as pltpu
from jax.sharding import PartitionSpec as P

adapter_scale = 2.0
f32 = jnp.float32
bf16 = jnp.bfloat16
lane_count = 128


def ring_order(count, snake):
    if snake and count % 2 == 0:
        return list(range(0, count, 2)) + list(range(count - 1, 0, -2))
    return list(range(count))


def matmul(a, b):
    return jnp.dot(a, b, preferred_element_type=f32)


def matmul_bt(a, b):
    return lax.dot_general(a, b, (((1,), (1,)), ((), ())), preferred_element_type=f32)


def matmul_at(a, b):
    return lax.dot_general(a, b, (((0,), (0,)), ((), ())), preferred_element_type=f32)


def stacked(piece_refs, span):
    return jnp.concatenate([ref[:, span] for ref in piece_refs], axis=0)


class Plan:
    def __init__(self, parts, depth, model_width, hidden_width, rank, experts):
        self.parts = parts
        self.depth = depth
        self.model_width = model_width
        self.hidden_width = hidden_width
        self.rank = rank
        self.experts = experts
        self.wide = experts * hidden_width
        self.ranks = experts * rank

    def spans(self):
        if self.parts == 1:
            return [slice(0, self.model_width)]
        core = lax.axis_index("dp")
        return [
            pl.ds(pl.multiple_of(at * self.depth, self.depth), self.depth) for at in (core, 1 - core)
        ]

    def forward(self, token_refs, factor_in_ref, weight_refs):
        gate_pre, up_pre = 0.0, 0.0
        for span, weight in zip(self.spans(), weight_refs):
            tokens_in = stacked(token_refs, span)
            gate_pre += matmul(tokens_in, weight[:, : self.wide])
            up_pre += matmul(tokens_in, weight[:, self.wide : 2 * self.wide])
        logistic = 1.0 / (1.0 + jnp.exp(-gate_pre))
        activation = gate_pre * logistic
        derivative = logistic * (1.0 + gate_pre * (1.0 - logistic))
        hidden = (activation * up_pre).astype(bf16)
        low_rank = matmul_bt(hidden, factor_in_ref[...])
        return activation, up_pre * derivative, hidden, low_rank

    def scales(self, grad_refs):
        columns = stacked(grad_refs, slice(self.model_width, None)).astype(f32)
        lane = lax.broadcasted_iota(jnp.int32, columns.shape, 1)
        first = lax.axis_index("expert") * self.experts
        return [
            jnp.sum(jnp.where(lane == first + j, columns, 0.0), axis=1, keepdims=True)
            for j in range(self.experts)
        ]

    def spread(self, scales, width):
        rows = scales[0].shape[0]
        at = lax.broadcasted_iota(jnp.int32, (rows, self.experts * width), 1)
        out = jnp.broadcast_to(scales[0], at.shape)
        for j in range(1, self.experts):
            out = jnp.where(at >= j * width, scales[j], out)
        return out

    def backward(
        self, grad_refs, activation, slope, factor_in_ref, factor_out_ref, weight_refs, rows_ref
    ):
        scales = self.scales(grad_refs)
        adapter_back, grad_down = 0.0, 0.0
        spans = self.spans()
        for span, weight in zip(spans, weight_refs):
            grad_in = stacked(grad_refs, span)
            adapter_back += matmul_bt(grad_in, factor_out_ref[:, span])
            grad_down += matmul(grad_in, weight[:, 2 * self.wide :])
        adapter_back = adapter_back.astype(bf16)
        grad_hidden = self.spread(scales, self.hidden_width) * (
            grad_down + adapter_scale * matmul(adapter_back, factor_in_ref[...])
        )
        grad_gate = (grad_hidden * slope).astype(bf16)
        grad_up = (grad_hidden * activation).astype(bf16)
        for span, weight in zip(spans, weight_refs):
            rows_ref[:, span] = matmul_bt(grad_gate, weight[:, : self.wide]) + matmul_bt(
                grad_up, weight[:, self.wide : 2 * self.wide]
            )
        rank_scale = self.spread(scales, self.rank)
        return rank_scale, (rank_scale * adapter_back.astype(f32)).astype(bf16)

    def adapters(self, grad_refs, hidden, low_scaled, back_scaled, total_refs, out_refs):
        grad_all = stacked(grad_refs, slice(0, self.model_width))
        for total, out, value in zip(
            total_refs, out_refs, (matmul_at(back_scaled, hidden), matmul_at(low_scaled, grad_all))
        ):
            out[...] = total[...] + adapter_scale * value


def whole_kernel(plan, pieces, blocks, keep_rows, *refs):
    token_refs, grad_refs, refs = refs[:pieces], refs[pieces : 2 * pieces], refs[2 * pieces :]
    factor_in_ref, factor_out_ref, refs = refs[0], refs[1], refs[2:]
    weight_refs, refs = refs[: plan.parts], refs[plan.parts :]
    total_refs, refs = refs[:2], refs[2:]
    if keep_rows:
        rows_ref, refs = refs[0], refs[1:]
    else:
        *refs, rows_ref = refs
    out_refs, send_refs = refs[:2], refs[2:]
    activation, slope, hidden, low_rank = plan.forward(token_refs, factor_in_ref, weight_refs)
    rank_scale, back_scaled = plan.backward(
        grad_refs, activation, slope, factor_in_ref, factor_out_ref, weight_refs, rows_ref
    )
    for (first_row, span), send_ref in zip(blocks, send_refs):
        send_ref[...] = rows_ref[first_row : first_row + send_ref.shape[0], span].astype(bf16)
    low_scaled = (rank_scale * low_rank).astype(bf16)
    plan.adapters(grad_refs, hidden, low_scaled, back_scaled, total_refs, out_refs)


def prepare_kernel(plan, *refs):
    raw_refs, refs = refs[:3], refs[3:]
    out_grad_ref, ids_ref, route_ref, factor_ref = refs[:4]
    tokens_ref, refs = refs[4], refs[5:]
    packed_ref, grads_ref, tokens_held_ref, factor_in_ref, ids_held, route_held, sems = refs
    width, rank = plan.hidden_width, plan.rank
    pairs = [(ids_ref, ids_held), (route_ref, route_held)]
    pairs.append((out_grad_ref, grads_ref.at[:, : plan.model_width]))
    pairs.append((tokens_ref, tokens_held_ref.at[:, : plan.model_width]))
    for kind in range(3):
        for expert in range(plan.experts):
            at = kind * plan.wide + expert * width
            pairs.append((raw_refs[kind].at[expert], packed_ref.at[:, at : at + width]))
    for expert in range(plan.experts):
        block = factor_in_ref.at[
            expert * rank : (expert + 1) * rank, expert * width : (expert + 1) * width
        ]
        pairs.append((factor_ref.at[expert], block))
    copies = [
        pltpu.make_async_copy(source, target, sems.at[at])
        for at, (source, target) in enumerate(pairs)
    ]
    for copy in copies:
        copy.start()
    for expert in range(plan.experts):
        for other in range(plan.experts):
            if other != expert:
                factor_in_ref[
                    expert * rank : (expert + 1) * rank, other * width : (other + 1) * width
                ] = jnp.zeros((rank, width), bf16)
    copies[0].wait()
    copies[1].wait()
    rows, lanes = grads_ref.shape[0], grads_ref.shape[1] - plan.model_width
    expert_at = lax.broadcasted_iota(jnp.int32, (lanes, rows), 0)
    ids, route = ids_held[...], route_held[...].astype(f32)
    dense = jnp.zeros((lanes, rows), f32)
    for k in range(ids.shape[0]):
        dense = jnp.where(ids[k : k + 1, :] == expert_at, route[k : k + 1, :], dense)
    dense = dense.T.astype(bf16)
    grads_ref[:, plan.model_width :] = dense
    tokens_held_ref[:, plan.model_width :] = dense
    for copy in copies[2:]:
        copy.wait()


def add_kernel(blocks, skip, *refs):
    rows_ref, refs = refs[0], list(refs[1:])
    skipped_ref = refs.pop(len(blocks)) if skip else None
    for at, (first_row, span, taken, way) in enumerate(blocks):
        out = refs[len(blocks) + at]
        rows = rows_ref[first_row : first_row + out.shape[0], span]
        total = rows + refs[at][:, taken].astype(f32)
        if skip:
            here = skip[0]() == (way == "ahead")
            total = total + jnp.where(here, skipped_ref[:, skip[1]].astype(f32), 0.0)
        out[...] = total.astype(bf16)


def add_sums(rows, row_count, blocks, arrived, skip):
    operands = [rows, *arrived]
    return pl.pallas_call(
        functools.partial(add_kernel, blocks, skip),
        out_shape=tuple(
            jax.ShapeDtypeStruct((row_count, len(range(*span.indices(rows.shape[1])))), bf16)
            for _, span, _, _ in blocks
        ),
        in_specs=[pl.BlockSpec(memory_space=pltpu.VMEM)] * len(operands),
        out_specs=(pl.BlockSpec(memory_space=pltpu.VMEM),) * len(blocks),
        compiler_params=pltpu.CompilerParams(vmem_limit_bytes=16 * 1024 * 1024),
    )(*operands)


def half_rows_kernel(half, first_ref, second_ref, top_ref, bottom_ref):
    top_ref[...] = first_ref[:half]
    bottom_ref[...] = second_ref[half:]


def halves(first, second, half):
    out = ((half, first.shape[1]), first.dtype)
    return simple_call(functools.partial(half_rows_kernel, half), [first, second], [out, out])


def halves_kernel(plan, total_in_ref, total_out_ref, keep_ref, send_ref):
    first = lax.axis_index("dp") == 0
    middle, narrow = plan.model_width // 2, plan.hidden_width // 2
    low, high = total_out_ref[:, :middle], total_out_ref[:, middle:]
    keep_ref[:, :middle] = jnp.where(first, low, high)
    send_ref[:, :middle] = jnp.where(first, high, low)
    for expert in range(plan.experts):
        rows = slice(expert * plan.rank, (expert + 1) * plan.rank)
        block = total_in_ref[rows, expert * plan.hidden_width : (expert + 1) * plan.hidden_width]
        low, high = block[:, :narrow], block[:, narrow:]
        keep_ref[rows, middle:] = jnp.where(first, low, high)
        send_ref[rows, middle:] = jnp.where(first, high, low)


def joined_kernel(plan, keep_ref, other_ref, in_ref, out_ref):
    middle = plan.model_width // 2
    for expert in range(plan.experts):
        rows = slice(expert * plan.rank, (expert + 1) * plan.rank)
        out_ref[expert] = keep_ref[rows, :middle] + other_ref[rows, :middle]
        in_ref[expert] = keep_ref[rows, middle:] + other_ref[rows, middle:]


def last_kernel(first_row, spans, *refs):
    rows_ref, out_ref = refs[0], refs[-1]
    for at, span in enumerate(spans):
        total = rows_ref[first_row : first_row + out_ref.shape[0], span]
        for incoming in refs[1 + 2 * at : 3 + 2 * at]:
            total = total + incoming[...].astype(f32)
        out_ref[:, span] = total.astype(bf16)


def simple_call(kernel, operands, outs):
    return pl.pallas_call(
        kernel,
        out_shape=tuple(jax.ShapeDtypeStruct(shape, dtype) for shape, dtype in outs),
        in_specs=[pl.BlockSpec(memory_space=pltpu.VMEM)] * len(operands),
        out_specs=(pl.BlockSpec(memory_space=pltpu.VMEM),) * len(outs),
        compiler_params=pltpu.CompilerParams(vmem_limit_bytes=16 * 1024 * 1024),
    )(*operands)


def expert_call(plan, pieces, blocks, block_rows, operands, totals, keep_rows):
    rows = sum(piece[0].shape[0] for piece in pieces)
    operands = [p[0] for p in pieces] + [p[1] for p in pieces] + [*operands, *totals]
    shape = (rows, plan.model_width)
    outs = [(shape, f32)] * keep_rows + [(total.shape, f32) for total in totals]
    widths = [len(range(*span.indices(plan.model_width))) for _, span in blocks]
    outs += [((block_rows, width), bf16) for width in widths]
    return pl.pallas_call(
        functools.partial(whole_kernel, plan, len(pieces), blocks, keep_rows),
        scratch_shapes=[] if keep_rows else [pltpu.VMEM(shape, f32)],
        out_shape=tuple(jax.ShapeDtypeStruct(shape, dtype) for shape, dtype in outs),
        in_specs=[pl.BlockSpec(memory_space=pltpu.VMEM)] * len(operands),
        out_specs=(pl.BlockSpec(memory_space=pltpu.VMEM),) * len(outs),
        compiler_params=pltpu.CompilerParams(vmem_limit_bytes=16 * 1024 * 1024),
        cost_estimate=pl.CostEstimate(
            flops=10 * rows * plan.model_width * plan.wide,
            bytes_accessed=sum(op.size * op.dtype.itemsize for op in operands),
            transcendentals=0,
        ),
    )(*operands)


def per_device(
    snake,
    tokens,
    out_grad,
    expert_ids,
    route_weight,
    gate_weight,
    up_weight,
    down_weight,
    adapter_in,
    adapter_out,
):
    peer_count = lax.axis_size("expert")
    dp_count = lax.axis_size("dp")
    token_count, model_width = tokens.shape
    local_count, depth, hidden_width = gate_weight.shape
    rank = adapter_in.shape[1]
    expert_total = local_count * peer_count
    order = ring_order(peer_count, snake)
    forward = [(order[i], order[(i + 1) % peer_count]) for i in range(peer_count)]
    backward = [(b, a) for a, b in forward]
    swap = [(0, 1), (1, 0)]
    parts = 2 if dp_count == 2 else 1
    plan = Plan(parts, depth, model_width, hidden_width, rank, local_count)
    wide, ranks = plan.wide, plan.ranks

    lanes = -(-expert_total // lane_count) * lane_count
    mine, grads, tokens_held, factor_in = pl.pallas_call(
        functools.partial(prepare_kernel, plan),
        out_shape=(
            jax.ShapeDtypeStruct((depth, 3 * wide), bf16),
            jax.ShapeDtypeStruct((token_count, model_width + lanes), bf16),
            jax.ShapeDtypeStruct((token_count, model_width + lanes), bf16),
            jax.ShapeDtypeStruct((ranks, wide), bf16),
        ),
        in_specs=[pl.BlockSpec(memory_space=pltpu.HBM)] * 8,
        out_specs=(pl.BlockSpec(memory_space=pltpu.VMEM),) * 4,
        scratch_shapes=[
            pltpu.VMEM(expert_ids.shape[::-1], jnp.int32),
            pltpu.VMEM(route_weight.shape[::-1], bf16),
            pltpu.SemaphoreType.DMA((4 + 4 * local_count,)),
        ],
        compiler_params=pltpu.CompilerParams(vmem_limit_bytes=16 * 1024 * 1024),
    )(
        *(
            pltpu.with_memory_space_constraint(x, pltpu.HBM)
            for x in (
                gate_weight,
                up_weight,
                down_weight,
                out_grad,
                expert_ids.T,
                route_weight.T,
                adapter_in,
                tokens,
            )
        )
    )
    if parts == 2:
        weights = [mine, lax.ppermute(mine, "dp", swap)]
    else:
        weights = [lax.all_gather(mine, "dp", axis=0, tiled=True)]
    weights = [pltpu.with_memory_space_constraint(w, pltpu.VMEM) for w in weights]
    factor_out = adapter_out.reshape(ranks, model_width)

    full = (peer_count - 1) // 2
    split = peer_count % 2 == 0
    totals = (jnp.zeros((ranks, wide), f32), jnp.zeros((ranks, model_width), f32))
    behind, ahead = [(tokens_held, grads)], [(tokens_held, grads)]
    rows_at = [None]

    middle = model_width // 2
    columns = {"left": slice(0, middle), "right": slice(middle, model_width)}
    everything = slice(0, model_width)
    ways = {"back": (0, backward), "ahead": (token_count, forward)}
    moving = {}

    def send(value, way):
        return lax.ppermute(value, "expert", ways[way][1])

    def run(pieces, blocks, totals, keep_rows=True):
        operands = [factor_in, factor_out, *weights]
        return expert_call(plan, pieces, blocks, token_count, operands, totals, keep_rows)

    def after(value, *arrays):
        held = []
        for x in arrays:
            x, value = lax.optimization_barrier((x, value))
            held.append(x)
        return value, held

    for d in range(full):
        if d > 1:
            totals, (tokens_b, tokens_a) = after(totals, behind[d][0], ahead[d][0])
            grads_b, grads_a = behind[d][1], ahead[d][1]
            behind[d], ahead[d] = (tokens_b, grads_b), (tokens_a, grads_a)
        behind.append(tuple(lax.ppermute(x, "expert", forward) for x in behind[d]))
        ahead.append(tuple(lax.ppermute(x, "expert", backward) for x in ahead[d]))
        if d > 0:
            pieces = [behind[d], ahead[d]] + ([behind[0]] if d == 1 else [])
            rows_d, *totals = run(pieces, [], totals)
            rows_at.append(rows_d)
    if split:
        half = token_count // 2
        totals, (tokens_b, tokens_a) = after(totals, behind[full][0], ahead[full][0])
        tokens_b, tokens_a = halves(tokens_b, tokens_a, half)
        grads_b, grads_a = halves(behind[full][1], ahead[full][1], half)
        far = [
            tuple(lax.ppermute(x, "expert", forward) for x in (tokens_b, grads_b)),
            tuple(lax.ppermute(x, "expert", backward) for x in (tokens_a, grads_a)),
        ]
    pieces = [behind[full], ahead[full]]
    blocks = [(first_row, everything) for first_row, _ in ways.values()]
    outs = run(pieces, blocks, totals, keep_rows=False)
    totals = outs[:2]
    for way, value in zip(ways, outs[2:]):
        for side in columns:
            moving[side, way] = send(value, way) if side == "left" else moving["left", way]
    skipped = []
    if split:
        *totals, value = run(far, [(0, everything)], totals, keep_rows=False)
        pairs = [
            (order[i], order[(i + (full if i % 2 == 0 else -full)) % peer_count])
            for i in range(peer_count)
        ]
        skipped.append(lax.ppermute(value, "expert", pairs))

    def goes_ahead():
        me = lax.axis_index("expert")
        place = jnp.where(me % 2 == 0, me // 2, peer_count - 1 - me // 2) if snake else me
        return (place + full) % 2 == 0

    for d in range(full - 1, 0, -1):
        for side, span in columns.items():
            blocks, arrived = [], []
            for way, (first_row, _) in ways.items():
                blocks.append((first_row, span, span if d == full - 1 else slice(0, middle), way))
                arrived.append(moving[side, way])
            skip = (goes_ahead, span) if d == 1 and split else None
            values = add_sums(
                rows_at[d], token_count, blocks, arrived + (skipped if skip else []), skip
            )
            for way, value in zip(ways, values):
                moving[side, way] = send(value, way)
    grad_tokens = pl.pallas_call(
        functools.partial(last_kernel, 2 * token_count, list(columns.values())),
        out_shape=jax.ShapeDtypeStruct((token_count, model_width), bf16),
        in_specs=[pl.BlockSpec(memory_space=pltpu.VMEM)] * 5,
        out_specs=pl.BlockSpec(memory_space=pltpu.VMEM),
        compiler_params=pltpu.CompilerParams(vmem_limit_bytes=16 * 1024 * 1024),
    )(rows_at[1], *(moving[side, way] for side in columns for way in ways))

    narrow = hidden_width // dp_count
    if dp_count == 2:
        half = ((ranks, middle + narrow), f32)
        keep, other = simple_call(functools.partial(halves_kernel, plan), totals, [half, half])
        grad_in_all, grad_out_all = simple_call(
            functools.partial(joined_kernel, plan),
            [keep, lax.ppermute(other, "dp", swap)],
            [((local_count, rank, narrow), f32), ((local_count, rank, middle), f32)],
        )
        return (grad_tokens, grad_in_all, grad_out_all)
    grad_in = jnp.stack(
        [
            totals[0][j * rank : (j + 1) * rank, j * hidden_width : (j + 1) * hidden_width]
            for j in range(local_count)
        ]
    )
    both = jnp.concatenate(
        [
            grad_in.reshape(ranks, dp_count, narrow),
            totals[1].reshape(ranks, dp_count, model_width // dp_count),
        ],
        axis=2,
    ).transpose(1, 0, 2)
    summed = lax.psum_scatter(both, "dp", scatter_dimension=0, tiled=False)
    grad_in_all = summed[:, :narrow].reshape(local_count, rank, narrow)
    grad_out_all = summed[:, narrow:].reshape(local_count, rank, model_width // dp_count)
    return (grad_tokens, grad_in_all, grad_out_all)


def solution(mesh):
    snake = mesh.shape["dp"] == 2
    return jax.shard_map(
        functools.partial(per_device, snake),
        mesh=mesh,
        in_specs=(
            P(("group", "expert", "dp"), None),
            P(("group", "expert", "dp"), None),
            P(("group", "expert", "dp"), None),
            P(("group", "expert", "dp"), None),
            P("expert", "dp", None),
            P("expert", "dp", None),
            P("expert", "dp", None),
            P("expert", None, None),
            P("expert", None, None),
        ),
        out_specs=(
            P(("group", "expert", "dp"), None),
            P(("group", "expert"), None, "dp"),
            P(("group", "expert"), None, "dp"),
        ),
        check_vma=False,
    )
```

```python
import functools

import jax
import jax.numpy as jnp
from jax import lax
from jax.experimental import pallas as pl
from jax.experimental.pallas import tpu as pltpu
from jax.sharding import PartitionSpec as P

adapter_scale = 2.0
f32 = jnp.float32
bf16 = jnp.bfloat16
lane_count = 128


def ring_order(count, snake):
    if snake and count % 2 == 0:
        return list(range(0, count, 2)) + list(range(count - 1, 0, -2))
    return list(range(count))


def matmul(a, b):
    return jnp.dot(a, b, preferred_element_type=f32)


def matmul_bt(a, b):
    return lax.dot_general(a, b, (((1,), (1,)), ((), ())), preferred_element_type=f32)


def matmul_at(a, b):
    return lax.dot_general(a, b, (((0,), (0,)), ((), ())), preferred_element_type=f32)


def stacked(piece_refs, span):
    return jnp.concatenate([ref[:, span] for ref in piece_refs], axis=0)


class Plan:
    def __init__(self, parts, depth, model_width, hidden_width, rank, experts, peers, snake):
        self.parts = parts
        self.depth = depth
        self.model_width = model_width
        self.hidden_width = hidden_width
        self.rank = rank
        self.experts = experts
        self.wide = experts * hidden_width
        self.ranks = experts * rank
        self.peers = peers
        self.snake = snake

    def spans(self):
        if self.parts == 1:
            return [slice(0, self.model_width)]
        core = lax.axis_index("dp")
        return [
            pl.ds(pl.multiple_of(at * self.depth, self.depth), self.depth) for at in (core, 1 - core)
        ]

    def forward(self, token_refs, factor_in_ref, weight_refs):
        gate_pre, up_pre = 0.0, 0.0
        for span, weight in zip(self.spans(), weight_refs):
            tokens_in = stacked(token_refs, span)
            gate_pre += matmul(tokens_in, weight[:, : self.wide])
            up_pre += matmul(tokens_in, weight[:, self.wide : 2 * self.wide])
        logistic = 1.0 / (1.0 + jnp.exp(-gate_pre))
        activation = gate_pre * logistic
        derivative = logistic * (1.0 + gate_pre * (1.0 - logistic))
        hidden = (activation * up_pre).astype(bf16)
        low_rank = matmul_bt(hidden, factor_in_ref[...])
        return activation, up_pre * derivative, hidden, low_rank

    def scales(self, share_ref, offsets, rows):
        place = self.place()
        pieces = []
        for offset in offsets:
            source = self.device_at(lax.rem(place + offset + self.peers, self.peers))
            block = jnp.zeros(share_ref.shape[1:], f32)
            for peer in range(self.peers):
                block = jnp.where(source == peer, share_ref[peer], block)
            pieces.append(block.T[:rows, :])
        columns = jnp.concatenate(pieces, axis=0)
        return [columns[:, j : j + 1] for j in range(self.experts)]

    def place(self):
        me = lax.axis_index("expert")
        return jnp.where(me % 2 == 0, me // 2, self.peers - 1 - me // 2) if self.snake else me

    def device_at(self, place):
        if not self.snake:
            return place
        return jnp.where(place < self.peers // 2, 2 * place, 2 * (self.peers - 1 - place) + 1)

    def spread(self, scales, width):
        rows = scales[0].shape[0]
        at = lax.broadcasted_iota(jnp.int32, (rows, self.experts * width), 1)
        out = jnp.broadcast_to(scales[0], at.shape)
        for j in range(1, self.experts):
            out = jnp.where(at >= j * width, scales[j], out)
        return out

    def backward(
        self, grad_refs, scales, activation, slope, factor_in_ref, factor_out_ref, weight_refs, rows_ref
    ):
        adapter_back, grad_down = 0.0, 0.0
        spans = self.spans()
        for span, weight in zip(spans, weight_refs):
            grad_in = stacked(grad_refs, span)
            adapter_back += matmul_bt(grad_in, factor_out_ref[:, span])
            grad_down += matmul(grad_in, weight[:, 2 * self.wide :])
        adapter_back = adapter_back.astype(bf16)
        grad_hidden = self.spread(scales, self.hidden_width) * (
            grad_down + adapter_scale * matmul(adapter_back, factor_in_ref[...])
        )
        grad_gate = (grad_hidden * slope).astype(bf16)
        grad_up = (grad_hidden * activation).astype(bf16)
        for span, weight in zip(spans, weight_refs):
            rows_ref[:, span] = matmul_bt(grad_gate, weight[:, : self.wide]) + matmul_bt(
                grad_up, weight[:, self.wide : 2 * self.wide]
            )
        rank_scale = self.spread(scales, self.rank)
        return rank_scale, (rank_scale * adapter_back.astype(f32)).astype(bf16)

    def adapters(self, grad_refs, hidden, low_scaled, back_scaled, total_refs, out_refs):
        grad_all = stacked(grad_refs, slice(0, self.model_width))
        for total, out, value in zip(
            total_refs, out_refs, (matmul_at(back_scaled, hidden), matmul_at(low_scaled, grad_all))
        ):
            out[...] = total[...] + adapter_scale * value


def whole_kernel(plan, pieces, blocks, keep_rows, offsets, piece_rows, *refs):
    token_refs, grad_refs, refs = refs[:pieces], refs[pieces : 2 * pieces], refs[2 * pieces :]
    share_ref, factor_in_ref, factor_out_ref, refs = refs[0], refs[1], refs[2], refs[3:]
    weight_refs, refs = refs[: plan.parts], refs[plan.parts :]
    total_refs, refs = refs[:2], refs[2:]
    if keep_rows:
        rows_ref, refs = refs[0], refs[1:]
    else:
        *refs, rows_ref = refs
    out_refs, send_refs = refs[:2], refs[2:]
    activation, slope, hidden, low_rank = plan.forward(token_refs, factor_in_ref, weight_refs)
    rank_scale, back_scaled = plan.backward(
        grad_refs,
        plan.scales(share_ref, offsets, piece_rows),
        activation,
        slope,
        factor_in_ref,
        factor_out_ref,
        weight_refs,
        rows_ref,
    )
    for (first_row, span), send_ref in zip(blocks, send_refs):
        send_ref[...] = rows_ref[first_row : first_row + send_ref.shape[0], span].astype(bf16)
    low_scaled = (rank_scale * low_rank).astype(bf16)
    plan.adapters(grad_refs, hidden, low_scaled, back_scaled, total_refs, out_refs)


def prepare_kernel(plan, *refs):
    raw_refs, ids_ref, route_ref, factor_ref = refs[:3], refs[3], refs[4], refs[5]
    packed_ref, share_ref, factor_in_ref, ids_held, route_held, sems = refs[6:]
    width, rank = plan.hidden_width, plan.rank
    pairs = [(ids_ref, ids_held), (route_ref, route_held)]
    for kind in range(3):
        for expert in range(plan.experts):
            at = kind * plan.wide + expert * width
            pairs.append((raw_refs[kind].at[expert], packed_ref.at[:, at : at + width]))
    for expert in range(plan.experts):
        block = factor_in_ref.at[
            expert * rank : (expert + 1) * rank, expert * width : (expert + 1) * width
        ]
        pairs.append((factor_ref.at[expert], block))
    copies = [
        pltpu.make_async_copy(source, target, sems.at[at])
        for at, (source, target) in enumerate(pairs)
    ]
    for copy in copies:
        copy.start()
    for expert in range(plan.experts):
        for other in range(plan.experts):
            if other != expert:
                factor_in_ref[
                    expert * rank : (expert + 1) * rank, other * width : (other + 1) * width
                ] = jnp.zeros((rank, width), bf16)
    copies[0].wait()
    copies[1].wait()
    ids, route = ids_held[...], route_held[...].astype(f32)
    rows = ids.shape[1]
    sublanes, lanes = share_ref.shape[1:]
    row_at = lax.broadcasted_iota(jnp.int32, (plan.peers * sublanes, rows), 0)
    expert_at = row_at // sublanes * plan.experts + row_at % sublanes
    expert_at = jnp.where(row_at % sublanes < plan.experts, expert_at, -1)
    dense = jnp.zeros(expert_at.shape, f32)
    for k in range(ids.shape[0]):
        dense = jnp.where(ids[k : k + 1, :] == expert_at, route[k : k + 1, :], dense)
    share_ref[...] = jnp.zeros(share_ref.shape, f32)
    for peer in range(plan.peers):
        share_ref[peer, :, :rows] = dense[peer * sublanes : (peer + 1) * sublanes, :]
    for copy in copies[2:]:
        copy.wait()


def add_kernel(blocks, skip, *refs):
    rows_ref, refs = refs[0], list(refs[1:])
    skipped_ref = refs.pop(len(blocks)) if skip else None
    for at, (first_row, span, taken, way) in enumerate(blocks):
        out = refs[len(blocks) + at]
        rows = rows_ref[first_row : first_row + out.shape[0], span]
        total = rows + refs[at][:, taken].astype(f32)
        if skip:
            here = skip[0]() == (way == "ahead")
            total = total + jnp.where(here, skipped_ref[:, skip[1]].astype(f32), 0.0)
        out[...] = total.astype(bf16)


def add_sums(rows, row_count, blocks, arrived, skip):
    operands = [rows, *arrived]
    return pl.pallas_call(
        functools.partial(add_kernel, blocks, skip),
        out_shape=tuple(
            jax.ShapeDtypeStruct((row_count, len(range(*span.indices(rows.shape[1])))), bf16)
            for _, span, _, _ in blocks
        ),
        in_specs=[pl.BlockSpec(memory_space=pltpu.VMEM)] * len(operands),
        out_specs=(pl.BlockSpec(memory_space=pltpu.VMEM),) * len(blocks),
        compiler_params=pltpu.CompilerParams(vmem_limit_bytes=20 * 1024 * 1024),
    )(*operands)


def half_rows_kernel(half, first_ref, second_ref, top_ref, bottom_ref):
    top_ref[...] = first_ref[:half]
    bottom_ref[...] = second_ref[half:]


def halves(first, second, half):
    out = ((half, first.shape[1]), first.dtype)
    return simple_call(functools.partial(half_rows_kernel, half), [first, second], [out, out])


def halves_kernel(plan, total_in_ref, total_out_ref, keep_ref, send_ref):
    first = lax.axis_index("dp") == 0
    middle, narrow = plan.model_width // 2, plan.hidden_width // 2
    low, high = total_out_ref[:, :middle], total_out_ref[:, middle:]
    keep_ref[:, :middle] = jnp.where(first, low, high)
    send_ref[:, :middle] = jnp.where(first, high, low)
    for expert in range(plan.experts):
        rows = slice(expert * plan.rank, (expert + 1) * plan.rank)
        block = total_in_ref[rows, expert * plan.hidden_width : (expert + 1) * plan.hidden_width]
        low, high = block[:, :narrow], block[:, narrow:]
        keep_ref[rows, middle:] = jnp.where(first, low, high)
        send_ref[rows, middle:] = jnp.where(first, high, low)


def joined_kernel(plan, keep_ref, other_ref, in_ref, out_ref):
    middle = plan.model_width // 2
    for expert in range(plan.experts):
        rows = slice(expert * plan.rank, (expert + 1) * plan.rank)
        out_ref[expert] = keep_ref[rows, :middle] + other_ref[rows, :middle]
        in_ref[expert] = keep_ref[rows, middle:] + other_ref[rows, middle:]


def last_kernel(first_row, spans, *refs):
    rows_ref, out_ref = refs[0], refs[-1]
    for at, span in enumerate(spans):
        total = rows_ref[first_row : first_row + out_ref.shape[0], span]
        for incoming in refs[1 + 2 * at : 3 + 2 * at]:
            total = total + incoming[...].astype(f32)
        out_ref[:, span] = total.astype(bf16)


def simple_call(kernel, operands, outs):
    return pl.pallas_call(
        kernel,
        out_shape=tuple(jax.ShapeDtypeStruct(shape, dtype) for shape, dtype in outs),
        in_specs=[pl.BlockSpec(memory_space=pltpu.VMEM)] * len(operands),
        out_specs=(pl.BlockSpec(memory_space=pltpu.VMEM),) * len(outs),
        compiler_params=pltpu.CompilerParams(vmem_limit_bytes=20 * 1024 * 1024),
    )(*operands)


def expert_call(plan, pieces, offsets, blocks, block_rows, operands, totals, keep_rows):
    rows = sum(piece[0].shape[0] for piece in pieces)
    operands = [p[0] for p in pieces] + [p[1] for p in pieces] + [*operands, *totals]
    shape = (rows, plan.model_width)
    outs = [(shape, f32)] * keep_rows + [(total.shape, f32) for total in totals]
    widths = [len(range(*span.indices(plan.model_width))) for _, span in blocks]
    outs += [((block_rows, width), bf16) for width in widths]
    return pl.pallas_call(
        functools.partial(whole_kernel, plan, len(pieces), blocks, keep_rows, offsets, block_rows),
        scratch_shapes=[] if keep_rows else [pltpu.VMEM(shape, f32)],
        out_shape=tuple(jax.ShapeDtypeStruct(shape, dtype) for shape, dtype in outs),
        in_specs=[pl.BlockSpec(memory_space=pltpu.VMEM)] * len(operands),
        out_specs=(pl.BlockSpec(memory_space=pltpu.VMEM),) * len(outs),
        compiler_params=pltpu.CompilerParams(vmem_limit_bytes=20 * 1024 * 1024),
        cost_estimate=pl.CostEstimate(
            flops=10 * rows * plan.model_width * plan.wide,
            bytes_accessed=sum(op.size * op.dtype.itemsize for op in operands),
            transcendentals=0,
        ),
    )(*operands)


def per_device(
    snake,
    tokens,
    out_grad,
    expert_ids,
    route_weight,
    gate_weight,
    up_weight,
    down_weight,
    adapter_in,
    adapter_out,
):
    peer_count = lax.axis_size("expert")
    dp_count = lax.axis_size("dp")
    token_count, model_width = tokens.shape
    local_count, depth, hidden_width = gate_weight.shape
    rank = adapter_in.shape[1]
    expert_total = local_count * peer_count
    order = ring_order(peer_count, snake)
    forward = [(order[i], order[(i + 1) % peer_count]) for i in range(peer_count)]
    backward = [(b, a) for a, b in forward]
    swap = [(0, 1), (1, 0)]
    parts = 2 if dp_count == 2 else 1
    plan = Plan(parts, depth, model_width, hidden_width, rank, local_count, peer_count, snake)
    wide, ranks = plan.wide, plan.ranks

    sublanes = -(-local_count // 8) * 8
    lanes = -(-token_count // lane_count) * lane_count
    mine, share, factor_in = pl.pallas_call(
        functools.partial(prepare_kernel, plan),
        out_shape=(
            jax.ShapeDtypeStruct((depth, 3 * wide), bf16),
            jax.ShapeDtypeStruct((peer_count, sublanes, lanes), f32),
            jax.ShapeDtypeStruct((ranks, wide), bf16),
        ),
        in_specs=[pl.BlockSpec(memory_space=pltpu.HBM)] * 6,
        out_specs=(pl.BlockSpec(memory_space=pltpu.VMEM),) * 3,
        scratch_shapes=[
            pltpu.VMEM(expert_ids.shape[::-1], jnp.int32),
            pltpu.VMEM(route_weight.shape[::-1], bf16),
            pltpu.SemaphoreType.DMA((2 + 4 * local_count,)),
        ],
        compiler_params=pltpu.CompilerParams(vmem_limit_bytes=20 * 1024 * 1024),
    )(
        *(
            pltpu.with_memory_space_constraint(x, pltpu.HBM)
            for x in (gate_weight, up_weight, down_weight, expert_ids.T, route_weight.T, adapter_in)
        )
    )
    share = lax.all_to_all(share, "expert", split_axis=0, concat_axis=0, tiled=True)
    if parts == 2:
        weights = [mine, lax.ppermute(mine, "dp", swap)]
    else:
        weights = [lax.all_gather(mine, "dp", axis=0, tiled=True)]
    weights = [pltpu.with_memory_space_constraint(w, pltpu.VMEM) for w in weights]
    factor_out = adapter_out.reshape(ranks, model_width)

    full = (peer_count - 1) // 2
    split = peer_count % 2 == 0
    totals = (jnp.zeros((ranks, wide), f32), jnp.zeros((ranks, model_width), f32))
    behind, ahead = [(tokens, out_grad)], [(tokens, out_grad)]
    rows_at = [None]

    middle = model_width // 2
    columns = {"left": slice(0, middle), "right": slice(middle, model_width)}
    everything = slice(0, model_width)
    ways = {"back": (0, backward), "ahead": (token_count, forward)}
    moving = {}

    def send(value, way):
        return lax.ppermute(value, "expert", ways[way][1])

    def run(pieces, offsets, blocks, totals, keep_rows=True):
        operands = [share, factor_in, factor_out, *weights]
        return expert_call(
            plan, pieces, offsets, blocks, token_count, operands, totals, keep_rows
        )

    def after(value, *arrays):
        held = []
        for x in arrays:
            x, value = lax.optimization_barrier((x, value))
            held.append(x)
        return value, held

    for d in range(full):
        if d > 1:
            totals, (tokens_b, tokens_a) = after(totals, behind[d][0], ahead[d][0])
            grads_b, grads_a = behind[d][1], ahead[d][1]
            behind[d], ahead[d] = (tokens_b, grads_b), (tokens_a, grads_a)
        behind.append(tuple(lax.ppermute(x, "expert", forward) for x in behind[d]))
        ahead.append(tuple(lax.ppermute(x, "expert", backward) for x in ahead[d]))
        if d > 0:
            pieces = [behind[d], ahead[d]] + ([behind[0]] if d == 1 else [])
            rows_d, *totals = run(pieces, [-d, d] + [0] * (d == 1), [], totals)
            rows_at.append(rows_d)
    if split:
        half = token_count // 2
        totals, (tokens_b, tokens_a) = after(totals, behind[full][0], ahead[full][0])
        tokens_b, tokens_a = halves(tokens_b, tokens_a, half)
        grads_b, grads_a = halves(behind[full][1], ahead[full][1], half)
        far = [
            tuple(lax.ppermute(x, "expert", forward) for x in (tokens_b, grads_b)),
            tuple(lax.ppermute(x, "expert", backward) for x in (tokens_a, grads_a)),
        ]
    pieces = [behind[full], ahead[full]]
    blocks = [(first_row, everything) for first_row, _ in ways.values()]
    outs = run(pieces, [-full, full], blocks, totals, keep_rows=False)
    totals = outs[:2]
    for way, value in zip(ways, outs[2:]):
        for side in columns:
            moving[side, way] = send(value, way) if side == "left" else moving["left", way]
    skipped = []
    if split:
        *totals, value = run(far, [peer_count // 2], [(0, everything)], totals, keep_rows=False)
        pairs = [
            (order[i], order[(i + (full if i % 2 == 0 else -full)) % peer_count])
            for i in range(peer_count)
        ]
        skipped.append(lax.ppermute(value, "expert", pairs))

    def goes_ahead():
        return (plan.place() + full) % 2 == 0

    for d in range(full - 1, 0, -1):
        for side, span in columns.items():
            blocks, arrived = [], []
            for way, (first_row, _) in ways.items():
                blocks.append((first_row, span, span if d == full - 1 else slice(0, middle), way))
                arrived.append(moving[side, way])
            skip = (goes_ahead, span) if d == 1 and split else None
            values = add_sums(
                rows_at[d], token_count, blocks, arrived + (skipped if skip else []), skip
            )
            for way, value in zip(ways, values):
                moving[side, way] = send(value, way)
    grad_tokens = pl.pallas_call(
        functools.partial(last_kernel, 2 * token_count, list(columns.values())),
        out_shape=jax.ShapeDtypeStruct((token_count, model_width), bf16),
        in_specs=[pl.BlockSpec(memory_space=pltpu.VMEM)] * 5,
        out_specs=pl.BlockSpec(memory_space=pltpu.VMEM),
        compiler_params=pltpu.CompilerParams(vmem_limit_bytes=20 * 1024 * 1024),
    )(rows_at[1], *(moving[side, way] for side in columns for way in ways))

    narrow = hidden_width // dp_count
    if dp_count == 2:
        half = ((ranks, middle + narrow), f32)
        keep, other = simple_call(functools.partial(halves_kernel, plan), totals, [half, half])
        grad_in_all, grad_out_all = simple_call(
            functools.partial(joined_kernel, plan),
            [keep, lax.ppermute(other, "dp", swap)],
            [((local_count, rank, narrow), f32), ((local_count, rank, middle), f32)],
        )
        return (grad_tokens, grad_in_all, grad_out_all)
    grad_in = jnp.stack(
        [
            totals[0][j * rank : (j + 1) * rank, j * hidden_width : (j + 1) * hidden_width]
            for j in range(local_count)
        ]
    )
    both = jnp.concatenate(
        [
            grad_in.reshape(ranks, dp_count, narrow),
            totals[1].reshape(ranks, dp_count, model_width // dp_count),
        ],
        axis=2,
    ).transpose(1, 0, 2)
    summed = lax.psum_scatter(both, "dp", scatter_dimension=0, tiled=False)
    grad_in_all = summed[:, :narrow].reshape(local_count, rank, narrow)
    grad_out_all = summed[:, narrow:].reshape(local_count, rank, model_width // dp_count)
    return (grad_tokens, grad_in_all, grad_out_all)


def solution(mesh):
    snake = mesh.shape["dp"] == 2
    return jax.shard_map(
        functools.partial(per_device, snake),
        mesh=mesh,
        in_specs=(
            P(("group", "expert", "dp"), None),
            P(("group", "expert", "dp"), None),
            P(("group", "expert", "dp"), None),
            P(("group", "expert", "dp"), None),
            P("expert", "dp", None),
            P("expert", "dp", None),
            P("expert", "dp", None),
            P("expert", None, None),
            P("expert", None, None),
        ),
        out_specs=(
            P(("group", "expert", "dp"), None),
            P(("group", "expert"), None, "dp"),
            P(("group", "expert"), None, "dp"),
        ),
        check_vma=False,
    )
```

```python
import functools

import jax
import jax.numpy as jnp
from jax import lax
from jax.experimental import pallas as pl
from jax.experimental.pallas import tpu as pltpu
from jax.sharding import PartitionSpec as P

adapter_scale = 2.0
f32 = jnp.float32
bf16 = jnp.bfloat16
lane_count = 128


def ring_order(count, snake):
    if snake and count % 2 == 0:
        return list(range(0, count, 2)) + list(range(count - 1, 0, -2))
    return list(range(count))


def matmul(a, b):
    return jnp.dot(a, b, preferred_element_type=f32)


def matmul_bt(a, b):
    return lax.dot_general(a, b, (((1,), (1,)), ((), ())), preferred_element_type=f32)


def matmul_at(a, b):
    return lax.dot_general(a, b, (((0,), (0,)), ((), ())), preferred_element_type=f32)


def stacked(piece_refs, span):
    return jnp.concatenate([ref[:, span] for ref in piece_refs], axis=0)


class Plan:
    def __init__(self, parts, depth, model_width, hidden_width, rank, experts):
        self.parts = parts
        self.depth = depth
        self.model_width = model_width
        self.hidden_width = hidden_width
        self.rank = rank
        self.experts = experts
        self.wide = experts * hidden_width
        self.ranks = experts * rank

    def spans(self):
        if self.parts == 1:
            return [slice(0, self.model_width)]
        core = lax.axis_index("dp")
        return [
            pl.ds(pl.multiple_of(at * self.depth, self.depth), self.depth) for at in (core, 1 - core)
        ]

    def forward(self, token_refs, factor_in_ref, weight_refs):
        gate_pre, up_pre = 0.0, 0.0
        for span, weight in zip(self.spans(), weight_refs):
            tokens_in = stacked(token_refs, span)
            gate_pre += matmul(tokens_in, weight[:, : self.wide])
            up_pre += matmul(tokens_in, weight[:, self.wide : 2 * self.wide])
        logistic = 1.0 / (1.0 + jnp.exp(-gate_pre))
        activation = gate_pre * logistic
        derivative = logistic * (1.0 + gate_pre * (1.0 - logistic))
        hidden = (activation * up_pre).astype(bf16)
        low_rank = matmul_bt(hidden, factor_in_ref[...])
        return activation, up_pre * derivative, hidden, low_rank

    def scales(self, grad_refs):
        columns = stacked(grad_refs, slice(self.model_width, None)).astype(f32)
        lane = lax.broadcasted_iota(jnp.int32, columns.shape, 1)
        first = lax.axis_index("expert") * self.experts
        return [
            jnp.sum(jnp.where(lane == first + j, columns, 0.0), axis=1, keepdims=True)
            for j in range(self.experts)
        ]

    def spread(self, scales, width):
        rows = scales[0].shape[0]
        at = lax.broadcasted_iota(jnp.int32, (rows, self.experts * width), 1)
        out = jnp.broadcast_to(scales[0], at.shape)
        for j in range(1, self.experts):
            out = jnp.where(at >= j * width, scales[j], out)
        return out

    def backward(
        self, grad_refs, activation, slope, factor_in_ref, factor_out_ref, weight_refs, rows_ref
    ):
        scales = self.scales(grad_refs)
        adapter_back, grad_down = 0.0, 0.0
        spans = self.spans()
        for span, weight in zip(spans, weight_refs):
            grad_in = stacked(grad_refs, span)
            adapter_back += matmul_bt(grad_in, factor_out_ref[:, span])
            grad_down += matmul(grad_in, weight[:, 2 * self.wide :])
        adapter_back = adapter_back.astype(bf16)
        grad_hidden = self.spread(scales, self.hidden_width) * (
            grad_down + adapter_scale * matmul(adapter_back, factor_in_ref[...])
        )
        grad_gate = (grad_hidden * slope).astype(bf16)
        grad_up = (grad_hidden * activation).astype(bf16)
        for span, weight in zip(spans, weight_refs):
            rows_ref[:, span] = matmul_bt(grad_gate, weight[:, : self.wide]) + matmul_bt(
                grad_up, weight[:, self.wide : 2 * self.wide]
            )
        rank_scale = self.spread(scales, self.rank)
        return rank_scale, (rank_scale * adapter_back.astype(f32)).astype(bf16)

    def adapters(self, grad_refs, hidden, low_scaled, back_scaled, total_refs, out_refs):
        grad_all = stacked(grad_refs, slice(0, self.model_width))
        for total, out, value in zip(
            total_refs, out_refs, (matmul_at(back_scaled, hidden), matmul_at(low_scaled, grad_all))
        ):
            out[...] = total[...] + adapter_scale * value


def whole_kernel(plan, pieces, *refs):
    token_refs, grad_refs, refs = refs[:pieces], refs[pieces : 2 * pieces], refs[2 * pieces :]
    factor_in_ref, factor_out_ref, refs = refs[0], refs[1], refs[2:]
    weight_refs, refs = refs[: plan.parts], refs[plan.parts :]
    total_refs, refs = refs[:2], refs[2:]
    rows_ref, out_refs = refs[0], refs[1:]
    activation, slope, hidden, low_rank = plan.forward(token_refs, factor_in_ref, weight_refs)
    rank_scale, back_scaled = plan.backward(
        grad_refs, activation, slope, factor_in_ref, factor_out_ref, weight_refs, rows_ref
    )
    low_scaled = (rank_scale * low_rank).astype(bf16)
    plan.adapters(grad_refs, hidden, low_scaled, back_scaled, total_refs, out_refs)


def forward_kernel(plan, pieces, *refs):
    token_refs, factor_in_ref, refs = refs[:pieces], refs[pieces], refs[pieces + 1 :]
    weight_refs, out_refs = refs[: plan.parts], refs[plan.parts :]
    for out, value in zip(out_refs, plan.forward(token_refs, factor_in_ref, weight_refs)):
        out[...] = value


def finish(plan, grad_refs, forward, factor_in_ref, factor_out_ref, weight_refs, refs):
    low_scaled_ref, back_scaled_ref, *send_refs, rows_ref = refs
    activation, slope, low_rank = forward
    rank_scale, back_scaled = plan.backward(
        grad_refs, activation, slope, factor_in_ref, factor_out_ref, weight_refs, rows_ref
    )
    for at, send_ref in enumerate(send_refs):
        count = send_ref.shape[0]
        send_ref[...] = rows_ref[at * count : (at + 1) * count, :].astype(bf16)
    low_scaled_ref[...] = (rank_scale * low_rank).astype(bf16)
    back_scaled_ref[...] = back_scaled


def backward_kernel(plan, pieces, *refs):
    grad_refs, refs = refs[:pieces], refs[pieces:]
    activation_ref, slope_ref, low_rank_ref, factor_in_ref, factor_out_ref = refs[:5]
    weight_refs, refs = refs[5 : 5 + plan.parts], refs[5 + plan.parts :]
    forward = (activation_ref[...], slope_ref[...], low_rank_ref[...])
    finish(plan, grad_refs, forward, factor_in_ref, factor_out_ref, weight_refs, refs)


def rows_kernel(plan, pieces, *refs):
    token_refs, grad_refs, refs = refs[:pieces], refs[pieces : 2 * pieces], refs[2 * pieces :]
    factor_in_ref, factor_out_ref, refs = refs[0], refs[1], refs[2:]
    weight_refs, hidden_ref, refs = refs[: plan.parts], refs[plan.parts], refs[plan.parts + 1 :]
    activation, slope, hidden, low_rank = plan.forward(token_refs, factor_in_ref, weight_refs)
    hidden_ref[...] = hidden
    forward = (activation, slope, low_rank)
    finish(plan, grad_refs, forward, factor_in_ref, factor_out_ref, weight_refs, refs)


def adapters_kernel(plan, pieces, groups, *refs):
    grad_refs, refs = refs[:pieces], refs[pieces:]
    hidden, low_scaled, back_scaled = [
        jnp.concatenate([ref[...] for ref in refs[at * groups : (at + 1) * groups]], axis=0)
        for at in range(3)
    ]
    refs = refs[3 * groups :]
    plan.adapters(grad_refs, hidden, low_scaled, back_scaled, refs[:2], refs[2:])


def prepare_kernel(plan, *refs):
    raw_refs, refs = refs[:3], refs[3:]
    out_grad_ref, ids_ref, route_ref, factor_ref = refs[:4]
    tokens_ref, refs = refs[4], refs[5:]
    packed_ref, grads_ref, tokens_held_ref, factor_in_ref, ids_held, route_held, sems = refs
    width, rank = plan.hidden_width, plan.rank
    pairs = [(ids_ref, ids_held), (route_ref, route_held)]
    pairs.append((out_grad_ref, grads_ref.at[:, : plan.model_width]))
    pairs.append((tokens_ref, tokens_held_ref.at[:, : plan.model_width]))
    for kind in range(3):
        for expert in range(plan.experts):
            at = kind * plan.wide + expert * width
            pairs.append((raw_refs[kind].at[expert], packed_ref.at[:, at : at + width]))
    for expert in range(plan.experts):
        block = factor_in_ref.at[
            expert * rank : (expert + 1) * rank, expert * width : (expert + 1) * width
        ]
        pairs.append((factor_ref.at[expert], block))
    copies = [
        pltpu.make_async_copy(source, target, sems.at[at])
        for at, (source, target) in enumerate(pairs)
    ]
    for copy in copies:
        copy.start()
    for expert in range(plan.experts):
        for other in range(plan.experts):
            if other != expert:
                factor_in_ref[
                    expert * rank : (expert + 1) * rank, other * width : (other + 1) * width
                ] = jnp.zeros((rank, width), bf16)
    copies[0].wait()
    copies[1].wait()
    rows, lanes = grads_ref.shape[0], grads_ref.shape[1] - plan.model_width
    expert_at = lax.broadcasted_iota(jnp.int32, (lanes, rows), 0)
    ids, route = ids_held[...], route_held[...].astype(f32)
    dense = jnp.zeros((lanes, rows), f32)
    for k in range(ids.shape[0]):
        dense = jnp.where(ids[k : k + 1, :] == expert_at, route[k : k + 1, :], dense)
    dense = dense.T.astype(bf16)
    grads_ref[:, plan.model_width :] = dense
    tokens_held_ref[:, plan.model_width :] = dense
    for copy in copies[2:]:
        copy.wait()


def add_kernel(blocks, skip, *refs):
    rows_ref, refs = refs[0], list(refs[1:])
    skipped_ref = refs.pop(len(blocks)) if skip else None
    for at, (first_row, span, taken, way) in enumerate(blocks):
        out = refs[len(blocks) + at]
        rows = rows_ref[first_row : first_row + out.shape[0], span]
        total = rows + refs[at][:, taken].astype(f32)
        if skip:
            here = skip[0]() == (way == "ahead")
            total = total + jnp.where(here, skipped_ref[:, skip[1]].astype(f32), 0.0)
        out[...] = total.astype(bf16)


def add_sums(rows, row_count, blocks, arrived, skip):
    operands = [rows, *arrived]
    return pl.pallas_call(
        functools.partial(add_kernel, blocks, skip),
        out_shape=tuple(
            jax.ShapeDtypeStruct((row_count, len(range(*span.indices(rows.shape[1])))), bf16)
            for _, span, _, _ in blocks
        ),
        in_specs=[pl.BlockSpec(memory_space=pltpu.VMEM)] * len(operands),
        out_specs=(pl.BlockSpec(memory_space=pltpu.VMEM),) * len(blocks),
        compiler_params=pltpu.CompilerParams(vmem_limit_bytes=16 * 1024 * 1024),
    )(*operands)


def half_rows_kernel(half, first_ref, second_ref, top_ref, bottom_ref):
    top_ref[...] = first_ref[:half]
    bottom_ref[...] = second_ref[half:]


def halves(first, second, half):
    out = ((half, first.shape[1]), first.dtype)
    return simple_call(functools.partial(half_rows_kernel, half), [first, second], [out, out])


def halves_kernel(plan, total_in_ref, total_out_ref, keep_ref, send_ref):
    first = lax.axis_index("dp") == 0
    middle, narrow = plan.model_width // 2, plan.hidden_width // 2
    low, high = total_out_ref[:, :middle], total_out_ref[:, middle:]
    keep_ref[:, :middle] = jnp.where(first, low, high)
    send_ref[:, :middle] = jnp.where(first, high, low)
    for expert in range(plan.experts):
        rows = slice(expert * plan.rank, (expert + 1) * plan.rank)
        block = total_in_ref[rows, expert * plan.hidden_width : (expert + 1) * plan.hidden_width]
        low, high = block[:, :narrow], block[:, narrow:]
        keep_ref[rows, middle:] = jnp.where(first, low, high)
        send_ref[rows, middle:] = jnp.where(first, high, low)


def joined_kernel(plan, keep_ref, other_ref, in_ref, out_ref):
    middle = plan.model_width // 2
    for expert in range(plan.experts):
        rows = slice(expert * plan.rank, (expert + 1) * plan.rank)
        out_ref[expert] = keep_ref[rows, :middle] + other_ref[rows, :middle]
        in_ref[expert] = keep_ref[rows, middle:] + other_ref[rows, middle:]


def last_kernel(first_row, spans, *refs):
    rows_ref, out_ref = refs[0], refs[-1]
    for at, span in enumerate(spans):
        total = rows_ref[first_row : first_row + out_ref.shape[0], span]
        for incoming in refs[1 + 2 * at : 3 + 2 * at]:
            total = total + incoming[...].astype(f32)
        out_ref[:, span] = total.astype(bf16)


def simple_call(kernel, operands, outs, scratch=(), flops=0):
    return pl.pallas_call(
        kernel,
        scratch_shapes=list(scratch),
        cost_estimate=pl.CostEstimate(
            flops=flops,
            bytes_accessed=sum(op.size * op.dtype.itemsize for op in operands),
            transcendentals=0,
        ),
        out_shape=tuple(jax.ShapeDtypeStruct(shape, dtype) for shape, dtype in outs),
        in_specs=[pl.BlockSpec(memory_space=pltpu.VMEM)] * len(operands),
        out_specs=(pl.BlockSpec(memory_space=pltpu.VMEM),) * len(outs),
        compiler_params=pltpu.CompilerParams(vmem_limit_bytes=16 * 1024 * 1024),
    )(*operands)


def expert_call(plan, pieces, operands, totals):
    rows = sum(piece[0].shape[0] for piece in pieces)
    return simple_call(
        functools.partial(whole_kernel, plan, len(pieces)),
        [p[0] for p in pieces] + [p[1] for p in pieces] + [*operands, *totals],
        [((rows, plan.model_width), f32)] + [(total.shape, f32) for total in totals],
        flops=10 * rows * plan.model_width * plan.wide,
    )


def per_device(
    snake,
    tokens,
    out_grad,
    expert_ids,
    route_weight,
    gate_weight,
    up_weight,
    down_weight,
    adapter_in,
    adapter_out,
):
    peer_count = lax.axis_size("expert")
    dp_count = lax.axis_size("dp")
    token_count, model_width = tokens.shape
    local_count, depth, hidden_width = gate_weight.shape
    rank = adapter_in.shape[1]
    expert_total = local_count * peer_count
    order = ring_order(peer_count, snake)
    forward = [(order[i], order[(i + 1) % peer_count]) for i in range(peer_count)]
    backward = [(b, a) for a, b in forward]
    swap = [(0, 1), (1, 0)]
    parts = 2 if dp_count == 2 else 1
    plan = Plan(parts, depth, model_width, hidden_width, rank, local_count)
    wide, ranks = plan.wide, plan.ranks

    lanes = -(-expert_total // lane_count) * lane_count
    mine, grads, tokens_held, factor_in = pl.pallas_call(
        functools.partial(prepare_kernel, plan),
        out_shape=(
            jax.ShapeDtypeStruct((depth, 3 * wide), bf16),
            jax.ShapeDtypeStruct((token_count, model_width + lanes), bf16),
            jax.ShapeDtypeStruct((token_count, model_width + lanes), bf16),
            jax.ShapeDtypeStruct((ranks, wide), bf16),
        ),
        in_specs=[pl.BlockSpec(memory_space=pltpu.HBM)] * 8,
        out_specs=(pl.BlockSpec(memory_space=pltpu.VMEM),) * 4,
        scratch_shapes=[
            pltpu.VMEM(expert_ids.shape[::-1], jnp.int32),
            pltpu.VMEM(route_weight.shape[::-1], bf16),
            pltpu.SemaphoreType.DMA((4 + 4 * local_count,)),
        ],
        compiler_params=pltpu.CompilerParams(vmem_limit_bytes=16 * 1024 * 1024),
    )(
        *(
            pltpu.with_memory_space_constraint(x, pltpu.HBM)
            for x in (
                gate_weight,
                up_weight,
                down_weight,
                out_grad,
                expert_ids.T,
                route_weight.T,
                adapter_in,
                tokens,
            )
        )
    )
    if parts == 2:
        weights = [mine, lax.ppermute(mine, "dp", swap)]
    else:
        weights = [lax.all_gather(mine, "dp", axis=0, tiled=True)]
    weights = [pltpu.with_memory_space_constraint(w, pltpu.VMEM) for w in weights]
    factor_out = adapter_out.reshape(ranks, model_width)

    full = (peer_count - 1) // 2
    split = peer_count % 2 == 0
    totals = (jnp.zeros((ranks, wide), f32), jnp.zeros((ranks, model_width), f32))
    behind, ahead = [(tokens_held, grads)], [(tokens_held, grads)]
    rows_at = [None]

    middle = model_width // 2
    columns = {"left": slice(0, middle), "right": slice(middle, model_width)}
    everything = slice(0, model_width)
    ways = {"back": (0, backward), "ahead": (token_count, forward)}
    moving = {}

    def send(value, way):
        return lax.ppermute(value, "expert", ways[way][1])

    flops = 2 * token_count * model_width * wide

    def forward_part(pieces, count):
        rows = count * token_count
        return simple_call(
            functools.partial(forward_kernel, plan, len(pieces)),
            [piece[0] for piece in pieces] + [factor_in, *weights],
            [((rows, wide), f32)] * 2 + [((rows, wide), bf16), ((rows, ranks), f32)],
            flops=2 * count * flops,
        )

    def finished(count):
        rows = count * token_count
        outs = [((rows, ranks), bf16)] * 2 + [((token_count, model_width), bf16)] * count
        return outs, [pltpu.VMEM((rows, model_width), f32)]

    def after(value, *arrays):
        held = []
        for x in arrays:
            x, value = lax.optimization_barrier((x, value))
            held.append(x)
        return value, held

    for d in range(full):
        if d > 1:
            totals, (grads_b, grads_a) = after(totals, behind[d][1], ahead[d][1])
            behind[d], ahead[d] = (behind[d][0], grads_b), (ahead[d][0], grads_a)
        behind.append(tuple(lax.ppermute(x, "expert", forward) for x in behind[d]))
        ahead.append(tuple(lax.ppermute(x, "expert", backward) for x in ahead[d]))
        if d > 0:
            pieces = [behind[d], ahead[d]] + ([behind[0]] if d == 1 else [])
            rows_d, *totals = expert_call(
                plan, pieces, [factor_in, factor_out, *weights], totals
            )
            rows_at.append(rows_d)
    pieces = [behind[full], ahead[full]]
    activation, slope, hidden, low_rank = forward_part(pieces, 2)
    if split:
        half = token_count // 2
        totals, (tokens_b, tokens_a) = after(totals, behind[full][0], ahead[full][0])
        _, (grads_b, grads_a) = after(low_rank, behind[full][1], ahead[full][1])
        tokens_b, tokens_a = halves(tokens_b, tokens_a, half)
        grads_b, grads_a = halves(grads_b, grads_a, half)
        far = [
            tuple(lax.ppermute(x, "expert", forward) for x in (tokens_b, grads_b)),
            tuple(lax.ppermute(x, "expert", backward) for x in (tokens_a, grads_a)),
        ]
    outs, scratch = finished(2)
    low_scaled, back_scaled, *values = simple_call(
        functools.partial(backward_kernel, plan, 2),
        [piece[1] for piece in pieces]
        + [activation, slope, low_rank, factor_in, factor_out, *weights],
        outs,
        scratch,
        6 * flops,
    )
    for way, value in zip(ways, values):
        for side in columns:
            moving[side, way] = send(value, way) if side == "left" else moving["left", way]
    late = [(hidden, low_scaled, back_scaled)]
    late_grads = [piece[1] for piece in pieces]
    skipped = []
    if split:
        outs, scratch = finished(1)
        hidden, low_scaled, back_scaled, value = simple_call(
            functools.partial(rows_kernel, plan, 2),
            [piece[0] for piece in far]
            + [piece[1] for piece in far]
            + [factor_in, factor_out, *weights],
            [((token_count, wide), bf16), *outs],
            scratch,
            5 * flops,
        )
        late.append((hidden, low_scaled, back_scaled))
        late_grads += [piece[1] for piece in far]
        pairs = [
            (order[i], order[(i + (full if i % 2 == 0 else -full)) % peer_count])
            for i in range(peer_count)
        ]
        skipped.append(lax.ppermute(value, "expert", pairs))
    totals = simple_call(
        functools.partial(adapters_kernel, plan, len(late_grads), len(late)),
        late_grads + [x for kind in zip(*late) for x in kind] + [*totals],
        [(total.shape, f32) for total in totals],
        flops=flops // 4,
    )

    def goes_ahead():
        me = lax.axis_index("expert")
        place = jnp.where(me % 2 == 0, me // 2, peer_count - 1 - me // 2) if snake else me
        return (place + full) % 2 == 0

    for d in range(full - 1, 0, -1):
        for side, span in columns.items():
            blocks, arrived = [], []
            for way, (first_row, _) in ways.items():
                blocks.append((first_row, span, span if d == full - 1 else slice(0, middle), way))
                arrived.append(moving[side, way])
            skip = (goes_ahead, span) if d == 1 and split else None
            values = add_sums(
                rows_at[d], token_count, blocks, arrived + (skipped if skip else []), skip
            )
            for way, value in zip(ways, values):
                moving[side, way] = send(value, way)
    grad_tokens = pl.pallas_call(
        functools.partial(last_kernel, 2 * token_count, list(columns.values())),
        out_shape=jax.ShapeDtypeStruct((token_count, model_width), bf16),
        in_specs=[pl.BlockSpec(memory_space=pltpu.VMEM)] * 5,
        out_specs=pl.BlockSpec(memory_space=pltpu.VMEM),
        compiler_params=pltpu.CompilerParams(vmem_limit_bytes=16 * 1024 * 1024),
    )(rows_at[1], *(moving[side, way] for side in columns for way in ways))

    narrow = hidden_width // dp_count
    if dp_count == 2:
        half = ((ranks, middle + narrow), f32)
        keep, other = simple_call(functools.partial(halves_kernel, plan), totals, [half, half])
        grad_in_all, grad_out_all = simple_call(
            functools.partial(joined_kernel, plan),
            [keep, lax.ppermute(other, "dp", swap)],
            [((local_count, rank, narrow), f32), ((local_count, rank, middle), f32)],
        )
        return (grad_tokens, grad_in_all, grad_out_all)
    grad_in = jnp.stack(
        [
            totals[0][j * rank : (j + 1) * rank, j * hidden_width : (j + 1) * hidden_width]
            for j in range(local_count)
        ]
    )
    both = jnp.concatenate(
        [
            grad_in.reshape(ranks, dp_count, narrow),
            totals[1].reshape(ranks, dp_count, model_width // dp_count),
        ],
        axis=2,
    ).transpose(1, 0, 2)
    summed = lax.psum_scatter(both, "dp", scatter_dimension=0, tiled=False)
    grad_in_all = summed[:, :narrow].reshape(local_count, rank, narrow)
    grad_out_all = summed[:, narrow:].reshape(local_count, rank, model_width // dp_count)
    return (grad_tokens, grad_in_all, grad_out_all)


def solution(mesh):
    snake = mesh.shape["dp"] == 2
    return jax.shard_map(
        functools.partial(per_device, snake),
        mesh=mesh,
        in_specs=(
            P(("group", "expert", "dp"), None),
            P(("group", "expert", "dp"), None),
            P(("group", "expert", "dp"), None),
            P(("group", "expert", "dp"), None),
            P("expert", "dp", None),
            P("expert", "dp", None),
            P("expert", "dp", None),
            P("expert", None, None),
            P("expert", None, None),
        ),
        out_specs=(
            P(("group", "expert", "dp"), None),
            P(("group", "expert"), None, "dp"),
            P(("group", "expert"), None, "dp"),
        ),
        check_vma=False,
    )
```

```python
import functools

import jax
import jax.numpy as jnp
from jax import lax
from jax.experimental import pallas as pl
from jax.experimental.pallas import tpu as pltpu
from jax.sharding import PartitionSpec as P

adapter_scale = 2.0
f32 = jnp.float32
bf16 = jnp.bfloat16
lane_count = 128


def ring_order(count, snake):
    if snake and count % 2 == 0:
        return list(range(0, count, 2)) + list(range(count - 1, 0, -2))
    return list(range(count))


def matmul(a, b):
    return jnp.dot(a, b, preferred_element_type=f32)


def matmul_bt(a, b):
    return lax.dot_general(a, b, (((1,), (1,)), ((), ())), preferred_element_type=f32)


def matmul_at(a, b):
    return lax.dot_general(a, b, (((0,), (0,)), ((), ())), preferred_element_type=f32)


def stacked(piece_refs, span):
    return jnp.concatenate([ref[:, span] for ref in piece_refs], axis=0)


class Plan:
    def __init__(self, parts, depth, model_width, hidden_width, rank, experts):
        self.parts = parts
        self.depth = depth
        self.model_width = model_width
        self.hidden_width = hidden_width
        self.rank = rank
        self.experts = experts
        self.wide = experts * hidden_width
        self.ranks = experts * rank

    def spans(self):
        if self.parts == 1:
            return [slice(0, self.model_width)]
        core = lax.axis_index("dp")
        return [
            pl.ds(pl.multiple_of(at * self.depth, self.depth), self.depth) for at in (core, 1 - core)
        ]

    def forward(self, token_refs, factor_in_ref, weight_refs):
        gate_pre, up_pre = 0.0, 0.0
        for span, weight in zip(self.spans(), weight_refs):
            tokens_in = stacked(token_refs, span)
            gate_pre += matmul(tokens_in, weight[:, : self.wide])
            up_pre += matmul(tokens_in, weight[:, self.wide : 2 * self.wide])
        logistic = 1.0 / (1.0 + jnp.exp(-gate_pre))
        activation = gate_pre * logistic
        derivative = logistic * (1.0 + gate_pre * (1.0 - logistic))
        hidden = (activation * up_pre).astype(bf16)
        low_rank = matmul_bt(hidden, factor_in_ref[...])
        return activation, up_pre * derivative, hidden, low_rank

    def scales(self, token_refs):
        columns = stacked(token_refs, slice(self.model_width, None)).astype(f32)
        lane = lax.broadcasted_iota(jnp.int32, columns.shape, 1)
        first = lax.axis_index("expert") * self.experts
        return [
            jnp.sum(jnp.where(lane == first + j, columns, 0.0), axis=1, keepdims=True)
            for j in range(self.experts)
        ]

    def spread(self, scales, width):
        rows = scales[0].shape[0]
        at = lax.broadcasted_iota(jnp.int32, (rows, self.experts * width), 1)
        out = jnp.broadcast_to(scales[0], at.shape)
        for j in range(1, self.experts):
            out = jnp.where(at >= j * width, scales[j], out)
        return out

    def backward(
        self, token_refs, grad_refs, activation, slope, factor_in_ref, factor_out_ref, weight_refs, rows_ref
    ):
        scales = self.scales(token_refs)
        adapter_back, grad_down = 0.0, 0.0
        spans = self.spans()
        for span, weight in zip(spans, weight_refs):
            grad_in = stacked(grad_refs, span)
            adapter_back += matmul_bt(grad_in, factor_out_ref[:, span])
            grad_down += matmul(grad_in, weight[:, 2 * self.wide :])
        adapter_back = adapter_back.astype(bf16)
        grad_hidden = self.spread(scales, self.hidden_width) * (
            grad_down + adapter_scale * matmul(adapter_back, factor_in_ref[...])
        )
        grad_gate = (grad_hidden * slope).astype(bf16)
        grad_up = (grad_hidden * activation).astype(bf16)
        for span, weight in zip(spans, weight_refs):
            rows_ref[:, span] = matmul_bt(grad_gate, weight[:, : self.wide]) + matmul_bt(
                grad_up, weight[:, self.wide : 2 * self.wide]
            )
        rank_scale = self.spread(scales, self.rank)
        return rank_scale, (rank_scale * adapter_back.astype(f32)).astype(bf16)

    def adapters(self, grad_refs, hidden, low_scaled, back_scaled, total_refs, out_refs):
        grad_all = stacked(grad_refs, slice(0, self.model_width))
        for total, out, value in zip(
            total_refs, out_refs, (matmul_at(back_scaled, hidden), matmul_at(low_scaled, grad_all))
        ):
            out[...] = total[...] + adapter_scale * value


def whole_kernel(plan, pieces, blocks, keep_rows, *refs):
    token_refs, grad_refs, refs = refs[:pieces], refs[pieces : 2 * pieces], refs[2 * pieces :]
    factor_in_ref, factor_out_ref, refs = refs[0], refs[1], refs[2:]
    weight_refs, refs = refs[: plan.parts], refs[plan.parts :]
    total_refs, refs = refs[:2], refs[2:]
    if keep_rows:
        rows_ref, refs = refs[0], refs[1:]
    else:
        *refs, rows_ref = refs
    out_refs, send_refs = refs[:2], refs[2:]
    activation, slope, hidden, low_rank = plan.forward(token_refs, factor_in_ref, weight_refs)
    rank_scale, back_scaled = plan.backward(
        token_refs, grad_refs, activation, slope, factor_in_ref, factor_out_ref, weight_refs, rows_ref
    )
    for (first_row, span), send_ref in zip(blocks, send_refs):
        send_ref[...] = rows_ref[first_row : first_row + send_ref.shape[0], span].astype(bf16)
    low_scaled = (rank_scale * low_rank).astype(bf16)
    plan.adapters(grad_refs, hidden, low_scaled, back_scaled, total_refs, out_refs)


def prepare_kernel(plan, *refs):
    raw_refs, refs = refs[:3], refs[3:]
    out_grad_ref, ids_ref, route_ref, factor_ref = refs[:4]
    tokens_ref, refs = refs[4], refs[5:]
    packed_ref, grads_ref, tokens_held_ref, factor_in_ref, ids_held, route_held, sems = refs
    width, rank = plan.hidden_width, plan.rank
    pairs = [(ids_ref, ids_held), (route_ref, route_held)]
    pairs.append((out_grad_ref, grads_ref))
    pairs.append((tokens_ref, tokens_held_ref.at[:, : plan.model_width]))
    for kind in range(3):
        for expert in range(plan.experts):
            at = kind * plan.wide + expert * width
            pairs.append((raw_refs[kind].at[expert], packed_ref.at[:, at : at + width]))
    for expert in range(plan.experts):
        block = factor_in_ref.at[
            expert * rank : (expert + 1) * rank, expert * width : (expert + 1) * width
        ]
        pairs.append((factor_ref.at[expert], block))
    copies = [
        pltpu.make_async_copy(source, target, sems.at[at])
        for at, (source, target) in enumerate(pairs)
    ]
    for copy in copies:
        copy.start()
    for expert in range(plan.experts):
        for other in range(plan.experts):
            if other != expert:
                factor_in_ref[
                    expert * rank : (expert + 1) * rank, other * width : (other + 1) * width
                ] = jnp.zeros((rank, width), bf16)
    copies[0].wait()
    copies[1].wait()
    rows, lanes = grads_ref.shape[0], tokens_held_ref.shape[1] - plan.model_width
    expert_at = lax.broadcasted_iota(jnp.int32, (lanes, rows), 0)
    ids, route = ids_held[...], route_held[...].astype(f32)
    dense = jnp.zeros((lanes, rows), f32)
    for k in range(ids.shape[0]):
        dense = jnp.where(ids[k : k + 1, :] == expert_at, route[k : k + 1, :], dense)
    dense = dense.T.astype(bf16)
    tokens_held_ref[:, plan.model_width :] = dense
    for copy in copies[2:]:
        copy.wait()


def add_kernel(blocks, skip, *refs):
    rows_ref, refs = refs[0], list(refs[1:])
    skipped_ref = refs.pop(len(blocks)) if skip else None
    for at, (first_row, span, taken, way) in enumerate(blocks):
        out = refs[len(blocks) + at]
        rows = rows_ref[first_row : first_row + out.shape[0], span]
        total = rows + refs[at][:, taken].astype(f32)
        if skip:
            here = skip[0]() == (way == "ahead")
            total = total + jnp.where(here, skipped_ref[:, skip[1]].astype(f32), 0.0)
        out[...] = total.astype(bf16)


def add_sums(rows, row_count, blocks, arrived, skip):
    operands = [rows, *arrived]
    return pl.pallas_call(
        functools.partial(add_kernel, blocks, skip),
        out_shape=tuple(
            jax.ShapeDtypeStruct((row_count, len(range(*span.indices(rows.shape[1])))), bf16)
            for _, span, _, _ in blocks
        ),
        in_specs=[pl.BlockSpec(memory_space=pltpu.VMEM)] * len(operands),
        out_specs=(pl.BlockSpec(memory_space=pltpu.VMEM),) * len(blocks),
        compiler_params=pltpu.CompilerParams(vmem_limit_bytes=16 * 1024 * 1024),
    )(*operands)


def half_rows_kernel(half, first_ref, second_ref, top_ref, bottom_ref):
    top_ref[...] = first_ref[:half]
    bottom_ref[...] = second_ref[half:]


def halves(first, second, half):
    out = ((half, first.shape[1]), first.dtype)
    return simple_call(functools.partial(half_rows_kernel, half), [first, second], [out, out])


def halves_kernel(plan, total_in_ref, total_out_ref, keep_ref, send_ref):
    first = lax.axis_index("dp") == 0
    middle, narrow = plan.model_width // 2, plan.hidden_width // 2
    low, high = total_out_ref[:, :middle], total_out_ref[:, middle:]
    keep_ref[:, :middle] = jnp.where(first, low, high)
    send_ref[:, :middle] = jnp.where(first, high, low)
    for expert in range(plan.experts):
        rows = slice(expert * plan.rank, (expert + 1) * plan.rank)
        block = total_in_ref[rows, expert * plan.hidden_width : (expert + 1) * plan.hidden_width]
        low, high = block[:, :narrow], block[:, narrow:]
        keep_ref[rows, middle:] = jnp.where(first, low, high)
        send_ref[rows, middle:] = jnp.where(first, high, low)


def joined_kernel(plan, keep_ref, other_ref, in_ref, out_ref):
    middle = plan.model_width // 2
    for expert in range(plan.experts):
        rows = slice(expert * plan.rank, (expert + 1) * plan.rank)
        out_ref[expert] = keep_ref[rows, :middle] + other_ref[rows, :middle]
        in_ref[expert] = keep_ref[rows, middle:] + other_ref[rows, middle:]


def last_kernel(first_row, spans, *refs):
    rows_ref, out_ref = refs[0], refs[-1]
    for at, span in enumerate(spans):
        total = rows_ref[first_row : first_row + out_ref.shape[0], span]
        for incoming in refs[1 + 2 * at : 3 + 2 * at]:
            total = total + incoming[...].astype(f32)
        out_ref[:, span] = total.astype(bf16)


def simple_call(kernel, operands, outs):
    return pl.pallas_call(
        kernel,
        out_shape=tuple(jax.ShapeDtypeStruct(shape, dtype) for shape, dtype in outs),
        in_specs=[pl.BlockSpec(memory_space=pltpu.VMEM)] * len(operands),
        out_specs=(pl.BlockSpec(memory_space=pltpu.VMEM),) * len(outs),
        compiler_params=pltpu.CompilerParams(vmem_limit_bytes=16 * 1024 * 1024),
    )(*operands)


def expert_call(plan, pieces, blocks, block_rows, operands, totals, keep_rows):
    rows = sum(piece[0].shape[0] for piece in pieces)
    operands = [p[0] for p in pieces] + [p[1] for p in pieces] + [*operands, *totals]
    shape = (rows, plan.model_width)
    outs = [(shape, f32)] * keep_rows + [(total.shape, f32) for total in totals]
    widths = [len(range(*span.indices(plan.model_width))) for _, span in blocks]
    outs += [((block_rows, width), bf16) for width in widths]
    return pl.pallas_call(
        functools.partial(whole_kernel, plan, len(pieces), blocks, keep_rows),
        scratch_shapes=[] if keep_rows else [pltpu.VMEM(shape, f32)],
        out_shape=tuple(jax.ShapeDtypeStruct(shape, dtype) for shape, dtype in outs),
        in_specs=[pl.BlockSpec(memory_space=pltpu.VMEM)] * len(operands),
        out_specs=(pl.BlockSpec(memory_space=pltpu.VMEM),) * len(outs),
        compiler_params=pltpu.CompilerParams(vmem_limit_bytes=16 * 1024 * 1024),
        cost_estimate=pl.CostEstimate(
            flops=10 * rows * plan.model_width * plan.wide,
            bytes_accessed=sum(op.size * op.dtype.itemsize for op in operands),
            transcendentals=0,
        ),
    )(*operands)


def per_device(
    snake,
    tokens,
    out_grad,
    expert_ids,
    route_weight,
    gate_weight,
    up_weight,
    down_weight,
    adapter_in,
    adapter_out,
):
    peer_count = lax.axis_size("expert")
    dp_count = lax.axis_size("dp")
    token_count, model_width = tokens.shape
    local_count, depth, hidden_width = gate_weight.shape
    rank = adapter_in.shape[1]
    expert_total = local_count * peer_count
    order = ring_order(peer_count, snake)
    forward = [(order[i], order[(i + 1) % peer_count]) for i in range(peer_count)]
    backward = [(b, a) for a, b in forward]
    swap = [(0, 1), (1, 0)]
    parts = 2 if dp_count == 2 else 1
    plan = Plan(parts, depth, model_width, hidden_width, rank, local_count)
    wide, ranks = plan.wide, plan.ranks

    lanes = -(-expert_total // lane_count) * lane_count
    mine, grads, tokens_held, factor_in = pl.pallas_call(
        functools.partial(prepare_kernel, plan),
        out_shape=(
            jax.ShapeDtypeStruct((depth, 3 * wide), bf16),
            jax.ShapeDtypeStruct((token_count, model_width), bf16),
            jax.ShapeDtypeStruct((token_count, model_width + lanes), bf16),
            jax.ShapeDtypeStruct((ranks, wide), bf16),
        ),
        in_specs=[pl.BlockSpec(memory_space=pltpu.HBM)] * 8,
        out_specs=(pl.BlockSpec(memory_space=pltpu.VMEM),) * 4,
        scratch_shapes=[
            pltpu.VMEM(expert_ids.shape[::-1], jnp.int32),
            pltpu.VMEM(route_weight.shape[::-1], bf16),
            pltpu.SemaphoreType.DMA((4 + 4 * local_count,)),
        ],
        compiler_params=pltpu.CompilerParams(vmem_limit_bytes=16 * 1024 * 1024),
    )(
        *(
            pltpu.with_memory_space_constraint(x, pltpu.HBM)
            for x in (
                gate_weight,
                up_weight,
                down_weight,
                out_grad,
                expert_ids.T,
                route_weight.T,
                adapter_in,
                tokens,
            )
        )
    )
    if parts == 2:
        weights = [mine, lax.ppermute(mine, "dp", swap)]
    else:
        weights = [lax.all_gather(mine, "dp", axis=0, tiled=True)]
    weights = [pltpu.with_memory_space_constraint(w, pltpu.VMEM) for w in weights]
    factor_out = adapter_out.reshape(ranks, model_width)

    full = (peer_count - 1) // 2
    split = peer_count % 2 == 0
    totals = (jnp.zeros((ranks, wide), f32), jnp.zeros((ranks, model_width), f32))
    behind, ahead = [(tokens_held, grads)], [(tokens_held, grads)]
    rows_at = [None]

    middle = model_width // 2
    columns = {"left": slice(0, middle), "right": slice(middle, model_width)}
    everything = slice(0, model_width)
    ways = {"back": (0, backward), "ahead": (token_count, forward)}
    moving = {}

    def send(value, way):
        return lax.ppermute(value, "expert", ways[way][1])

    def run(pieces, blocks, totals, keep_rows=True):
        operands = [factor_in, factor_out, *weights]
        return expert_call(plan, pieces, blocks, token_count, operands, totals, keep_rows)

    def after(value, *arrays):
        held = []
        for x in arrays:
            x, value = lax.optimization_barrier((x, value))
            held.append(x)
        return value, held

    for d in range(full):
        if d > 1:
            totals, (tokens_b, tokens_a) = after(totals, behind[d][0], ahead[d][0])
            grads_b, grads_a = behind[d][1], ahead[d][1]
            behind[d], ahead[d] = (tokens_b, grads_b), (tokens_a, grads_a)
        behind.append(tuple(lax.ppermute(x, "expert", forward) for x in behind[d]))
        ahead.append(tuple(lax.ppermute(x, "expert", backward) for x in ahead[d]))
        if d > 0:
            pieces = [behind[d], ahead[d]] + ([behind[0]] if d == 1 else [])
            rows_d, *totals = run(pieces, [], totals)
            rows_at.append(rows_d)
    if split:
        half = token_count // 2
        totals, (tokens_b, tokens_a) = after(totals, behind[full][0], ahead[full][0])
        tokens_b, tokens_a = halves(tokens_b, tokens_a, half)
        grads_b, grads_a = halves(behind[full][1], ahead[full][1], half)
        far = [
            tuple(lax.ppermute(x, "expert", forward) for x in (tokens_b, grads_b)),
            tuple(lax.ppermute(x, "expert", backward) for x in (tokens_a, grads_a)),
        ]
    pieces = [behind[full], ahead[full]]
    blocks = [(first_row, everything) for first_row, _ in ways.values()]
    outs = run(pieces, blocks, totals, keep_rows=False)
    totals = outs[:2]
    for way, value in zip(ways, outs[2:]):
        for side in columns:
            moving[side, way] = send(value, way) if side == "left" else moving["left", way]
    skipped = []
    if split:
        *totals, value = run(far, [(0, everything)], totals, keep_rows=False)
        pairs = [
            (order[i], order[(i + (full if i % 2 == 0 else -full)) % peer_count])
            for i in range(peer_count)
        ]
        skipped.append(lax.ppermute(value, "expert", pairs))

    def goes_ahead():
        me = lax.axis_index("expert")
        place = jnp.where(me % 2 == 0, me // 2, peer_count - 1 - me // 2) if snake else me
        return (place + full) % 2 == 0

    for d in range(full - 1, 0, -1):
        for side, span in columns.items():
            blocks, arrived = [], []
            for way, (first_row, _) in ways.items():
                blocks.append((first_row, span, span if d == full - 1 else slice(0, middle), way))
                arrived.append(moving[side, way])
            skip = (goes_ahead, span) if d == 1 and split else None
            values = add_sums(
                rows_at[d], token_count, blocks, arrived + (skipped if skip else []), skip
            )
            for way, value in zip(ways, values):
                moving[side, way] = send(value, way)
    grad_tokens = pl.pallas_call(
        functools.partial(last_kernel, 2 * token_count, list(columns.values())),
        out_shape=jax.ShapeDtypeStruct((token_count, model_width), bf16),
        in_specs=[pl.BlockSpec(memory_space=pltpu.VMEM)] * 5,
        out_specs=pl.BlockSpec(memory_space=pltpu.VMEM),
        compiler_params=pltpu.CompilerParams(vmem_limit_bytes=16 * 1024 * 1024),
    )(rows_at[1], *(moving[side, way] for side in columns for way in ways))

    narrow = hidden_width // dp_count
    if dp_count == 2:
        half = ((ranks, middle + narrow), f32)
        keep, other = simple_call(functools.partial(halves_kernel, plan), totals, [half, half])
        grad_in_all, grad_out_all = simple_call(
            functools.partial(joined_kernel, plan),
            [keep, lax.ppermute(other, "dp", swap)],
            [((local_count, rank, narrow), f32), ((local_count, rank, middle), f32)],
        )
        return (grad_tokens, grad_in_all, grad_out_all)
    grad_in = jnp.stack(
        [
            totals[0][j * rank : (j + 1) * rank, j * hidden_width : (j + 1) * hidden_width]
            for j in range(local_count)
        ]
    )
    both = jnp.concatenate(
        [
            grad_in.reshape(ranks, dp_count, narrow),
            totals[1].reshape(ranks, dp_count, model_width // dp_count),
        ],
        axis=2,
    ).transpose(1, 0, 2)
    summed = lax.psum_scatter(both, "dp", scatter_dimension=0, tiled=False)
    grad_in_all = summed[:, :narrow].reshape(local_count, rank, narrow)
    grad_out_all = summed[:, narrow:].reshape(local_count, rank, model_width // dp_count)
    return (grad_tokens, grad_in_all, grad_out_all)


def solution(mesh):
    snake = mesh.shape["dp"] == 2
    return jax.shard_map(
        functools.partial(per_device, snake),
        mesh=mesh,
        in_specs=(
            P(("group", "expert", "dp"), None),
            P(("group", "expert", "dp"), None),
            P(("group", "expert", "dp"), None),
            P(("group", "expert", "dp"), None),
            P("expert", "dp", None),
            P("expert", "dp", None),
            P("expert", "dp", None),
            P("expert", None, None),
            P("expert", None, None),
        ),
        out_specs=(
            P(("group", "expert", "dp"), None),
            P(("group", "expert"), None, "dp"),
            P(("group", "expert"), None, "dp"),
        ),
        check_vma=False,
    )
```

```python
import functools
import math

import jax
import jax.numpy as jnp
from jax import lax
from jax.experimental import pallas as pl
from jax.experimental.pallas import tpu as pltpu
from jax.sharding import PartitionSpec as P

adapter_scale = 2.0
f32 = jnp.float32
bf16 = jnp.bfloat16
lane_count = 128


def ring_order(count, snake):
    if snake and count % 2 == 0:
        return list(range(0, count, 2)) + list(range(count - 1, 0, -2))
    return list(range(count))


def matmul(a, b):
    return jnp.dot(a, b, preferred_element_type=f32)


def matmul_bt(a, b):
    return lax.dot_general(a, b, (((1,), (1,)), ((), ())), preferred_element_type=f32)


def matmul_at(a, b):
    return lax.dot_general(a, b, (((0,), (0,)), ((), ())), preferred_element_type=f32)


def stacked(piece_refs, span):
    return jnp.concatenate([ref[:, span] for ref in piece_refs], axis=0)


class Plan:
    def __init__(self, parts, depth, model_width, hidden_width, rank, experts):
        self.parts = parts
        self.depth = depth
        self.model_width = model_width
        self.hidden_width = hidden_width
        self.rank = rank
        self.experts = experts
        self.wide = experts * hidden_width
        self.ranks = experts * rank
        self.cuts = 4 if depth % 64 == 0 else 1

    def spans(self):
        if self.parts == 1:
            return [slice(0, self.model_width)]
        core = lax.axis_index("dp")
        return [
            pl.ds(pl.multiple_of(at * self.depth, self.depth), self.depth) for at in (core, 1 - core)
        ]

    def forward(self, token_refs, factor_in_ref, weight_refs):
        gate_pre, up_pre = 0.0, 0.0
        for span, weight in zip(self.spans(), weight_refs):
            tokens_in = stacked(token_refs, span)
            gate_pre += matmul(tokens_in, weight[:, : self.wide])
            up_pre += matmul(tokens_in, weight[:, self.wide : 2 * self.wide])
        logistic = 1.0 / (1.0 + jnp.exp(-gate_pre))
        activation = gate_pre * logistic
        derivative = logistic * (1.0 + gate_pre * (1.0 - logistic))
        hidden = (activation * up_pre).astype(bf16)
        low_rank = matmul_bt(hidden, factor_in_ref[...])
        return activation, up_pre * derivative, hidden, low_rank

    def scales(self, token_refs):
        columns = stacked(token_refs, slice(self.model_width, None)).astype(f32)
        lane = lax.broadcasted_iota(jnp.int32, columns.shape, 1)
        first = lax.axis_index("expert") * self.experts
        return [
            jnp.sum(jnp.where(lane == first + j, columns, 0.0), axis=1, keepdims=True)
            for j in range(self.experts)
        ]

    def spread(self, scales, width):
        rows = scales[0].shape[0]
        at = lax.broadcasted_iota(jnp.int32, (rows, self.experts * width), 1)
        out = jnp.broadcast_to(scales[0], at.shape)
        for j in range(1, self.experts):
            out = jnp.where(at >= j * width, scales[j], out)
        return out

    def backward(
        self, token_refs, grad_refs, activation, slope, factor_in_ref, factor_out_ref, weight_refs, turned_refs, rows_ref
    ):
        scales = self.scales(token_refs)
        adapter_back, grad_down = 0.0, 0.0
        spans = self.spans()
        for span, weight in zip(spans, weight_refs):
            grad_in = stacked(grad_refs, span)
            adapter_back += matmul_bt(grad_in, factor_out_ref[:, span])
            grad_down += matmul(grad_in, weight[:, 2 * self.wide :])
        adapter_back = adapter_back.astype(bf16)
        grad_hidden = self.spread(scales, self.hidden_width) * (
            grad_down + adapter_scale * matmul(adapter_back, factor_in_ref[...])
        )
        grad_gate = (grad_hidden * slope).astype(bf16)
        grad_up = (grad_hidden * activation).astype(bf16)
        for span, weight, turned in zip(spans, weight_refs, turned_refs or weight_refs):
            if turned_refs:
                rows_ref[:, span] = matmul(grad_gate, turned[: self.wide, :]) + matmul(
                    grad_up, turned[self.wide :, :]
                )
            else:
                rows_ref[:, span] = matmul_bt(grad_gate, weight[:, : self.wide]) + matmul_bt(
                    grad_up, weight[:, self.wide : 2 * self.wide]
                )
        rank_scale = self.spread(scales, self.rank)
        return rank_scale, (rank_scale * adapter_back.astype(f32)).astype(bf16)

    def adapters(self, grad_refs, hidden, low_scaled, back_scaled, total_refs, out_refs):
        grad_all = stacked(grad_refs, slice(0, self.model_width))
        for total, out, value in zip(
            total_refs, out_refs, (matmul_at(back_scaled, hidden), matmul_at(low_scaled, grad_all))
        ):
            out[...] = total[...] + adapter_scale * value


def whole_kernel(plan, pieces, blocks, keep_rows, is_turned, *refs):
    token_refs, grad_refs, refs = refs[:pieces], refs[pieces : 2 * pieces], refs[2 * pieces :]
    factor_in_ref, factor_out_ref, refs = refs[0], refs[1], refs[2:]
    weight_refs, refs = refs[: plan.parts], refs[plan.parts :]
    turned_refs = refs[: plan.parts] if is_turned else ()
    refs = refs[len(turned_refs) :]
    total_refs, refs = refs[:2], refs[2:]
    if keep_rows:
        rows_ref, refs = refs[0], refs[1:]
    else:
        *refs, rows_ref = refs
    out_refs, send_refs = refs[:2], refs[2:]
    activation, slope, hidden, low_rank = plan.forward(token_refs, factor_in_ref, weight_refs)
    rank_scale, back_scaled = plan.backward(
        token_refs, grad_refs, activation, slope, factor_in_ref, factor_out_ref, weight_refs, turned_refs, rows_ref
    )
    for (first_row, span), send_ref in zip(blocks, send_refs):
        send_ref[...] = rows_ref[first_row : first_row + send_ref.shape[0], span].astype(bf16)
    low_scaled = (rank_scale * low_rank).astype(bf16)
    plan.adapters(grad_refs, hidden, low_scaled, back_scaled, total_refs, out_refs)


def prepare_kernel(plan, *refs):
    raw_refs, refs = refs[:3], refs[3:]
    out_grad_ref, ids_ref, route_ref, factor_ref = refs[:4]
    tokens_ref, refs = refs[4], refs[5:]
    packed_ref, grads_ref, tokens_held_ref, factor_in_ref, ids_held, route_held, sems = refs
    width, rank, cuts = plan.hidden_width, plan.rank, plan.cuts
    pairs = [(ids_ref, ids_held), (route_ref, route_held)]
    pairs.append((out_grad_ref, grads_ref))
    pairs.append((tokens_ref, tokens_held_ref.at[:, : plan.model_width]))
    for kind in range(3):
        for expert in range(plan.experts):
            at = kind * plan.wide + expert * width
            for cut in range(cuts):
                rows = slice(cut * plan.depth // cuts, (cut + 1) * plan.depth // cuts)
                source = raw_refs[kind].at[expert, rows, :]
                pairs.append((source, packed_ref.at[rows, at : at + width]))
    for expert in range(plan.experts):
        block = factor_in_ref.at[
            expert * rank : (expert + 1) * rank, expert * width : (expert + 1) * width
        ]
        pairs.append((factor_ref.at[expert], block))
    copies = [
        pltpu.make_async_copy(source, target, sems.at[at])
        for at, (source, target) in enumerate(pairs)
    ]
    for copy in copies:
        copy.start()
    for expert in range(plan.experts):
        for other in range(plan.experts):
            if other != expert:
                factor_in_ref[
                    expert * rank : (expert + 1) * rank, other * width : (other + 1) * width
                ] = jnp.zeros((rank, width), bf16)
    copies[0].wait()
    copies[1].wait()
    rows, lanes = grads_ref.shape[0], tokens_held_ref.shape[1] - plan.model_width
    expert_at = lax.broadcasted_iota(jnp.int32, (lanes, rows), 0)
    ids, route = ids_held[...], route_held[...].astype(f32)
    dense = jnp.zeros((lanes, rows), f32)
    for k in range(ids.shape[0]):
        dense = jnp.where(ids[k : k + 1, :] == expert_at, route[k : k + 1, :], dense)
    dense = dense.T.astype(bf16)
    tokens_held_ref[:, plan.model_width :] = dense
    for copy in copies[2:]:
        copy.wait()


def add_kernel(blocks, skip, *refs):
    rows_ref, refs = refs[0], list(refs[1:])
    skipped_ref = refs.pop(len(blocks)) if skip else None
    for at, (first_row, span, taken, way) in enumerate(blocks):
        out = refs[len(blocks) + at]
        rows = rows_ref[first_row : first_row + out.shape[0], span]
        total = rows + refs[at][:, taken].astype(f32)
        if skip:
            here = skip[0]() == (way == "ahead")
            total = total + jnp.where(here, skipped_ref[:, skip[1]].astype(f32), 0.0)
        out[...] = total.astype(bf16)


def add_sums(rows, row_count, blocks, arrived, skip):
    operands = [rows, *arrived]
    return pl.pallas_call(
        functools.partial(add_kernel, blocks, skip),
        out_shape=tuple(
            jax.ShapeDtypeStruct((row_count, len(range(*span.indices(rows.shape[1])))), bf16)
            for _, span, _, _ in blocks
        ),
        in_specs=[pl.BlockSpec(memory_space=pltpu.VMEM)] * len(operands),
        out_specs=(pl.BlockSpec(memory_space=pltpu.VMEM),) * len(blocks),
        compiler_params=pltpu.CompilerParams(vmem_limit_bytes=16 * 1024 * 1024),
    )(*operands)


def turn_kernel(plan, *refs):
    for weight_ref, turned_ref in zip(refs, refs[plan.parts :]):
        step = math.gcd(2 * plan.wide, 256)
        for at in range(0, 2 * plan.wide, step):
            turned_ref[at : at + step, :] = weight_ref[:, at : at + step].T


def half_rows_kernel(half, first_ref, second_ref, top_ref, bottom_ref):
    top_ref[...] = first_ref[:half]
    bottom_ref[...] = second_ref[half:]


def halves(first, second, half):
    out = ((half, first.shape[1]), first.dtype)
    return simple_call(functools.partial(half_rows_kernel, half), [first, second], [out, out])


def halves_kernel(plan, total_in_ref, total_out_ref, keep_ref, send_ref):
    first = lax.axis_index("dp") == 0
    middle, narrow = plan.model_width // 2, plan.hidden_width // 2
    low, high = total_out_ref[:, :middle], total_out_ref[:, middle:]
    keep_ref[:, :middle] = jnp.where(first, low, high)
    send_ref[:, :middle] = jnp.where(first, high, low)
    for expert in range(plan.experts):
        rows = slice(expert * plan.rank, (expert + 1) * plan.rank)
        block = total_in_ref[rows, expert * plan.hidden_width : (expert + 1) * plan.hidden_width]
        low, high = block[:, :narrow], block[:, narrow:]
        keep_ref[rows, middle:] = jnp.where(first, low, high)
        send_ref[rows, middle:] = jnp.where(first, high, low)


def joined_kernel(plan, keep_ref, other_ref, in_ref, out_ref):
    middle = plan.model_width // 2
    for expert in range(plan.experts):
        rows = slice(expert * plan.rank, (expert + 1) * plan.rank)
        out_ref[expert] = keep_ref[rows, :middle] + other_ref[rows, :middle]
        in_ref[expert] = keep_ref[rows, middle:] + other_ref[rows, middle:]


def last_kernel(first_row, spans, *refs):
    rows_ref, out_ref = refs[0], refs[-1]
    for at, span in enumerate(spans):
        total = rows_ref[first_row : first_row + out_ref.shape[0], span]
        for incoming in refs[1 + 2 * at : 3 + 2 * at]:
            total = total + incoming[...].astype(f32)
        out_ref[:, span] = total.astype(bf16)


def simple_call(kernel, operands, outs):
    return pl.pallas_call(
        kernel,
        out_shape=tuple(jax.ShapeDtypeStruct(shape, dtype) for shape, dtype in outs),
        in_specs=[pl.BlockSpec(memory_space=pltpu.VMEM)] * len(operands),
        out_specs=(pl.BlockSpec(memory_space=pltpu.VMEM),) * len(outs),
        compiler_params=pltpu.CompilerParams(vmem_limit_bytes=16 * 1024 * 1024),
    )(*operands)


def expert_call(plan, pieces, blocks, block_rows, operands, totals, keep_rows, is_turned):
    rows = sum(piece[0].shape[0] for piece in pieces)
    operands = [p[0] for p in pieces] + [p[1] for p in pieces] + [*operands, *totals]
    shape = (rows, plan.model_width)
    outs = [(shape, f32)] * keep_rows + [(total.shape, f32) for total in totals]
    widths = [len(range(*span.indices(plan.model_width))) for _, span in blocks]
    outs += [((block_rows, width), bf16) for width in widths]
    return pl.pallas_call(
        functools.partial(whole_kernel, plan, len(pieces), blocks, keep_rows, is_turned),
        scratch_shapes=[] if keep_rows else [pltpu.VMEM(shape, f32)],
        out_shape=tuple(jax.ShapeDtypeStruct(shape, dtype) for shape, dtype in outs),
        in_specs=[pl.BlockSpec(memory_space=pltpu.VMEM)] * len(operands),
        out_specs=(pl.BlockSpec(memory_space=pltpu.VMEM),) * len(outs),
        compiler_params=pltpu.CompilerParams(vmem_limit_bytes=16 * 1024 * 1024),
        cost_estimate=pl.CostEstimate(
            flops=10 * rows * plan.model_width * plan.wide,
            bytes_accessed=sum(op.size * op.dtype.itemsize for op in operands),
            transcendentals=0,
        ),
    )(*operands)


def per_device(
    snake,
    tokens,
    out_grad,
    expert_ids,
    route_weight,
    gate_weight,
    up_weight,
    down_weight,
    adapter_in,
    adapter_out,
):
    peer_count = lax.axis_size("expert")
    dp_count = lax.axis_size("dp")
    token_count, model_width = tokens.shape
    local_count, depth, hidden_width = gate_weight.shape
    rank = adapter_in.shape[1]
    expert_total = local_count * peer_count
    order = ring_order(peer_count, snake)
    forward = [(order[i], order[(i + 1) % peer_count]) for i in range(peer_count)]
    backward = [(b, a) for a, b in forward]
    swap = [(0, 1), (1, 0)]
    parts = 2 if dp_count == 2 else 1
    plan = Plan(parts, depth, model_width, hidden_width, rank, local_count)
    wide, ranks = plan.wide, plan.ranks

    lanes = -(-expert_total // lane_count) * lane_count
    mine, grads, tokens_held, factor_in = pl.pallas_call(
        functools.partial(prepare_kernel, plan),
        out_shape=(
            jax.ShapeDtypeStruct((depth, 3 * wide), bf16),
            jax.ShapeDtypeStruct((token_count, model_width), bf16),
            jax.ShapeDtypeStruct((token_count, model_width + lanes), bf16),
            jax.ShapeDtypeStruct((ranks, wide), bf16),
        ),
        in_specs=[pl.BlockSpec(memory_space=pltpu.HBM)] * 8,
        out_specs=(pl.BlockSpec(memory_space=pltpu.VMEM),) * 4,
        scratch_shapes=[
            pltpu.VMEM(expert_ids.shape[::-1], jnp.int32),
            pltpu.VMEM(route_weight.shape[::-1], bf16),
            pltpu.SemaphoreType.DMA((4 + (3 * plan.cuts + 1) * local_count,)),
        ],
        compiler_params=pltpu.CompilerParams(vmem_limit_bytes=16 * 1024 * 1024),
    )(
        *(
            pltpu.with_memory_space_constraint(x, pltpu.HBM)
            for x in (
                gate_weight,
                up_weight,
                down_weight,
                out_grad,
                expert_ids.T,
                route_weight.T,
                adapter_in,
                tokens,
            )
        )
    )
    if parts == 2:
        weights = [mine, lax.ppermute(mine, "dp", swap)]
    else:
        weights = [lax.all_gather(mine, "dp", axis=0, tiled=True)]
    weights = [pltpu.with_memory_space_constraint(w, pltpu.VMEM) for w in weights]
    factor_out = adapter_out.reshape(ranks, model_width)

    full = (peer_count - 1) // 2
    split = peer_count % 2 == 0
    totals = (jnp.zeros((ranks, wide), f32), jnp.zeros((ranks, model_width), f32))
    behind, ahead = [(tokens_held, grads)], [(tokens_held, grads)]
    rows_at = [None]

    middle = model_width // 2
    columns = {"left": slice(0, middle), "right": slice(middle, model_width)}
    everything = slice(0, model_width)
    ways = {"back": (0, backward), "ahead": (token_count, forward)}
    moving = {}

    def send(value, way):
        return lax.ppermute(value, "expert", ways[way][1])

    def run(pieces, blocks, totals, keep_rows=True, turned=()):
        operands = [factor_in, factor_out, *weights, *turned]
        return expert_call(
            plan, pieces, blocks, token_count, operands, totals, keep_rows, bool(turned)
        )

    def after(value, *arrays):
        held = []
        for x in arrays:
            x, value = lax.optimization_barrier((x, value))
            held.append(x)
        return value, held

    for d in range(full):
        if d > 1:
            totals, (tokens_b, tokens_a) = after(totals, behind[d][0], ahead[d][0])
            grads_b, grads_a = behind[d][1], ahead[d][1]
            behind[d], ahead[d] = (tokens_b, grads_b), (tokens_a, grads_a)
        behind.append(tuple(lax.ppermute(x, "expert", forward) for x in behind[d]))
        ahead.append(tuple(lax.ppermute(x, "expert", backward) for x in ahead[d]))
        if d > 0:
            pieces = [behind[d], ahead[d]] + ([behind[0]] if d == 1 else [])
            rows_d, *totals = run(pieces, [], totals)
            rows_at.append(rows_d)
    turned = simple_call(
        functools.partial(turn_kernel, plan),
        weights,
        [((2 * wide, w.shape[0]), bf16) for w in weights],
    )
    if split:
        half = token_count // 2
        totals, (tokens_b, tokens_a) = after(totals, behind[full][0], ahead[full][0])
        (grads_b,) = after(turned[0], behind[full][1])[1]
        (grads_a,) = after(turned[0], ahead[full][1])[1]
        tokens_b, tokens_a = halves(tokens_b, tokens_a, half)
        grads_b, grads_a = halves(grads_b, grads_a, half)
        far = [
            tuple(lax.ppermute(x, "expert", forward) for x in (tokens_b, grads_b)),
            tuple(lax.ppermute(x, "expert", backward) for x in (tokens_a, grads_a)),
        ]
    pieces = [behind[full], ahead[full]]
    blocks = [(first_row, everything) for first_row, _ in ways.values()]
    outs = run(pieces, blocks, totals, keep_rows=False, turned=turned)
    totals = outs[:2]
    for way, value in zip(ways, outs[2:]):
        for side in columns:
            moving[side, way] = send(value, way) if side == "left" else moving["left", way]
    skipped = []
    if split:
        *totals, value = run(far, [(0, everything)], totals, keep_rows=False, turned=turned)
        pairs = [
            (order[i], order[(i + (full if i % 2 == 0 else -full)) % peer_count])
            for i in range(peer_count)
        ]
        skipped.append(lax.ppermute(value, "expert", pairs))

    def goes_ahead():
        me = lax.axis_index("expert")
        place = jnp.where(me % 2 == 0, me // 2, peer_count - 1 - me // 2) if snake else me
        return (place + full) % 2 == 0

    for d in range(full - 1, 0, -1):
        for side, span in columns.items():
            blocks, arrived = [], []
            for way, (first_row, _) in ways.items():
                blocks.append((first_row, span, span if d == full - 1 else slice(0, middle), way))
                arrived.append(moving[side, way])
            skip = (goes_ahead, span) if d == 1 and split else None
            values = add_sums(
                rows_at[d], token_count, blocks, arrived + (skipped if skip else []), skip
            )
            for way, value in zip(ways, values):
                moving[side, way] = send(value, way)
    grad_tokens = pl.pallas_call(
        functools.partial(last_kernel, 2 * token_count, list(columns.values())),
        out_shape=jax.ShapeDtypeStruct((token_count, model_width), bf16),
        in_specs=[pl.BlockSpec(memory_space=pltpu.VMEM)] * 5,
        out_specs=pl.BlockSpec(memory_space=pltpu.VMEM),
        compiler_params=pltpu.CompilerParams(vmem_limit_bytes=16 * 1024 * 1024),
    )(rows_at[1], *(moving[side, way] for side in columns for way in ways))

    narrow = hidden_width // dp_count
    if dp_count == 2:
        half = ((ranks, middle + narrow), f32)
        keep, other = simple_call(functools.partial(halves_kernel, plan), totals, [half, half])
        grad_in_all, grad_out_all = simple_call(
            functools.partial(joined_kernel, plan),
            [keep, lax.ppermute(other, "dp", swap)],
            [((local_count, rank, narrow), f32), ((local_count, rank, middle), f32)],
        )
        return (grad_tokens, grad_in_all, grad_out_all)
    grad_in = jnp.stack(
        [
            totals[0][j * rank : (j + 1) * rank, j * hidden_width : (j + 1) * hidden_width]
            for j in range(local_count)
        ]
    )
    both = jnp.concatenate(
        [
            grad_in.reshape(ranks, dp_count, narrow),
            totals[1].reshape(ranks, dp_count, model_width // dp_count),
        ],
        axis=2,
    ).transpose(1, 0, 2)
    summed = lax.psum_scatter(both, "dp", scatter_dimension=0, tiled=False)
    grad_in_all = summed[:, :narrow].reshape(local_count, rank, narrow)
    grad_out_all = summed[:, narrow:].reshape(local_count, rank, model_width // dp_count)
    return (grad_tokens, grad_in_all, grad_out_all)


def solution(mesh):
    snake = mesh.shape["dp"] == 2
    return jax.shard_map(
        functools.partial(per_device, snake),
        mesh=mesh,
        in_specs=(
            P(("group", "expert", "dp"), None),
            P(("group", "expert", "dp"), None),
            P(("group", "expert", "dp"), None),
            P(("group", "expert", "dp"), None),
            P("expert", "dp", None),
            P("expert", "dp", None),
            P("expert", "dp", None),
            P("expert", None, None),
            P("expert", None, None),
        ),
        out_specs=(
            P(("group", "expert", "dp"), None),
            P(("group", "expert"), None, "dp"),
            P(("group", "expert"), None, "dp"),
        ),
        check_vma=False,
    )
```

```python
import functools
import math

import jax
import jax.numpy as jnp
from jax import lax
from jax.experimental import pallas as pl
from jax.experimental.pallas import tpu as pltpu
from jax.sharding import PartitionSpec as P

adapter_scale = 2.0
f32 = jnp.float32
bf16 = jnp.bfloat16
lane_count = 128


def ring_order(count, snake):
    if snake and count % 2 == 0:
        return list(range(0, count, 2)) + list(range(count - 1, 0, -2))
    return list(range(count))


def matmul(a, b):
    return jnp.dot(a, b, preferred_element_type=f32)


def matmul_bt(a, b):
    return lax.dot_general(a, b, (((1,), (1,)), ((), ())), preferred_element_type=f32)


def matmul_at(a, b):
    return lax.dot_general(a, b, (((0,), (0,)), ((), ())), preferred_element_type=f32)


def stacked(piece_refs, span):
    return jnp.concatenate([ref[:, span] for ref in piece_refs], axis=0)


class Plan:
    def __init__(self, parts, depth, model_width, hidden_width, rank, experts):
        self.parts = parts
        self.depth = depth
        self.model_width = model_width
        self.hidden_width = hidden_width
        self.rank = rank
        self.experts = experts
        self.wide = experts * hidden_width
        self.ranks = experts * rank
        self.cuts = 4 if depth % 64 == 0 else 1

    def spans(self):
        if self.parts == 1:
            return [slice(0, self.model_width)]
        core = lax.axis_index("dp")
        return [
            pl.ds(pl.multiple_of(at * self.depth, self.depth), self.depth) for at in (core, 1 - core)
        ]

    def forward(self, token_refs, factor_in_ref, weight_refs):
        gate_pre, up_pre = 0.0, 0.0
        for span, weight in zip(self.spans(), weight_refs):
            tokens_in = stacked(token_refs, span)
            gate_pre += matmul(tokens_in, weight[:, : self.wide])
            up_pre += matmul(tokens_in, weight[:, self.wide : 2 * self.wide])
        logistic = 1.0 / (1.0 + jnp.exp(-gate_pre))
        activation = gate_pre * logistic
        derivative = logistic * (1.0 + gate_pre * (1.0 - logistic))
        hidden = (activation * up_pre).astype(bf16)
        low_rank = matmul_bt(hidden, factor_in_ref[...])
        return activation, up_pre * derivative, hidden, low_rank

    def scales(self, token_refs):
        columns = stacked(token_refs, slice(self.model_width, None)).astype(f32)
        lane = lax.broadcasted_iota(jnp.int32, columns.shape, 1)
        first = lax.axis_index("expert") * self.experts
        return [
            jnp.sum(jnp.where(lane == first + j, columns, 0.0), axis=1, keepdims=True)
            for j in range(self.experts)
        ]

    def spread(self, scales, width):
        rows = scales[0].shape[0]
        at = lax.broadcasted_iota(jnp.int32, (rows, self.experts * width), 1)
        out = jnp.broadcast_to(scales[0], at.shape)
        for j in range(1, self.experts):
            out = jnp.where(at >= j * width, scales[j], out)
        return out

    def backward(
        self, token_refs, grad_refs, activation, slope, factor_in_ref, factor_out_ref, weight_refs, turned_refs, rows_ref
    ):
        scales = self.scales(token_refs)
        adapter_back, grad_down = 0.0, 0.0
        spans = self.spans()
        for span, weight in zip(spans, weight_refs):
            grad_in = stacked(grad_refs, span)
            adapter_back += matmul_bt(grad_in, factor_out_ref[:, span])
            grad_down += matmul(grad_in, weight[:, 2 * self.wide :])
        adapter_back = adapter_back.astype(bf16)
        grad_hidden = self.spread(scales, self.hidden_width) * (
            grad_down + adapter_scale * matmul(adapter_back, factor_in_ref[...])
        )
        grad_gate = (grad_hidden * slope).astype(bf16)
        grad_up = (grad_hidden * activation).astype(bf16)
        for span, weight, turned in zip(spans, weight_refs, turned_refs or weight_refs):
            if turned_refs:
                rows_ref[:, span] = matmul(grad_gate, turned[: self.wide, :]) + matmul(
                    grad_up, turned[self.wide :, :]
                )
            else:
                rows_ref[:, span] = matmul_bt(grad_gate, weight[:, : self.wide]) + matmul_bt(
                    grad_up, weight[:, self.wide : 2 * self.wide]
                )
        rank_scale = self.spread(scales, self.rank)
        return rank_scale, (rank_scale * adapter_back.astype(f32)).astype(bf16)

    def adapters(self, grad_refs, hidden, low_scaled, back_scaled, total_refs, out_refs):
        grad_all = stacked(grad_refs, slice(0, self.model_width))
        for total, out, value in zip(
            total_refs, out_refs, (matmul_at(back_scaled, hidden), matmul_at(low_scaled, grad_all))
        ):
            out[...] = total[...] + adapter_scale * value


def whole_kernel(plan, pieces, blocks, keep_rows, is_turned, *refs):
    token_refs, grad_refs, refs = refs[:pieces], refs[pieces : 2 * pieces], refs[2 * pieces :]
    factor_in_ref, factor_out_ref, refs = refs[0], refs[1], refs[2:]
    weight_refs, refs = refs[: plan.parts], refs[plan.parts :]
    turned_refs = refs[: plan.parts] if is_turned else ()
    refs = refs[len(turned_refs) :]
    total_refs, refs = refs[:2], refs[2:]
    if keep_rows:
        rows_ref, refs = refs[0], refs[1:]
    else:
        *refs, rows_ref = refs
    out_refs, send_refs = refs[:2], refs[2:]
    activation, slope, hidden, low_rank = plan.forward(token_refs, factor_in_ref, weight_refs)
    rank_scale, back_scaled = plan.backward(
        token_refs, grad_refs, activation, slope, factor_in_ref, factor_out_ref, weight_refs, turned_refs, rows_ref
    )
    for (first_row, span), send_ref in zip(blocks, send_refs):
        send_ref[...] = rows_ref[first_row : first_row + send_ref.shape[0], span].astype(bf16)
    low_scaled = (rank_scale * low_rank).astype(bf16)
    plan.adapters(grad_refs, hidden, low_scaled, back_scaled, total_refs, out_refs)


def prepare_kernel(plan, *refs):
    raw_refs, refs = refs[:3], refs[3:]
    out_grad_ref, ids_ref, route_ref, factor_ref = refs[:4]
    tokens_ref, refs = refs[4], refs[5:]
    packed_ref, grads_ref, tokens_held_ref, factor_in_ref, ids_held, route_held, sems = refs
    width, rank, cuts = plan.hidden_width, plan.rank, plan.cuts
    pairs = [(ids_ref, ids_held), (route_ref, route_held)]
    pairs.append((out_grad_ref, grads_ref))
    pairs.append((tokens_ref, tokens_held_ref.at[:, : plan.model_width]))
    for kind in range(3):
        for expert in range(plan.experts):
            at = kind * plan.wide + expert * width
            for cut in range(cuts):
                rows = slice(cut * plan.depth // cuts, (cut + 1) * plan.depth // cuts)
                source = raw_refs[kind].at[expert, rows, :]
                pairs.append((source, packed_ref.at[rows, at : at + width]))
    for expert in range(plan.experts):
        block = factor_in_ref.at[
            expert * rank : (expert + 1) * rank, expert * width : (expert + 1) * width
        ]
        pairs.append((factor_ref.at[expert], block))
    copies = [
        pltpu.make_async_copy(source, target, sems.at[at])
        for at, (source, target) in enumerate(pairs)
    ]
    for copy in copies:
        copy.start()
    for expert in range(plan.experts):
        for other in range(plan.experts):
            if other != expert:
                factor_in_ref[
                    expert * rank : (expert + 1) * rank, other * width : (other + 1) * width
                ] = jnp.zeros((rank, width), bf16)
    copies[0].wait()
    copies[1].wait()
    rows, lanes = grads_ref.shape[0], tokens_held_ref.shape[1] - plan.model_width
    expert_at = lax.broadcasted_iota(jnp.int32, (lanes, rows), 0)
    ids, route = ids_held[...], route_held[...].astype(f32)
    dense = jnp.zeros((lanes, rows), f32)
    for k in range(ids.shape[0]):
        dense = jnp.where(ids[k : k + 1, :] == expert_at, route[k : k + 1, :], dense)
    dense = dense.T.astype(bf16)
    tokens_held_ref[:, plan.model_width :] = dense
    for copy in copies[2:]:
        copy.wait()


def add_kernel(blocks, skip, *refs):
    rows_ref, refs = refs[0], list(refs[1:])
    skipped_ref = refs.pop(len(blocks)) if skip else None
    for at, (first_row, span, taken, way) in enumerate(blocks):
        out = refs[len(blocks) + at]
        rows = rows_ref[first_row : first_row + out.shape[0], span]
        total = rows + refs[at][:, taken].astype(f32)
        if skip:
            here = skip[0]() == (way == "ahead")
            total = total + jnp.where(here, skipped_ref[:, skip[1]].astype(f32), 0.0)
        out[...] = total.astype(bf16)


def add_sums(rows, row_count, blocks, arrived, skip):
    operands = [rows, *arrived]
    return pl.pallas_call(
        functools.partial(add_kernel, blocks, skip),
        out_shape=tuple(
            jax.ShapeDtypeStruct((row_count, len(range(*span.indices(rows.shape[1])))), bf16)
            for _, span, _, _ in blocks
        ),
        in_specs=[pl.BlockSpec(memory_space=pltpu.VMEM)] * len(operands),
        out_specs=(pl.BlockSpec(memory_space=pltpu.VMEM),) * len(blocks),
        compiler_params=pltpu.CompilerParams(vmem_limit_bytes=16 * 1024 * 1024),
    )(*operands)


def turn_kernel(plan, *refs):
    for weight_ref, turned_ref in zip(refs, refs[plan.parts :]):
        step = math.gcd(2 * plan.wide, 256)
        for at in range(0, 2 * plan.wide, step):
            turned_ref[at : at + step, :] = weight_ref[:, at : at + step].T


def half_rows_kernel(half, first_ref, second_ref, top_ref, bottom_ref):
    top_ref[...] = first_ref[:half]
    bottom_ref[...] = second_ref[half:]


def halves(first, second, half):
    out = ((half, first.shape[1]), first.dtype)
    return simple_call(functools.partial(half_rows_kernel, half), [first, second], [out, out])


def halves_kernel(plan, total_in_ref, total_out_ref, keep_ref, send_ref):
    first = lax.axis_index("dp") == 0
    middle, narrow = plan.model_width // 2, plan.hidden_width // 2
    low, high = total_out_ref[:, :middle], total_out_ref[:, middle:]
    keep_ref[:, :middle] = jnp.where(first, low, high)
    send_ref[:, :middle] = jnp.where(first, high, low)
    for expert in range(plan.experts):
        rows = slice(expert * plan.rank, (expert + 1) * plan.rank)
        block = total_in_ref[rows, expert * plan.hidden_width : (expert + 1) * plan.hidden_width]
        low, high = block[:, :narrow], block[:, narrow:]
        keep_ref[rows, middle:] = jnp.where(first, low, high)
        send_ref[rows, middle:] = jnp.where(first, high, low)


def joined_kernel(plan, keep_ref, other_ref, in_ref, out_ref):
    middle = plan.model_width // 2
    for expert in range(plan.experts):
        rows = slice(expert * plan.rank, (expert + 1) * plan.rank)
        out_ref[expert] = keep_ref[rows, :middle] + other_ref[rows, :middle]
        in_ref[expert] = keep_ref[rows, middle:] + other_ref[rows, middle:]


def last_kernel(first_row, spans, *refs):
    rows_ref, out_ref = refs[0], refs[-1]
    for at, span in enumerate(spans):
        total = rows_ref[first_row : first_row + out_ref.shape[0], span]
        for incoming in refs[1 + 2 * at : 3 + 2 * at]:
            total = total + incoming[...].astype(f32)
        out_ref[:, span] = total.astype(bf16)


def simple_call(kernel, operands, outs):
    return pl.pallas_call(
        kernel,
        out_shape=tuple(jax.ShapeDtypeStruct(shape, dtype) for shape, dtype in outs),
        in_specs=[pl.BlockSpec(memory_space=pltpu.VMEM)] * len(operands),
        out_specs=(pl.BlockSpec(memory_space=pltpu.VMEM),) * len(outs),
        compiler_params=pltpu.CompilerParams(vmem_limit_bytes=16 * 1024 * 1024),
    )(*operands)


def expert_call(plan, pieces, blocks, block_rows, operands, totals, keep_rows, is_turned):
    rows = sum(piece[0].shape[0] for piece in pieces)
    operands = [p[0] for p in pieces] + [p[1] for p in pieces] + [*operands, *totals]
    shape = (rows, plan.model_width)
    outs = [(shape, f32)] * keep_rows + [(total.shape, f32) for total in totals]
    widths = [len(range(*span.indices(plan.model_width))) for _, span in blocks]
    outs += [((block_rows, width), bf16) for width in widths]
    return pl.pallas_call(
        functools.partial(whole_kernel, plan, len(pieces), blocks, keep_rows, is_turned),
        scratch_shapes=[] if keep_rows else [pltpu.VMEM(shape, f32)],
        out_shape=tuple(jax.ShapeDtypeStruct(shape, dtype) for shape, dtype in outs),
        in_specs=[pl.BlockSpec(memory_space=pltpu.VMEM)] * len(operands),
        out_specs=(pl.BlockSpec(memory_space=pltpu.VMEM),) * len(outs),
        compiler_params=pltpu.CompilerParams(vmem_limit_bytes=16 * 1024 * 1024),
        cost_estimate=pl.CostEstimate(
            flops=10 * rows * plan.model_width * plan.wide,
            bytes_accessed=sum(op.size * op.dtype.itemsize for op in operands),
            transcendentals=0,
        ),
    )(*operands)


def per_device(
    snake,
    tokens,
    out_grad,
    expert_ids,
    route_weight,
    gate_weight,
    up_weight,
    down_weight,
    adapter_in,
    adapter_out,
):
    peer_count = lax.axis_size("expert")
    dp_count = lax.axis_size("dp")
    token_count, model_width = tokens.shape
    local_count, depth, hidden_width = gate_weight.shape
    rank = adapter_in.shape[1]
    expert_total = local_count * peer_count
    order = ring_order(peer_count, snake)
    forward = [(order[i], order[(i + 1) % peer_count]) for i in range(peer_count)]
    backward = [(b, a) for a, b in forward]
    swap = [(0, 1), (1, 0)]
    parts = 2 if dp_count == 2 else 1
    plan = Plan(parts, depth, model_width, hidden_width, rank, local_count)
    wide, ranks = plan.wide, plan.ranks

    lanes = -(-expert_total // lane_count) * lane_count
    mine, grads, tokens_held, factor_in = pl.pallas_call(
        functools.partial(prepare_kernel, plan),
        out_shape=(
            jax.ShapeDtypeStruct((depth, 3 * wide), bf16),
            jax.ShapeDtypeStruct((token_count, model_width), bf16),
            jax.ShapeDtypeStruct((token_count, model_width + lanes), bf16),
            jax.ShapeDtypeStruct((ranks, wide), bf16),
        ),
        in_specs=[pl.BlockSpec(memory_space=pltpu.HBM)] * 8,
        out_specs=(pl.BlockSpec(memory_space=pltpu.VMEM),) * 4,
        scratch_shapes=[
            pltpu.VMEM(expert_ids.shape[::-1], jnp.int32),
            pltpu.VMEM(route_weight.shape[::-1], bf16),
            pltpu.SemaphoreType.DMA((4 + (3 * plan.cuts + 1) * local_count,)),
        ],
        compiler_params=pltpu.CompilerParams(vmem_limit_bytes=16 * 1024 * 1024),
    )(
        *(
            pltpu.with_memory_space_constraint(x, pltpu.HBM)
            for x in (
                gate_weight,
                up_weight,
                down_weight,
                out_grad,
                expert_ids.T,
                route_weight.T,
                adapter_in,
                tokens,
            )
        )
    )
    if parts == 2:
        weights = [mine, lax.ppermute(mine, "dp", swap)]
    else:
        weights = [lax.all_gather(mine, "dp", axis=0, tiled=True)]
    weights = [pltpu.with_memory_space_constraint(w, pltpu.VMEM) for w in weights]
    factor_out = adapter_out.reshape(ranks, model_width)

    full = (peer_count - 1) // 2
    split = peer_count % 2 == 0
    totals = (jnp.zeros((ranks, wide), f32), jnp.zeros((ranks, model_width), f32))
    behind, ahead = [(tokens_held, grads)], [(tokens_held, grads)]
    rows_at = [None]

    middle = model_width // 2
    columns = {"left": slice(0, middle), "right": slice(middle, model_width)}
    everything = slice(0, model_width)
    ways = {"back": (0, backward), "ahead": (token_count, forward)}
    moving = {}

    def send(value, way):
        return lax.ppermute(value, "expert", ways[way][1])

    def run(pieces, blocks, totals, keep_rows=True, turned=()):
        operands = [factor_in, factor_out, *weights, *turned]
        return expert_call(
            plan, pieces, blocks, token_count, operands, totals, keep_rows, bool(turned)
        )

    def after(value, *arrays):
        held = []
        for x in arrays:
            x, value = lax.optimization_barrier((x, value))
            held.append(x)
        return value, held

    for d in range(full):
        if d > 1:
            totals, (tokens_b, tokens_a) = after(totals, behind[d][0], ahead[d][0])
            grads_b, grads_a = behind[d][1], ahead[d][1]
            behind[d], ahead[d] = (tokens_b, grads_b), (tokens_a, grads_a)
        behind.append(tuple(lax.ppermute(x, "expert", forward) for x in behind[d]))
        ahead.append(tuple(lax.ppermute(x, "expert", backward) for x in ahead[d]))
        if d > 0:
            pieces = [behind[d], ahead[d]] + ([behind[0]] if d == 1 else [])
            rows_d, *totals = run(pieces, [], totals)
            rows_at.append(rows_d)
    turned = simple_call(
        functools.partial(turn_kernel, plan),
        weights,
        [((2 * wide, w.shape[0]), bf16) for w in weights],
    )
    if split:
        half = token_count // 2
        totals, (tokens_b, tokens_a) = after(totals, behind[full][0], ahead[full][0])
        (grads_b,) = after(turned[0], behind[full][1])[1]
        (grads_a,) = after(turned[0], ahead[full][1])[1]
        tokens_b, tokens_a = halves(tokens_b, tokens_a, half)
        grads_b, grads_a = halves(grads_b, grads_a, half)
        far = [
            tuple(lax.ppermute(x, "expert", forward) for x in (tokens_b, grads_b)),
            tuple(lax.ppermute(x, "expert", backward) for x in (tokens_a, grads_a)),
        ]
    pieces = [behind[full], ahead[full]]
    blocks = [(first_row, everything) for first_row, _ in ways.values()]
    outs = run(pieces, blocks, totals, keep_rows=False, turned=turned)
    totals = outs[:2]
    for way, value in zip(ways, outs[2:]):
        for side in columns:
            moving[side, way] = send(value, way) if side == "left" else moving["left", way]
    skipped = []
    if split:
        blocks = [(0, span) for span in columns.values()]
        outs = run(far, blocks, totals, keep_rows=False, turned=turned)
        totals = outs[:2]
        pairs = [
            (order[i], order[(i + (full if i % 2 == 0 else -full)) % peer_count])
            for i in range(peer_count)
        ]
        skipped = [lax.ppermute(value, "expert", pairs) for value in outs[2:]]

    def goes_ahead():
        me = lax.axis_index("expert")
        place = jnp.where(me % 2 == 0, me // 2, peer_count - 1 - me // 2) if snake else me
        return (place + full) % 2 == 0

    for d in range(full - 1, 0, -1):
        for at, (side, span) in enumerate(columns.items()):
            blocks, arrived = [], []
            for way, (first_row, _) in ways.items():
                blocks.append((first_row, span, span if d == full - 1 else slice(0, middle), way))
                arrived.append(moving[side, way])
            skip = (goes_ahead, slice(0, middle)) if d == 1 and split else None
            values = add_sums(
                rows_at[d], token_count, blocks, arrived + (skipped[at : at + 1] if skip else []), skip
            )
            for way, value in zip(ways, values):
                moving[side, way] = send(value, way)
    grad_tokens = pl.pallas_call(
        functools.partial(last_kernel, 2 * token_count, list(columns.values())),
        out_shape=jax.ShapeDtypeStruct((token_count, model_width), bf16),
        in_specs=[pl.BlockSpec(memory_space=pltpu.VMEM)] * 5,
        out_specs=pl.BlockSpec(memory_space=pltpu.VMEM),
        compiler_params=pltpu.CompilerParams(vmem_limit_bytes=16 * 1024 * 1024),
    )(rows_at[1], *(moving[side, way] for side in columns for way in ways))

    narrow = hidden_width // dp_count
    if dp_count == 2:
        half = ((ranks, middle + narrow), f32)
        keep, other = simple_call(functools.partial(halves_kernel, plan), totals, [half, half])
        grad_in_all, grad_out_all = simple_call(
            functools.partial(joined_kernel, plan),
            [keep, lax.ppermute(other, "dp", swap)],
            [((local_count, rank, narrow), f32), ((local_count, rank, middle), f32)],
        )
        return (grad_tokens, grad_in_all, grad_out_all)
    grad_in = jnp.stack(
        [
            totals[0][j * rank : (j + 1) * rank, j * hidden_width : (j + 1) * hidden_width]
            for j in range(local_count)
        ]
    )
    both = jnp.concatenate(
        [
            grad_in.reshape(ranks, dp_count, narrow),
            totals[1].reshape(ranks, dp_count, model_width // dp_count),
        ],
        axis=2,
    ).transpose(1, 0, 2)
    summed = lax.psum_scatter(both, "dp", scatter_dimension=0, tiled=False)
    grad_in_all = summed[:, :narrow].reshape(local_count, rank, narrow)
    grad_out_all = summed[:, narrow:].reshape(local_count, rank, model_width // dp_count)
    return (grad_tokens, grad_in_all, grad_out_all)


def solution(mesh):
    snake = mesh.shape["dp"] == 2
    return jax.shard_map(
        functools.partial(per_device, snake),
        mesh=mesh,
        in_specs=(
            P(("group", "expert", "dp"), None),
            P(("group", "expert", "dp"), None),
            P(("group", "expert", "dp"), None),
            P(("group", "expert", "dp"), None),
            P("expert", "dp", None),
            P("expert", "dp", None),
            P("expert", "dp", None),
            P("expert", None, None),
            P("expert", None, None),
        ),
        out_specs=(
            P(("group", "expert", "dp"), None),
            P(("group", "expert"), None, "dp"),
            P(("group", "expert"), None, "dp"),
        ),
        check_vma=False,
    )
```

```python
import functools
import math

import jax
import jax.numpy as jnp
from jax import lax
from jax.experimental import pallas as pl
from jax.experimental.pallas import tpu as pltpu
from jax.sharding import PartitionSpec as P

adapter_scale = 2.0
f32 = jnp.float32
bf16 = jnp.bfloat16
lane_count = 128


def ring_order(count, snake):
    if snake and count % 2 == 0:
        return list(range(0, count, 2)) + list(range(count - 1, 0, -2))
    return list(range(count))


def matmul(a, b):
    return jnp.dot(a, b, preferred_element_type=f32)


def matmul_bt(a, b):
    return lax.dot_general(a, b, (((1,), (1,)), ((), ())), preferred_element_type=f32)


def matmul_at(a, b):
    return lax.dot_general(a, b, (((0,), (0,)), ((), ())), preferred_element_type=f32)


def stacked(piece_refs, span):
    return jnp.concatenate([ref[:, span] for ref in piece_refs], axis=0)


class Plan:
    def __init__(self, parts, depth, model_width, hidden_width, rank, experts):
        self.parts = parts
        self.depth = depth
        self.model_width = model_width
        self.hidden_width = hidden_width
        self.rank = rank
        self.experts = experts
        self.wide = experts * hidden_width
        self.ranks = experts * rank
        self.cuts = 4 if depth % 64 == 0 else 1

    def spans(self):
        if self.parts == 1:
            return [slice(0, self.model_width)]
        core = lax.axis_index("dp")
        return [
            pl.ds(pl.multiple_of(at * self.depth, self.depth), self.depth) for at in (core, 1 - core)
        ]

    def forward(self, token_refs, factor_in_ref, weight_refs):
        gate_pre, up_pre = 0.0, 0.0
        for span, weight in zip(self.spans(), weight_refs):
            tokens_in = stacked(token_refs, span)
            gate_pre += matmul(tokens_in, weight[:, : self.wide])
            up_pre += matmul(tokens_in, weight[:, self.wide : 2 * self.wide])
        logistic = 1.0 / (1.0 + jnp.exp(-gate_pre))
        activation = gate_pre * logistic
        derivative = logistic * (1.0 + gate_pre * (1.0 - logistic))
        hidden = (activation * up_pre).astype(bf16)
        low_rank = matmul_bt(hidden, factor_in_ref[...])
        return activation, up_pre * derivative, hidden, low_rank

    def scales(self, token_refs):
        columns = stacked(token_refs, slice(self.model_width, None)).astype(f32)
        lane = lax.broadcasted_iota(jnp.int32, columns.shape, 1)
        first = lax.axis_index("expert") * self.experts
        return [
            jnp.sum(jnp.where(lane == first + j, columns, 0.0), axis=1, keepdims=True)
            for j in range(self.experts)
        ]

    def spread(self, scales, width):
        rows = scales[0].shape[0]
        at = lax.broadcasted_iota(jnp.int32, (rows, self.experts * width), 1)
        out = jnp.broadcast_to(scales[0], at.shape)
        for j in range(1, self.experts):
            out = jnp.where(at >= j * width, scales[j], out)
        return out

    def backward(
        self, token_refs, grad_refs, activation, slope, factor_in_ref, factor_out_ref, weight_refs, turned_refs, rows_ref
    ):
        scales = self.scales(token_refs)
        adapter_back, grad_down = 0.0, 0.0
        spans = self.spans()
        for span, weight in zip(spans, weight_refs):
            grad_in = stacked(grad_refs, span)
            adapter_back += matmul_bt(grad_in, factor_out_ref[:, span])
            grad_down += matmul(grad_in, weight[:, 2 * self.wide :])
        adapter_back = adapter_back.astype(bf16)
        grad_hidden = self.spread(scales, self.hidden_width) * (
            grad_down + adapter_scale * matmul(adapter_back, factor_in_ref[...])
        )
        grad_gate = (grad_hidden * slope).astype(bf16)
        grad_up = (grad_hidden * activation).astype(bf16)
        for span, weight, turned in zip(spans, weight_refs, turned_refs or weight_refs):
            if turned_refs:
                rows_ref[:, span] = matmul(grad_gate, turned[: self.wide, :]) + matmul(
                    grad_up, turned[self.wide :, :]
                )
            else:
                rows_ref[:, span] = matmul_bt(grad_gate, weight[:, : self.wide]) + matmul_bt(
                    grad_up, weight[:, self.wide : 2 * self.wide]
                )
        rank_scale = self.spread(scales, self.rank)
        return rank_scale, (rank_scale * adapter_back.astype(f32)).astype(bf16)

    def adapters(self, grad_refs, hidden, low_scaled, back_scaled, total_refs, out_refs):
        grad_all = stacked(grad_refs, slice(0, self.model_width))
        for total, out, value in zip(
            total_refs, out_refs, (matmul_at(back_scaled, hidden), matmul_at(low_scaled, grad_all))
        ):
            out[...] = total[...] + adapter_scale * value


def whole_kernel(plan, pieces, blocks, keep_rows, is_turned, *refs):
    token_refs, grad_refs, refs = refs[:pieces], refs[pieces : 2 * pieces], refs[2 * pieces :]
    factor_in_ref, factor_out_ref, refs = refs[0], refs[1], refs[2:]
    weight_refs, refs = refs[: plan.parts], refs[plan.parts :]
    turned_refs = refs[: plan.parts] if is_turned else ()
    refs = refs[len(turned_refs) :]
    total_refs, refs = refs[:2], refs[2:]
    if keep_rows:
        rows_ref, refs = refs[0], refs[1:]
    else:
        *refs, rows_ref = refs
    out_refs, send_refs = refs[:2], refs[2:]
    activation, slope, hidden, low_rank = plan.forward(token_refs, factor_in_ref, weight_refs)
    rank_scale, back_scaled = plan.backward(
        token_refs, grad_refs, activation, slope, factor_in_ref, factor_out_ref, weight_refs, turned_refs, rows_ref
    )
    for (first_row, span), send_ref in zip(blocks, send_refs):
        send_ref[...] = rows_ref[first_row : first_row + send_ref.shape[0], span].astype(bf16)
    low_scaled = (rank_scale * low_rank).astype(bf16)
    plan.adapters(grad_refs, hidden, low_scaled, back_scaled, total_refs, out_refs)


def prepare_kernel(plan, *refs):
    raw_refs, refs = refs[:3], refs[3:]
    out_grad_ref, ids_ref, route_ref, factor_ref = refs[:4]
    tokens_ref, refs = refs[4], refs[5:]
    packed_ref, grads_ref, tokens_held_ref, factor_in_ref, ids_held, sems = refs
    width, rank, cuts = plan.hidden_width, plan.rank, plan.cuts
    pairs = [(ids_ref, ids_held)]
    pairs.append((out_grad_ref, grads_ref))
    pairs.append((tokens_ref, tokens_held_ref.at[:, : plan.model_width]))
    for kind in range(3):
        for expert in range(plan.experts):
            at = kind * plan.wide + expert * width
            for cut in range(cuts):
                rows = slice(cut * plan.depth // cuts, (cut + 1) * plan.depth // cuts)
                source = raw_refs[kind].at[expert, rows, :]
                pairs.append((source, packed_ref.at[rows, at : at + width]))
    for expert in range(plan.experts):
        block = factor_in_ref.at[
            expert * rank : (expert + 1) * rank, expert * width : (expert + 1) * width
        ]
        pairs.append((factor_ref.at[expert], block))
    copies = [
        pltpu.make_async_copy(source, target, sems.at[at])
        for at, (source, target) in enumerate(pairs)
    ]
    for copy in copies:
        copy.start()
    for expert in range(plan.experts):
        for other in range(plan.experts):
            if other != expert:
                factor_in_ref[
                    expert * rank : (expert + 1) * rank, other * width : (other + 1) * width
                ] = jnp.zeros((rank, width), bf16)
    copies[0].wait()
    rows, lanes = grads_ref.shape[0], tokens_held_ref.shape[1] - plan.model_width
    expert_at = lax.broadcasted_iota(jnp.int32, (lanes, rows), 0)
    ids, route = ids_held[...], route_ref[...]
    dense = jnp.zeros((lanes, rows), f32)
    for k in range(ids.shape[0]):
        dense = jnp.where(ids[k : k + 1, :] == expert_at, route[k : k + 1, :], dense)
    dense = dense.T.astype(bf16)
    tokens_held_ref[:, plan.model_width :] = dense
    for copy in copies[1:]:
        copy.wait()


def add_kernel(blocks, skip, *refs):
    rows_ref, refs = refs[0], list(refs[1:])
    skipped_ref = refs.pop(len(blocks)) if skip else None
    for at, (first_row, span, taken, way) in enumerate(blocks):
        out = refs[len(blocks) + at]
        rows = rows_ref[first_row : first_row + out.shape[0], span]
        total = rows + refs[at][:, taken].astype(f32)
        if skip:
            here = skip[0]() == (way == "ahead")
            total = total + jnp.where(here, skipped_ref[:, skip[1]].astype(f32), 0.0)
        out[...] = total.astype(bf16)


def add_sums(rows, row_count, blocks, arrived, skip):
    operands = [rows, *arrived]
    return pl.pallas_call(
        functools.partial(add_kernel, blocks, skip),
        out_shape=tuple(
            jax.ShapeDtypeStruct((row_count, len(range(*span.indices(rows.shape[1])))), bf16)
            for _, span, _, _ in blocks
        ),
        in_specs=[pl.BlockSpec(memory_space=pltpu.VMEM)] * len(operands),
        out_specs=(pl.BlockSpec(memory_space=pltpu.VMEM),) * len(blocks),
        compiler_params=pltpu.CompilerParams(vmem_limit_bytes=16 * 1024 * 1024),
    )(*operands)


def turn_kernel(plan, *refs):
    for weight_ref, turned_ref in zip(refs, refs[plan.parts :]):
        step = math.gcd(2 * plan.wide, 256)
        for at in range(0, 2 * plan.wide, step):
            turned_ref[at : at + step, :] = weight_ref[:, at : at + step].T


def half_rows_kernel(half, first_ref, second_ref, top_ref, bottom_ref):
    top_ref[...] = first_ref[:half]
    bottom_ref[...] = second_ref[half:]


def halves(first, second, half):
    out = ((half, first.shape[1]), first.dtype)
    return simple_call(functools.partial(half_rows_kernel, half), [first, second], [out, out])


def halves_kernel(plan, total_in_ref, total_out_ref, keep_ref, send_ref):
    first = lax.axis_index("dp") == 0
    middle, narrow = plan.model_width // 2, plan.hidden_width // 2
    low, high = total_out_ref[:, :middle], total_out_ref[:, middle:]
    keep_ref[:, :middle] = jnp.where(first, low, high)
    send_ref[:, :middle] = jnp.where(first, high, low)
    for expert in range(plan.experts):
        rows = slice(expert * plan.rank, (expert + 1) * plan.rank)
        block = total_in_ref[rows, expert * plan.hidden_width : (expert + 1) * plan.hidden_width]
        low, high = block[:, :narrow], block[:, narrow:]
        keep_ref[rows, middle:] = jnp.where(first, low, high)
        send_ref[rows, middle:] = jnp.where(first, high, low)


def joined_kernel(plan, keep_ref, other_ref, in_ref, out_ref):
    middle = plan.model_width // 2
    for expert in range(plan.experts):
        rows = slice(expert * plan.rank, (expert + 1) * plan.rank)
        out_ref[expert] = keep_ref[rows, :middle] + other_ref[rows, :middle]
        in_ref[expert] = keep_ref[rows, middle:] + other_ref[rows, middle:]


def last_kernel(first_row, spans, *refs):
    rows_ref, out_ref = refs[0], refs[-1]
    for at, span in enumerate(spans):
        total = rows_ref[first_row : first_row + out_ref.shape[0], span]
        for incoming in refs[1 + 2 * at : 3 + 2 * at]:
            total = total + incoming[...].astype(f32)
        out_ref[:, span] = total.astype(bf16)


def simple_call(kernel, operands, outs):
    return pl.pallas_call(
        kernel,
        out_shape=tuple(jax.ShapeDtypeStruct(shape, dtype) for shape, dtype in outs),
        in_specs=[pl.BlockSpec(memory_space=pltpu.VMEM)] * len(operands),
        out_specs=(pl.BlockSpec(memory_space=pltpu.VMEM),) * len(outs),
        compiler_params=pltpu.CompilerParams(vmem_limit_bytes=16 * 1024 * 1024),
    )(*operands)


def expert_call(plan, pieces, blocks, block_rows, operands, totals, keep_rows, is_turned):
    rows = sum(piece[0].shape[0] for piece in pieces)
    operands = [p[0] for p in pieces] + [p[1] for p in pieces] + [*operands, *totals]
    shape = (rows, plan.model_width)
    outs = [(shape, f32)] * keep_rows + [(total.shape, f32) for total in totals]
    widths = [len(range(*span.indices(plan.model_width))) for _, span in blocks]
    outs += [((block_rows, width), bf16) for width in widths]
    return pl.pallas_call(
        functools.partial(whole_kernel, plan, len(pieces), blocks, keep_rows, is_turned),
        scratch_shapes=[] if keep_rows else [pltpu.VMEM(shape, f32)],
        out_shape=tuple(jax.ShapeDtypeStruct(shape, dtype) for shape, dtype in outs),
        in_specs=[pl.BlockSpec(memory_space=pltpu.VMEM)] * len(operands),
        out_specs=(pl.BlockSpec(memory_space=pltpu.VMEM),) * len(outs),
        compiler_params=pltpu.CompilerParams(vmem_limit_bytes=16 * 1024 * 1024),
        cost_estimate=pl.CostEstimate(
            flops=10 * rows * plan.model_width * plan.wide,
            bytes_accessed=sum(op.size * op.dtype.itemsize for op in operands),
            transcendentals=0,
        ),
    )(*operands)


def in_hbm(*arrays):
    return [pltpu.with_memory_space_constraint(x, pltpu.HBM) for x in arrays]


def per_device(
    snake,
    tokens,
    out_grad,
    expert_ids,
    route_weight,
    gate_weight,
    up_weight,
    down_weight,
    adapter_in,
    adapter_out,
):
    peer_count = lax.axis_size("expert")
    dp_count = lax.axis_size("dp")
    token_count, model_width = tokens.shape
    local_count, depth, hidden_width = gate_weight.shape
    rank = adapter_in.shape[1]
    expert_total = local_count * peer_count
    order = ring_order(peer_count, snake)
    forward = [(order[i], order[(i + 1) % peer_count]) for i in range(peer_count)]
    backward = [(b, a) for a, b in forward]
    swap = [(0, 1), (1, 0)]
    parts = 2 if dp_count == 2 else 1
    plan = Plan(parts, depth, model_width, hidden_width, rank, local_count)
    wide, ranks = plan.wide, plan.ranks

    lanes = -(-expert_total // lane_count) * lane_count
    mine, grads, tokens_held, factor_in = pl.pallas_call(
        functools.partial(prepare_kernel, plan),
        out_shape=(
            jax.ShapeDtypeStruct((depth, 3 * wide), bf16),
            jax.ShapeDtypeStruct((token_count, model_width), bf16),
            jax.ShapeDtypeStruct((token_count, model_width + lanes), bf16),
            jax.ShapeDtypeStruct((ranks, wide), bf16),
        ),
        in_specs=[pl.BlockSpec(memory_space=pltpu.HBM)] * 5
        + [pl.BlockSpec(memory_space=pltpu.VMEM)]
        + [pl.BlockSpec(memory_space=pltpu.HBM)] * 2,
        out_specs=(pl.BlockSpec(memory_space=pltpu.VMEM),) * 4,
        scratch_shapes=[
            pltpu.VMEM(expert_ids.shape[::-1], jnp.int32),
            pltpu.SemaphoreType.DMA((3 + (3 * plan.cuts + 1) * local_count,)),
        ],
        compiler_params=pltpu.CompilerParams(vmem_limit_bytes=16 * 1024 * 1024),
    )(
        *in_hbm(gate_weight, up_weight, down_weight, out_grad, expert_ids.T),
        route_weight.T.astype(f32),
        *in_hbm(adapter_in, tokens),
    )
    if parts == 2:
        weights = [mine, lax.ppermute(mine, "dp", swap)]
    else:
        weights = [lax.all_gather(mine, "dp", axis=0, tiled=True)]
    weights = [pltpu.with_memory_space_constraint(w, pltpu.VMEM) for w in weights]
    factor_out = adapter_out.reshape(ranks, model_width)

    full = (peer_count - 1) // 2
    split = peer_count % 2 == 0
    totals = (jnp.zeros((ranks, wide), f32), jnp.zeros((ranks, model_width), f32))
    behind, ahead = [(tokens_held, grads)], [(tokens_held, grads)]
    rows_at = [None]

    middle = model_width // 2
    columns = {"left": slice(0, middle), "right": slice(middle, model_width)}
    everything = slice(0, model_width)
    ways = {"back": (0, backward), "ahead": (token_count, forward)}
    moving = {}

    def send(value, way):
        return lax.ppermute(value, "expert", ways[way][1])

    def run(pieces, blocks, totals, keep_rows=True, turned=()):
        operands = [factor_in, factor_out, *weights, *turned]
        return expert_call(
            plan, pieces, blocks, token_count, operands, totals, keep_rows, bool(turned)
        )

    def after(value, *arrays):
        held = []
        for x in arrays:
            x, value = lax.optimization_barrier((x, value))
            held.append(x)
        return value, held

    for d in range(full):
        if d > 1:
            totals, (tokens_b, tokens_a) = after(totals, behind[d][0], ahead[d][0])
            grads_b, grads_a = behind[d][1], ahead[d][1]
            behind[d], ahead[d] = (tokens_b, grads_b), (tokens_a, grads_a)
        behind.append(tuple(lax.ppermute(x, "expert", forward) for x in behind[d]))
        ahead.append(tuple(lax.ppermute(x, "expert", backward) for x in ahead[d]))
        if d > 0:
            pieces = [behind[d], ahead[d]] + ([behind[0]] if d == 1 else [])
            rows_d, *totals = run(pieces, [], totals)
            rows_at.append(rows_d)
    turned = simple_call(
        functools.partial(turn_kernel, plan),
        weights,
        [((2 * wide, w.shape[0]), bf16) for w in weights],
    )
    if split:
        half = token_count // 2
        totals, (tokens_b, tokens_a) = after(totals, behind[full][0], ahead[full][0])
        (grads_b,) = after(turned[0], behind[full][1])[1]
        (grads_a,) = after(turned[0], ahead[full][1])[1]
        tokens_b, tokens_a = halves(tokens_b, tokens_a, half)
        grads_b, grads_a = halves(grads_b, grads_a, half)
        far = [
            tuple(lax.ppermute(x, "expert", forward) for x in (tokens_b, grads_b)),
            tuple(lax.ppermute(x, "expert", backward) for x in (tokens_a, grads_a)),
        ]
    pieces = [behind[full], ahead[full]]
    blocks = [(first_row, everything) for first_row, _ in ways.values()]
    outs = run(pieces, blocks, totals, keep_rows=False, turned=turned)
    totals = outs[:2]
    for way, value in zip(ways, outs[2:]):
        for side in columns:
            moving[side, way] = send(value, way) if side == "left" else moving["left", way]
    skipped = []
    if split:
        blocks = [(0, span) for span in columns.values()]
        outs = run(far, blocks, totals, keep_rows=False, turned=turned)
        totals = outs[:2]
        pairs = [
            (order[i], order[(i + (full if i % 2 == 0 else -full)) % peer_count])
            for i in range(peer_count)
        ]
        skipped = [lax.ppermute(value, "expert", pairs) for value in outs[2:]]

    def goes_ahead():
        me = lax.axis_index("expert")
        place = jnp.where(me % 2 == 0, me // 2, peer_count - 1 - me // 2) if snake else me
        return (place + full) % 2 == 0

    for d in range(full - 1, 0, -1):
        for at, (side, span) in enumerate(columns.items()):
            blocks, arrived = [], []
            for way, (first_row, _) in ways.items():
                blocks.append((first_row, span, span if d == full - 1 else slice(0, middle), way))
                arrived.append(moving[side, way])
            skip = (goes_ahead, slice(0, middle)) if d == 1 and split else None
            values = add_sums(
                rows_at[d], token_count, blocks, arrived + (skipped[at : at + 1] if skip else []), skip
            )
            for way, value in zip(ways, values):
                moving[side, way] = send(value, way)
    grad_tokens = pl.pallas_call(
        functools.partial(last_kernel, 2 * token_count, list(columns.values())),
        out_shape=jax.ShapeDtypeStruct((token_count, model_width), bf16),
        in_specs=[pl.BlockSpec(memory_space=pltpu.VMEM)] * 5,
        out_specs=pl.BlockSpec(memory_space=pltpu.VMEM),
        compiler_params=pltpu.CompilerParams(vmem_limit_bytes=16 * 1024 * 1024),
    )(rows_at[1], *(moving[side, way] for side in columns for way in ways))

    narrow = hidden_width // dp_count
    if dp_count == 2:
        half = ((ranks, middle + narrow), f32)
        keep, other = simple_call(functools.partial(halves_kernel, plan), totals, [half, half])
        grad_in_all, grad_out_all = simple_call(
            functools.partial(joined_kernel, plan),
            [keep, lax.ppermute(other, "dp", swap)],
            [((local_count, rank, narrow), f32), ((local_count, rank, middle), f32)],
        )
        return (grad_tokens, grad_in_all, grad_out_all)
    grad_in = jnp.stack(
        [
            totals[0][j * rank : (j + 1) * rank, j * hidden_width : (j + 1) * hidden_width]
            for j in range(local_count)
        ]
    )
    both = jnp.concatenate(
        [
            grad_in.reshape(ranks, dp_count, narrow),
            totals[1].reshape(ranks, dp_count, model_width // dp_count),
        ],
        axis=2,
    ).transpose(1, 0, 2)
    summed = lax.psum_scatter(both, "dp", scatter_dimension=0, tiled=False)
    grad_in_all = summed[:, :narrow].reshape(local_count, rank, narrow)
    grad_out_all = summed[:, narrow:].reshape(local_count, rank, model_width // dp_count)
    return (grad_tokens, grad_in_all, grad_out_all)


def solution(mesh):
    snake = mesh.shape["dp"] == 2
    return jax.shard_map(
        functools.partial(per_device, snake),
        mesh=mesh,
        in_specs=(
            P(("group", "expert", "dp"), None),
            P(("group", "expert", "dp"), None),
            P(("group", "expert", "dp"), None),
            P(("group", "expert", "dp"), None),
            P("expert", "dp", None),
            P("expert", "dp", None),
            P("expert", "dp", None),
            P("expert", None, None),
            P("expert", None, None),
        ),
        out_specs=(
            P(("group", "expert", "dp"), None),
            P(("group", "expert"), None, "dp"),
            P(("group", "expert"), None, "dp"),
        ),
        check_vma=False,
    )
```

```python
import functools
import math

import jax
import jax.numpy as jnp
from jax import lax
from jax.experimental import pallas as pl
from jax.experimental.pallas import tpu as pltpu
from jax.sharding import PartitionSpec as P

adapter_scale = 2.0
f32 = jnp.float32
bf16 = jnp.bfloat16
lane_count = 128


def ring_order(count, snake):
    if snake and count % 2 == 0:
        return list(range(0, count, 2)) + list(range(count - 1, 0, -2))
    return list(range(count))


def matmul(a, b):
    return jnp.dot(a, b, preferred_element_type=f32)


def matmul_bt(a, b):
    return lax.dot_general(a, b, (((1,), (1,)), ((), ())), preferred_element_type=f32)


def matmul_at(a, b):
    return lax.dot_general(a, b, (((0,), (0,)), ((), ())), preferred_element_type=f32)


def stacked(piece_refs, span):
    return jnp.concatenate([ref[:, span] for ref in piece_refs], axis=0)


class Plan:
    def __init__(self, parts, depth, model_width, hidden_width, rank, experts):
        self.parts = parts
        self.depth = depth
        self.model_width = model_width
        self.hidden_width = hidden_width
        self.rank = rank
        self.experts = experts
        self.wide = experts * hidden_width
        self.ranks = experts * rank
        self.cuts = 4 if depth % 64 == 0 else 1

    def spans(self):
        if self.parts == 1:
            return [slice(0, self.model_width)]
        core = lax.axis_index("dp")
        return [
            pl.ds(pl.multiple_of(at * self.depth, self.depth), self.depth) for at in (core, 1 - core)
        ]

    def forward(self, token_refs, factor_in_ref, weight_refs):
        gate_pre, up_pre = 0.0, 0.0
        for span, weight in zip(self.spans(), weight_refs):
            tokens_in = stacked(token_refs, span)
            gate_pre += matmul(tokens_in, weight[:, : self.wide])
            up_pre += matmul(tokens_in, weight[:, self.wide : 2 * self.wide])
        logistic = 1.0 / (1.0 + jnp.exp(-gate_pre))
        activation = gate_pre * logistic
        derivative = logistic * (1.0 + gate_pre * (1.0 - logistic))
        hidden = (activation * up_pre).astype(bf16)
        low_rank = matmul_bt(hidden, factor_in_ref[...])
        return activation, up_pre * derivative, hidden, low_rank

    def scales(self, token_refs):
        columns = stacked(token_refs, slice(self.model_width, None)).astype(f32)
        lane = lax.broadcasted_iota(jnp.int32, columns.shape, 1)
        first = lax.axis_index("expert") * self.experts
        return [
            jnp.sum(jnp.where(lane == first + j, columns, 0.0), axis=1, keepdims=True)
            for j in range(self.experts)
        ]

    def spread(self, scales, width):
        rows = scales[0].shape[0]
        at = lax.broadcasted_iota(jnp.int32, (rows, self.experts * width), 1)
        out = jnp.broadcast_to(scales[0], at.shape)
        for j in range(1, self.experts):
            out = jnp.where(at >= j * width, scales[j], out)
        return out

    def backward(
        self, token_refs, grad_refs, activation, slope, factor_in_ref, factor_out_ref, weight_refs, turned_refs, rows_ref
    ):
        scales = self.scales(token_refs)
        adapter_back, grad_down = 0.0, 0.0
        spans = self.spans()
        for span, weight in zip(spans, weight_refs):
            grad_in = stacked(grad_refs, span)
            adapter_back += matmul_bt(grad_in, factor_out_ref[:, span])
            grad_down += matmul(grad_in, weight[:, 2 * self.wide :])
        adapter_back = adapter_back.astype(bf16)
        grad_hidden = self.spread(scales, self.hidden_width) * (
            grad_down + adapter_scale * matmul(adapter_back, factor_in_ref[...])
        )
        grad_gate = (grad_hidden * slope).astype(bf16)
        grad_up = (grad_hidden * activation).astype(bf16)
        for span, weight, turned in zip(spans, weight_refs, turned_refs or weight_refs):
            if turned_refs:
                rows_ref[:, span] = matmul(grad_gate, turned[: self.wide, :]) + matmul(
                    grad_up, turned[self.wide :, :]
                )
            else:
                rows_ref[:, span] = matmul_bt(grad_gate, weight[:, : self.wide]) + matmul_bt(
                    grad_up, weight[:, self.wide : 2 * self.wide]
                )
        rank_scale = self.spread(scales, self.rank)
        return rank_scale, (rank_scale * adapter_back.astype(f32)).astype(bf16)

    def adapters(self, grad_refs, hidden, low_scaled, back_scaled, total_refs, out_refs):
        grad_all = stacked(grad_refs, slice(0, self.model_width))
        for total, out, value in zip(
            total_refs, out_refs, (matmul_at(back_scaled, hidden), matmul_at(low_scaled, grad_all))
        ):
            out[...] = total[...] + adapter_scale * value


def whole_kernel(plan, pieces, blocks, keep_rows, is_turned, *refs):
    token_refs, grad_refs, refs = refs[:pieces], refs[pieces : 2 * pieces], refs[2 * pieces :]
    factor_in_ref, factor_out_ref, refs = refs[0], refs[1], refs[2:]
    weight_refs, refs = refs[: plan.parts], refs[plan.parts :]
    turned_refs = refs[: plan.parts] if is_turned else ()
    refs = refs[len(turned_refs) :]
    total_refs, refs = refs[:2], refs[2:]
    if keep_rows:
        rows_ref, refs = refs[0], refs[1:]
    else:
        *refs, rows_ref = refs
    out_refs, send_refs = refs[:2], refs[2:]
    activation, slope, hidden, low_rank = plan.forward(token_refs, factor_in_ref, weight_refs)
    rank_scale, back_scaled = plan.backward(
        token_refs, grad_refs, activation, slope, factor_in_ref, factor_out_ref, weight_refs, turned_refs, rows_ref
    )
    for (first_row, span), send_ref in zip(blocks, send_refs):
        send_ref[...] = rows_ref[first_row : first_row + send_ref.shape[0], span].astype(bf16)
    low_scaled = (rank_scale * low_rank).astype(bf16)
    plan.adapters(grad_refs, hidden, low_scaled, back_scaled, total_refs, out_refs)


def prepare_kernel(plan, *refs):
    raw_refs, factor_ref, packed_ref, factor_in_ref, sems = refs[:3], *refs[3:]
    width, rank, cuts = plan.hidden_width, plan.rank, plan.cuts
    pairs = []
    for kind in range(3):
        for expert in range(plan.experts):
            at = kind * plan.wide + expert * width
            for cut in range(cuts):
                rows = slice(cut * plan.depth // cuts, (cut + 1) * plan.depth // cuts)
                source = raw_refs[kind].at[expert, rows, :]
                pairs.append((source, packed_ref.at[rows, at : at + width]))
    for expert in range(plan.experts):
        block = factor_in_ref.at[
            expert * rank : (expert + 1) * rank, expert * width : (expert + 1) * width
        ]
        pairs.append((factor_ref.at[expert], block))
    copies = [
        pltpu.make_async_copy(source, target, sems.at[at])
        for at, (source, target) in enumerate(pairs)
    ]
    for copy in copies:
        copy.start()
    for expert in range(plan.experts):
        for other in range(plan.experts):
            if other != expert:
                factor_in_ref[
                    expert * rank : (expert + 1) * rank, other * width : (other + 1) * width
                ] = jnp.zeros((rank, width), bf16)
    for copy in copies:
        copy.wait()


def tokens_kernel(plan, tokens_ref, ids_ref, route_ref, held_ref, sem):
    copy = pltpu.make_async_copy(tokens_ref, held_ref.at[:, : plan.model_width], sem)
    copy.start()
    rows, lanes = held_ref.shape[0], held_ref.shape[1] - plan.model_width
    expert_at = lax.broadcasted_iota(jnp.int32, (lanes, rows), 0)
    ids, route = ids_ref[...], route_ref[...].astype(f32)
    dense = jnp.zeros((lanes, rows), f32)
    for k in range(ids.shape[0]):
        dense = jnp.where(ids[k : k + 1, :] == expert_at, route[k : k + 1, :], dense)
    held_ref[:, plan.model_width :] = dense.T.astype(bf16)
    copy.wait()


def add_kernel(blocks, skip, *refs):
    rows_ref, refs = refs[0], list(refs[1:])
    skipped_ref = refs.pop(len(blocks)) if skip else None
    for at, (first_row, span, taken, way) in enumerate(blocks):
        out = refs[len(blocks) + at]
        rows = rows_ref[first_row : first_row + out.shape[0], span]
        total = rows + refs[at][:, taken].astype(f32)
        if skip:
            here = skip[0]() == (way == "ahead")
            total = total + jnp.where(here, skipped_ref[:, skip[1]].astype(f32), 0.0)
        out[...] = total.astype(bf16)


def add_sums(rows, row_count, blocks, arrived, skip):
    operands = [rows, *arrived]
    return pl.pallas_call(
        functools.partial(add_kernel, blocks, skip),
        out_shape=tuple(
            jax.ShapeDtypeStruct((row_count, len(range(*span.indices(rows.shape[1])))), bf16)
            for _, span, _, _ in blocks
        ),
        in_specs=[pl.BlockSpec(memory_space=pltpu.VMEM)] * len(operands),
        out_specs=(pl.BlockSpec(memory_space=pltpu.VMEM),) * len(blocks),
        compiler_params=pltpu.CompilerParams(vmem_limit_bytes=16 * 1024 * 1024),
    )(*operands)


def turn_kernel(plan, *refs):
    for weight_ref, turned_ref in zip(refs, refs[plan.parts :]):
        step = math.gcd(2 * plan.wide, 256)
        for at in range(0, 2 * plan.wide, step):
            turned_ref[at : at + step, :] = weight_ref[:, at : at + step].T


def half_rows_kernel(half, first_ref, second_ref, top_ref, bottom_ref):
    top_ref[...] = first_ref[:half]
    bottom_ref[...] = second_ref[half:]


def halves(first, second, half):
    out = ((half, first.shape[1]), first.dtype)
    return simple_call(functools.partial(half_rows_kernel, half), [first, second], [out, out])


def halves_kernel(plan, total_in_ref, total_out_ref, keep_ref, send_ref):
    first = lax.axis_index("dp") == 0
    middle, narrow = plan.model_width // 2, plan.hidden_width // 2
    low, high = total_out_ref[:, :middle], total_out_ref[:, middle:]
    keep_ref[:, :middle] = jnp.where(first, low, high)
    send_ref[:, :middle] = jnp.where(first, high, low)
    for expert in range(plan.experts):
        rows = slice(expert * plan.rank, (expert + 1) * plan.rank)
        block = total_in_ref[rows, expert * plan.hidden_width : (expert + 1) * plan.hidden_width]
        low, high = block[:, :narrow], block[:, narrow:]
        keep_ref[rows, middle:] = jnp.where(first, low, high)
        send_ref[rows, middle:] = jnp.where(first, high, low)


def joined_kernel(plan, keep_ref, other_ref, in_ref, out_ref):
    middle = plan.model_width // 2
    for expert in range(plan.experts):
        rows = slice(expert * plan.rank, (expert + 1) * plan.rank)
        out_ref[expert] = keep_ref[rows, :middle] + other_ref[rows, :middle]
        in_ref[expert] = keep_ref[rows, middle:] + other_ref[rows, middle:]


def last_kernel(first_row, spans, *refs):
    rows_ref, out_ref = refs[0], refs[-1]
    for at, span in enumerate(spans):
        total = rows_ref[first_row : first_row + out_ref.shape[0], span]
        for incoming in refs[1 + 2 * at : 3 + 2 * at]:
            total = total + incoming[...].astype(f32)
        out_ref[:, span] = total.astype(bf16)


def simple_call(kernel, operands, outs):
    return pl.pallas_call(
        kernel,
        out_shape=tuple(jax.ShapeDtypeStruct(shape, dtype) for shape, dtype in outs),
        in_specs=[pl.BlockSpec(memory_space=pltpu.VMEM)] * len(operands),
        out_specs=(pl.BlockSpec(memory_space=pltpu.VMEM),) * len(outs),
        compiler_params=pltpu.CompilerParams(vmem_limit_bytes=16 * 1024 * 1024),
    )(*operands)


def expert_call(plan, pieces, blocks, block_rows, operands, totals, keep_rows, is_turned):
    rows = sum(piece[0].shape[0] for piece in pieces)
    operands = [p[0] for p in pieces] + [p[1] for p in pieces] + [*operands, *totals]
    shape = (rows, plan.model_width)
    outs = [(shape, f32)] * keep_rows + [(total.shape, f32) for total in totals]
    widths = [len(range(*span.indices(plan.model_width))) for _, span in blocks]
    outs += [((block_rows, width), bf16) for width in widths]
    return pl.pallas_call(
        functools.partial(whole_kernel, plan, len(pieces), blocks, keep_rows, is_turned),
        scratch_shapes=[] if keep_rows else [pltpu.VMEM(shape, f32)],
        out_shape=tuple(jax.ShapeDtypeStruct(shape, dtype) for shape, dtype in outs),
        in_specs=[pl.BlockSpec(memory_space=pltpu.VMEM)] * len(operands),
        out_specs=(pl.BlockSpec(memory_space=pltpu.VMEM),) * len(outs),
        compiler_params=pltpu.CompilerParams(vmem_limit_bytes=16 * 1024 * 1024),
        cost_estimate=pl.CostEstimate(
            flops=10 * rows * plan.model_width * plan.wide,
            bytes_accessed=sum(op.size * op.dtype.itemsize for op in operands),
            transcendentals=0,
        ),
    )(*operands)


def in_hbm(*arrays):
    return [pltpu.with_memory_space_constraint(x, pltpu.HBM) for x in arrays]


def per_device(
    snake,
    tokens,
    out_grad,
    expert_ids,
    route_weight,
    gate_weight,
    up_weight,
    down_weight,
    adapter_in,
    adapter_out,
):
    peer_count = lax.axis_size("expert")
    dp_count = lax.axis_size("dp")
    token_count, model_width = tokens.shape
    local_count, depth, hidden_width = gate_weight.shape
    rank = adapter_in.shape[1]
    expert_total = local_count * peer_count
    order = ring_order(peer_count, snake)
    forward = [(order[i], order[(i + 1) % peer_count]) for i in range(peer_count)]
    backward = [(b, a) for a, b in forward]
    swap = [(0, 1), (1, 0)]
    parts = 2 if dp_count == 2 else 1
    plan = Plan(parts, depth, model_width, hidden_width, rank, local_count)
    wide, ranks = plan.wide, plan.ranks

    lanes = -(-expert_total // lane_count) * lane_count
    mine, factor_in = pl.pallas_call(
        functools.partial(prepare_kernel, plan),
        out_shape=(
            jax.ShapeDtypeStruct((depth, 3 * wide), bf16),
            jax.ShapeDtypeStruct((ranks, wide), bf16),
        ),
        in_specs=[pl.BlockSpec(memory_space=pltpu.HBM)] * 4,
        out_specs=(pl.BlockSpec(memory_space=pltpu.VMEM),) * 2,
        scratch_shapes=[pltpu.SemaphoreType.DMA(((3 * plan.cuts + 1) * local_count,))],
        compiler_params=pltpu.CompilerParams(vmem_limit_bytes=16 * 1024 * 1024),
    )(*in_hbm(gate_weight, up_weight, down_weight, adapter_in))
    tokens_held = pl.pallas_call(
        functools.partial(tokens_kernel, plan),
        out_shape=jax.ShapeDtypeStruct((token_count, model_width + lanes), bf16),
        in_specs=[
            pl.BlockSpec(memory_space=pltpu.HBM),
            pl.BlockSpec(memory_space=pltpu.VMEM),
            pl.BlockSpec(memory_space=pltpu.VMEM),
        ],
        out_specs=pl.BlockSpec(memory_space=pltpu.VMEM),
        scratch_shapes=[pltpu.SemaphoreType.DMA],
        compiler_params=pltpu.CompilerParams(vmem_limit_bytes=16 * 1024 * 1024),
    )(*in_hbm(tokens), expert_ids.T, route_weight.T)
    grads = out_grad
    if parts == 2:
        weights = [mine, lax.ppermute(mine, "dp", swap)]
    else:
        weights = [lax.all_gather(mine, "dp", axis=0, tiled=True)]
    weights = [pltpu.with_memory_space_constraint(w, pltpu.VMEM) for w in weights]
    factor_out = adapter_out.reshape(ranks, model_width)

    full = (peer_count - 1) // 2
    split = peer_count % 2 == 0
    totals = (jnp.zeros((ranks, wide), f32), jnp.zeros((ranks, model_width), f32))
    behind, ahead = [(tokens_held, grads)], [(tokens_held, grads)]
    rows_at = [None]

    middle = model_width // 2
    columns = {"left": slice(0, middle), "right": slice(middle, model_width)}
    everything = slice(0, model_width)
    ways = {"back": (0, backward), "ahead": (token_count, forward)}
    moving = {}

    def send(value, way):
        return lax.ppermute(value, "expert", ways[way][1])

    def run(pieces, blocks, totals, keep_rows=True, turned=()):
        operands = [factor_in, factor_out, *weights, *turned]
        return expert_call(
            plan, pieces, blocks, token_count, operands, totals, keep_rows, bool(turned)
        )

    def after(value, *arrays):
        held = []
        for x in arrays:
            x, value = lax.optimization_barrier((x, value))
            held.append(x)
        return value, held

    for d in range(full):
        if d > 1:
            totals, (tokens_b, tokens_a) = after(totals, behind[d][0], ahead[d][0])
            grads_b, grads_a = behind[d][1], ahead[d][1]
            behind[d], ahead[d] = (tokens_b, grads_b), (tokens_a, grads_a)
        behind.append(tuple(lax.ppermute(x, "expert", forward) for x in behind[d]))
        ahead.append(tuple(lax.ppermute(x, "expert", backward) for x in ahead[d]))
        if d > 0:
            pieces = [behind[d], ahead[d]] + ([behind[0]] if d == 1 else [])
            rows_d, *totals = run(pieces, [], totals)
            rows_at.append(rows_d)
    turned = simple_call(
        functools.partial(turn_kernel, plan),
        weights,
        [((2 * wide, w.shape[0]), bf16) for w in weights],
    )
    if split:
        half = token_count // 2
        totals, (tokens_b, tokens_a) = after(totals, behind[full][0], ahead[full][0])
        (grads_b,) = after(turned[0], behind[full][1])[1]
        (grads_a,) = after(turned[0], ahead[full][1])[1]
        tokens_b, tokens_a = halves(tokens_b, tokens_a, half)
        grads_b, grads_a = halves(grads_b, grads_a, half)
        far = [
            tuple(lax.ppermute(x, "expert", forward) for x in (tokens_b, grads_b)),
            tuple(lax.ppermute(x, "expert", backward) for x in (tokens_a, grads_a)),
        ]
    pieces = [behind[full], ahead[full]]
    blocks = [(first_row, everything) for first_row, _ in ways.values()]
    outs = run(pieces, blocks, totals, keep_rows=False, turned=turned)
    totals = outs[:2]
    for way, value in zip(ways, outs[2:]):
        for side in columns:
            moving[side, way] = send(value, way) if side == "left" else moving["left", way]
    skipped = []
    if split:
        blocks = [(0, span) for span in columns.values()]
        outs = run(far, blocks, totals, keep_rows=False, turned=turned)
        totals = outs[:2]
        pairs = [
            (order[i], order[(i + (full if i % 2 == 0 else -full)) % peer_count])
            for i in range(peer_count)
        ]
        skipped = [lax.ppermute(value, "expert", pairs) for value in outs[2:]]

    def goes_ahead():
        me = lax.axis_index("expert")
        place = jnp.where(me % 2 == 0, me // 2, peer_count - 1 - me // 2) if snake else me
        return (place + full) % 2 == 0

    for d in range(full - 1, 0, -1):
        for at, (side, span) in enumerate(columns.items()):
            blocks, arrived = [], []
            for way, (first_row, _) in ways.items():
                blocks.append((first_row, span, span if d == full - 1 else slice(0, middle), way))
                arrived.append(moving[side, way])
            skip = (goes_ahead, slice(0, middle)) if d == 1 and split else None
            values = add_sums(
                rows_at[d], token_count, blocks, arrived + (skipped[at : at + 1] if skip else []), skip
            )
            for way, value in zip(ways, values):
                moving[side, way] = send(value, way)
    grad_tokens = pl.pallas_call(
        functools.partial(last_kernel, 2 * token_count, list(columns.values())),
        out_shape=jax.ShapeDtypeStruct((token_count, model_width), bf16),
        in_specs=[pl.BlockSpec(memory_space=pltpu.VMEM)] * 5,
        out_specs=pl.BlockSpec(memory_space=pltpu.VMEM),
        compiler_params=pltpu.CompilerParams(vmem_limit_bytes=16 * 1024 * 1024),
    )(rows_at[1], *(moving[side, way] for side in columns for way in ways))

    narrow = hidden_width // dp_count
    if dp_count == 2:
        half = ((ranks, middle + narrow), f32)
        keep, other = simple_call(functools.partial(halves_kernel, plan), totals, [half, half])
        grad_in_all, grad_out_all = simple_call(
            functools.partial(joined_kernel, plan),
            [keep, lax.ppermute(other, "dp", swap)],
            [((local_count, rank, narrow), f32), ((local_count, rank, middle), f32)],
        )
        return (grad_tokens, grad_in_all, grad_out_all)
    grad_in = jnp.stack(
        [
            totals[0][j * rank : (j + 1) * rank, j * hidden_width : (j + 1) * hidden_width]
            for j in range(local_count)
        ]
    )
    both = jnp.concatenate(
        [
            grad_in.reshape(ranks, dp_count, narrow),
            totals[1].reshape(ranks, dp_count, model_width // dp_count),
        ],
        axis=2,
    ).transpose(1, 0, 2)
    summed = lax.psum_scatter(both, "dp", scatter_dimension=0, tiled=False)
    grad_in_all = summed[:, :narrow].reshape(local_count, rank, narrow)
    grad_out_all = summed[:, narrow:].reshape(local_count, rank, model_width // dp_count)
    return (grad_tokens, grad_in_all, grad_out_all)


def solution(mesh):
    snake = mesh.shape["dp"] == 2
    return jax.shard_map(
        functools.partial(per_device, snake),
        mesh=mesh,
        in_specs=(
            P(("group", "expert", "dp"), None),
            P(("group", "expert", "dp"), None),
            P(("group", "expert", "dp"), None),
            P(("group", "expert", "dp"), None),
            P("expert", "dp", None),
            P("expert", "dp", None),
            P("expert", "dp", None),
            P("expert", None, None),
            P("expert", None, None),
        ),
        out_specs=(
            P(("group", "expert", "dp"), None),
            P(("group", "expert"), None, "dp"),
            P(("group", "expert"), None, "dp"),
        ),
        check_vma=False,
    )
```

```python
import functools
import math

import jax
import jax.numpy as jnp
from jax import lax
from jax.experimental import pallas as pl
from jax.experimental.pallas import tpu as pltpu
from jax.sharding import PartitionSpec as P

adapter_scale = 2.0
f32 = jnp.float32
bf16 = jnp.bfloat16
lane_count = 128


def ring_order(count, snake):
    if snake and count % 2 == 0:
        return list(range(0, count, 2)) + list(range(count - 1, 0, -2))
    return list(range(count))


def matmul(a, b):
    return jnp.dot(a, b, preferred_element_type=f32)


def matmul_bt(a, b):
    return lax.dot_general(a, b, (((1,), (1,)), ((), ())), preferred_element_type=f32)


def matmul_at(a, b):
    return lax.dot_general(a, b, (((0,), (0,)), ((), ())), preferred_element_type=f32)


def stacked(piece_refs, span):
    return jnp.concatenate([ref[:, span] for ref in piece_refs], axis=0)


class Plan:
    def __init__(self, parts, depth, model_width, hidden_width, rank, experts):
        self.parts = parts
        self.depth = depth
        self.model_width = model_width
        self.hidden_width = hidden_width
        self.rank = rank
        self.experts = experts
        self.wide = experts * hidden_width
        self.ranks = experts * rank
        self.cuts = 4 if depth % 64 == 0 else 1

    def spans(self):
        if self.parts == 1:
            return [slice(0, self.model_width)]
        core = lax.axis_index("dp")
        return [
            pl.ds(pl.multiple_of(at * self.depth, self.depth), self.depth) for at in (core, 1 - core)
        ]

    def forward(self, token_refs, factor_in_ref, weight_refs):
        gate_pre, up_pre = 0.0, 0.0
        for span, weight in zip(self.spans(), weight_refs):
            tokens_in = stacked(token_refs, span)
            gate_pre += matmul(tokens_in, weight[:, : self.wide])
            up_pre += matmul(tokens_in, weight[:, self.wide : 2 * self.wide])
        logistic = 1.0 / (1.0 + jnp.exp(-gate_pre))
        activation = gate_pre * logistic
        derivative = logistic * (1.0 + gate_pre * (1.0 - logistic))
        hidden = (activation * up_pre).astype(bf16)
        low_rank = matmul_bt(hidden, factor_in_ref[...])
        return activation, up_pre * derivative, hidden, low_rank

    def scales(self, token_refs):
        columns = stacked(token_refs, slice(self.model_width, None)).astype(f32)
        lane = lax.broadcasted_iota(jnp.int32, columns.shape, 1)
        first = lax.axis_index("expert") * self.experts
        return [
            jnp.sum(jnp.where(lane == first + j, columns, 0.0), axis=1, keepdims=True)
            for j in range(self.experts)
        ]

    def spread(self, scales, width):
        rows = scales[0].shape[0]
        at = lax.broadcasted_iota(jnp.int32, (rows, self.experts * width), 1)
        out = jnp.broadcast_to(scales[0], at.shape)
        for j in range(1, self.experts):
            out = jnp.where(at >= j * width, scales[j], out)
        return out

    def backward(
        self, token_refs, grad_refs, activation, slope, factor_in_ref, factor_out_ref, weight_refs, turned_refs, rows_ref
    ):
        scales = self.scales(token_refs)
        adapter_back, grad_down = 0.0, 0.0
        spans = self.spans()
        for span, weight in zip(spans, weight_refs):
            grad_in = stacked(grad_refs, span)
            adapter_back += matmul_bt(grad_in, factor_out_ref[:, span])
            grad_down += matmul(grad_in, weight[:, 2 * self.wide :])
        adapter_back = adapter_back.astype(bf16)
        grad_hidden = self.spread(scales, self.hidden_width) * (
            grad_down + adapter_scale * matmul(adapter_back, factor_in_ref[...])
        )
        grad_gate = (grad_hidden * slope).astype(bf16)
        grad_up = (grad_hidden * activation).astype(bf16)
        for span, weight, turned in zip(spans, weight_refs, turned_refs or weight_refs):
            if turned_refs:
                rows_ref[:, span] = matmul(grad_gate, turned[: self.wide, :]) + matmul(
                    grad_up, turned[self.wide :, :]
                )
            else:
                rows_ref[:, span] = matmul_bt(grad_gate, weight[:, : self.wide]) + matmul_bt(
                    grad_up, weight[:, self.wide : 2 * self.wide]
                )
        rank_scale = self.spread(scales, self.rank)
        return rank_scale, (rank_scale * adapter_back.astype(f32)).astype(bf16)

    def adapters(self, grad_refs, hidden, low_scaled, back_scaled, total_refs, out_refs):
        grad_all = stacked(grad_refs, slice(0, self.model_width))
        for total, out, value in zip(
            total_refs, out_refs, (matmul_at(back_scaled, hidden), matmul_at(low_scaled, grad_all))
        ):
            out[...] = total[...] + adapter_scale * value


def whole_kernel(plan, pieces, blocks, keep_rows, is_turned, *refs):
    token_refs, grad_refs, refs = refs[:pieces], refs[pieces : 2 * pieces], refs[2 * pieces :]
    factor_in_ref, factor_out_ref, refs = refs[0], refs[1], refs[2:]
    weight_refs, refs = refs[: plan.parts], refs[plan.parts :]
    turned_refs = refs[: plan.parts] if is_turned else ()
    refs = refs[len(turned_refs) :]
    total_refs, refs = refs[:2], refs[2:]
    if keep_rows:
        rows_ref, refs = refs[0], refs[1:]
    else:
        *refs, rows_ref = refs
    out_refs, send_refs = refs[:2], refs[2:]
    activation, slope, hidden, low_rank = plan.forward(token_refs, factor_in_ref, weight_refs)
    rank_scale, back_scaled = plan.backward(
        token_refs, grad_refs, activation, slope, factor_in_ref, factor_out_ref, weight_refs, turned_refs, rows_ref
    )
    for (first_row, span), send_ref in zip(blocks, send_refs):
        send_ref[...] = rows_ref[first_row : first_row + send_ref.shape[0], span].astype(bf16)
    low_scaled = (rank_scale * low_rank).astype(bf16)
    plan.adapters(grad_refs, hidden, low_scaled, back_scaled, total_refs, out_refs)


def prepare_kernel(plan, *refs):
    raw_refs, factor_ref, packed_ref, factor_in_ref, sems = refs[:3], *refs[3:]
    width, rank, cuts = plan.hidden_width, plan.rank, plan.cuts
    pairs = []
    for kind in range(3):
        for expert in range(plan.experts):
            at = kind * plan.wide + expert * width
            for cut in range(cuts):
                rows = slice(cut * plan.depth // cuts, (cut + 1) * plan.depth // cuts)
                source = raw_refs[kind].at[expert, rows, :]
                pairs.append((source, packed_ref.at[rows, at : at + width]))
    for expert in range(plan.experts):
        block = factor_in_ref.at[
            expert * rank : (expert + 1) * rank, expert * width : (expert + 1) * width
        ]
        pairs.append((factor_ref.at[expert], block))
    copies = [
        pltpu.make_async_copy(source, target, sems.at[at])
        for at, (source, target) in enumerate(pairs)
    ]
    for copy in copies:
        copy.start()
    for expert in range(plan.experts):
        for other in range(plan.experts):
            if other != expert:
                factor_in_ref[
                    expert * rank : (expert + 1) * rank, other * width : (other + 1) * width
                ] = jnp.zeros((rank, width), bf16)
    for copy in copies:
        copy.wait()


def tokens_kernel(plan, tokens_ref, ids_ref, route_ref, held_ref, sem):
    copy = pltpu.make_async_copy(tokens_ref, held_ref.at[:, : plan.model_width], sem)
    copy.start()
    rows, lanes = held_ref.shape[0], held_ref.shape[1] - plan.model_width
    expert_at = lax.broadcasted_iota(jnp.int32, (lanes, rows), 0)
    ids, route = ids_ref[...], route_ref[...].astype(f32)
    dense = jnp.zeros((lanes, rows), f32)
    for k in range(ids.shape[0]):
        dense = jnp.where(ids[k : k + 1, :] == expert_at, route[k : k + 1, :], dense)
    held_ref[:, plan.model_width :] = dense.T.astype(bf16)
    copy.wait()


def add_kernel(blocks, skip, *refs):
    rows_ref, refs = refs[0], list(refs[1:])
    skipped_ref = refs.pop(len(blocks)) if skip else None
    for at, (first_row, span, taken, way) in enumerate(blocks):
        out = refs[len(blocks) + at]
        rows = rows_ref[first_row : first_row + out.shape[0], span]
        total = rows + refs[at][:, taken].astype(f32)
        if skip:
            here = skip[0]() == (way == "ahead")
            total = total + jnp.where(here, skipped_ref[:, skip[1]].astype(f32), 0.0)
        out[...] = total.astype(bf16)


def add_sums(rows, row_count, blocks, arrived, skip):
    operands = [rows, *arrived]
    return pl.pallas_call(
        functools.partial(add_kernel, blocks, skip),
        out_shape=tuple(
            jax.ShapeDtypeStruct((row_count, len(range(*span.indices(rows.shape[1])))), bf16)
            for _, span, _, _ in blocks
        ),
        in_specs=[pl.BlockSpec(memory_space=pltpu.VMEM)] * len(operands),
        out_specs=(pl.BlockSpec(memory_space=pltpu.VMEM),) * len(blocks),
        compiler_params=pltpu.CompilerParams(vmem_limit_bytes=16 * 1024 * 1024),
    )(*operands)


def turn_kernel(plan, *refs):
    for weight_ref, turned_ref in zip(refs, refs[plan.parts :]):
        step = math.gcd(2 * plan.wide, 256)
        for at in range(0, 2 * plan.wide, step):
            turned_ref[at : at + step, :] = weight_ref[:, at : at + step].T


def half_rows_kernel(half, first_ref, second_ref, top_ref, bottom_ref):
    top_ref[...] = first_ref[:half]
    bottom_ref[...] = second_ref[half:]


def halves(first, second, half):
    out = ((half, first.shape[1]), first.dtype)
    return simple_call(functools.partial(half_rows_kernel, half), [first, second], [out, out])


def halves_kernel(plan, total_in_ref, total_out_ref, keep_ref, send_ref):
    first = lax.axis_index("dp") == 0
    middle, narrow = plan.model_width // 2, plan.hidden_width // 2
    low, high = total_out_ref[:, :middle], total_out_ref[:, middle:]
    keep_ref[:, :middle] = jnp.where(first, low, high)
    send_ref[:, :middle] = jnp.where(first, high, low)
    for expert in range(plan.experts):
        rows = slice(expert * plan.rank, (expert + 1) * plan.rank)
        block = total_in_ref[rows, expert * plan.hidden_width : (expert + 1) * plan.hidden_width]
        low, high = block[:, :narrow], block[:, narrow:]
        keep_ref[rows, middle:] = jnp.where(first, low, high)
        send_ref[rows, middle:] = jnp.where(first, high, low)


def joined_kernel(plan, keep_ref, other_ref, in_ref, out_ref):
    middle = plan.model_width // 2
    for expert in range(plan.experts):
        rows = slice(expert * plan.rank, (expert + 1) * plan.rank)
        out_ref[expert] = keep_ref[rows, :middle] + other_ref[rows, :middle]
        in_ref[expert] = keep_ref[rows, middle:] + other_ref[rows, middle:]


def last_kernel(first_row, spans, *refs):
    rows_ref, out_ref = refs[0], refs[-1]
    for at, span in enumerate(spans):
        total = rows_ref[first_row : first_row + out_ref.shape[0], span]
        for incoming in refs[1 + 2 * at : 3 + 2 * at]:
            total = total + incoming[...].astype(f32)
        out_ref[:, span] = total.astype(bf16)


def simple_call(kernel, operands, outs):
    return pl.pallas_call(
        kernel,
        out_shape=tuple(jax.ShapeDtypeStruct(shape, dtype) for shape, dtype in outs),
        in_specs=[pl.BlockSpec(memory_space=pltpu.VMEM)] * len(operands),
        out_specs=(pl.BlockSpec(memory_space=pltpu.VMEM),) * len(outs),
        compiler_params=pltpu.CompilerParams(vmem_limit_bytes=16 * 1024 * 1024),
    )(*operands)


def expert_call(plan, pieces, blocks, block_rows, operands, totals, keep_rows, is_turned):
    rows = sum(piece[0].shape[0] for piece in pieces)
    operands = [p[0] for p in pieces] + [p[1] for p in pieces] + [*operands, *totals]
    shape = (rows, plan.model_width)
    outs = [(shape, f32)] * keep_rows + [(total.shape, f32) for total in totals]
    widths = [len(range(*span.indices(plan.model_width))) for _, span in blocks]
    outs += [((block_rows, width), bf16) for width in widths]
    return pl.pallas_call(
        functools.partial(whole_kernel, plan, len(pieces), blocks, keep_rows, is_turned),
        scratch_shapes=[] if keep_rows else [pltpu.VMEM(shape, f32)],
        out_shape=tuple(jax.ShapeDtypeStruct(shape, dtype) for shape, dtype in outs),
        in_specs=[pl.BlockSpec(memory_space=pltpu.VMEM)] * len(operands),
        out_specs=(pl.BlockSpec(memory_space=pltpu.VMEM),) * len(outs),
        compiler_params=pltpu.CompilerParams(vmem_limit_bytes=16 * 1024 * 1024),
        cost_estimate=pl.CostEstimate(
            flops=10 * rows * plan.model_width * plan.wide,
            bytes_accessed=sum(op.size * op.dtype.itemsize for op in operands),
            transcendentals=0,
        ),
    )(*operands)


def in_hbm(*arrays):
    return [pltpu.with_memory_space_constraint(x, pltpu.HBM) for x in arrays]


def per_device(
    snake,
    tokens,
    out_grad,
    expert_ids,
    route_weight,
    gate_weight,
    up_weight,
    down_weight,
    adapter_in,
    adapter_out,
):
    peer_count = lax.axis_size("expert")
    dp_count = lax.axis_size("dp")
    token_count, model_width = tokens.shape
    local_count, depth, hidden_width = gate_weight.shape
    rank = adapter_in.shape[1]
    expert_total = local_count * peer_count
    order = ring_order(peer_count, snake)
    forward = [(order[i], order[(i + 1) % peer_count]) for i in range(peer_count)]
    backward = [(b, a) for a, b in forward]
    swap = [(0, 1), (1, 0)]
    parts = 2 if dp_count == 2 else 1
    plan = Plan(parts, depth, model_width, hidden_width, rank, local_count)
    wide, ranks = plan.wide, plan.ranks

    lanes = -(-expert_total // lane_count) * lane_count
    mine, factor_in = pl.pallas_call(
        functools.partial(prepare_kernel, plan),
        out_shape=(
            jax.ShapeDtypeStruct((depth, 3 * wide), bf16),
            jax.ShapeDtypeStruct((ranks, wide), bf16),
        ),
        in_specs=[pl.BlockSpec(memory_space=pltpu.HBM)] * 4,
        out_specs=(pl.BlockSpec(memory_space=pltpu.VMEM),) * 2,
        scratch_shapes=[pltpu.SemaphoreType.DMA(((3 * plan.cuts + 1) * local_count,))],
        compiler_params=pltpu.CompilerParams(vmem_limit_bytes=16 * 1024 * 1024),
    )(*in_hbm(gate_weight, up_weight, down_weight, adapter_in))
    tokens_held = pl.pallas_call(
        functools.partial(tokens_kernel, plan),
        out_shape=jax.ShapeDtypeStruct((token_count, model_width + lanes), bf16),
        in_specs=[
            pl.BlockSpec(memory_space=pltpu.HBM),
            pl.BlockSpec(memory_space=pltpu.VMEM),
            pl.BlockSpec(memory_space=pltpu.VMEM),
        ],
        out_specs=pl.BlockSpec(memory_space=pltpu.VMEM),
        scratch_shapes=[pltpu.SemaphoreType.DMA],
        compiler_params=pltpu.CompilerParams(vmem_limit_bytes=16 * 1024 * 1024),
    )(*in_hbm(tokens), expert_ids.T, route_weight.T)
    grads = out_grad
    if parts == 2:
        weights = [mine, lax.ppermute(mine, "dp", swap)]
    else:
        weights = [lax.all_gather(mine, "dp", axis=0, tiled=True)]
    weights = [pltpu.with_memory_space_constraint(w, pltpu.VMEM) for w in weights]
    factor_out = adapter_out.reshape(ranks, model_width)

    full = (peer_count - 1) // 2
    split = peer_count % 2 == 0
    totals = (jnp.zeros((ranks, wide), f32), jnp.zeros((ranks, model_width), f32))
    behind, ahead = [(tokens_held, grads)], [(tokens_held, grads)]
    rows_at = [None]

    middle = model_width // 2
    columns = {"left": slice(0, middle), "right": slice(middle, model_width)}
    everything = slice(0, model_width)
    ways = {"back": (0, backward), "ahead": (token_count, forward)}
    moving = {}

    def send(value, way):
        return lax.ppermute(value, "expert", ways[way][1])

    def run(pieces, blocks, totals, keep_rows=True, turned=()):
        operands = [factor_in, factor_out, *weights, *turned]
        return expert_call(
            plan, pieces, blocks, token_count, operands, totals, keep_rows, bool(turned)
        )

    def after(value, *arrays):
        held = []
        for x in arrays:
            x, value = lax.optimization_barrier((x, value))
            held.append(x)
        return value, held

    turned = simple_call(
        functools.partial(turn_kernel, plan),
        weights,
        [((2 * wide, w.shape[0]), bf16) for w in weights],
    )
    for d in range(full):
        if d > 1:
            totals, (tokens_b, tokens_a) = after(totals, behind[d][0], ahead[d][0])
            grads_b, grads_a = behind[d][1], ahead[d][1]
            behind[d], ahead[d] = (tokens_b, grads_b), (tokens_a, grads_a)
        behind.append(tuple(lax.ppermute(x, "expert", forward) for x in behind[d]))
        ahead.append(tuple(lax.ppermute(x, "expert", backward) for x in ahead[d]))
        if d > 0:
            pieces = [behind[d], ahead[d]] + ([behind[0]] if d == full - 1 else [])
            rows_d, *totals = run(pieces, [], totals, turned=turned if d == full - 1 else ())
            rows_at.append(rows_d)
    if split:
        half = token_count // 2
        totals, (tokens_b, tokens_a) = after(totals, behind[full][0], ahead[full][0])
        (grads_b,) = after(turned[0], behind[full][1])[1]
        (grads_a,) = after(turned[0], ahead[full][1])[1]
        tokens_b, tokens_a = halves(tokens_b, tokens_a, half)
        grads_b, grads_a = halves(grads_b, grads_a, half)
        far = [
            tuple(lax.ppermute(x, "expert", forward) for x in (tokens_b, grads_b)),
            tuple(lax.ppermute(x, "expert", backward) for x in (tokens_a, grads_a)),
        ]
    pieces = [behind[full], ahead[full]]
    blocks = [(first_row, everything) for first_row, _ in ways.values()]
    outs = run(pieces, blocks, totals, keep_rows=False, turned=turned)
    totals = outs[:2]
    for way, value in zip(ways, outs[2:]):
        for side in columns:
            moving[side, way] = send(value, way) if side == "left" else moving["left", way]
    skipped = []
    if split:
        blocks = [(0, span) for span in columns.values()]
        outs = run(far, blocks, totals, keep_rows=False, turned=turned)
        totals = outs[:2]
        pairs = [
            (order[i], order[(i + (full if i % 2 == 0 else -full)) % peer_count])
            for i in range(peer_count)
        ]
        skipped = [lax.ppermute(value, "expert", pairs) for value in outs[2:]]

    def goes_ahead():
        me = lax.axis_index("expert")
        place = jnp.where(me % 2 == 0, me // 2, peer_count - 1 - me // 2) if snake else me
        return (place + full) % 2 == 0

    for d in range(full - 1, 0, -1):
        for at, (side, span) in enumerate(columns.items()):
            blocks, arrived = [], []
            for way, (first_row, _) in ways.items():
                blocks.append((first_row, span, span if d == full - 1 else slice(0, middle), way))
                arrived.append(moving[side, way])
            skip = (goes_ahead, slice(0, middle)) if d == 1 and split else None
            values = add_sums(
                rows_at[d], token_count, blocks, arrived + (skipped[at : at + 1] if skip else []), skip
            )
            for way, value in zip(ways, values):
                moving[side, way] = send(value, way)
    grad_tokens = pl.pallas_call(
        functools.partial(last_kernel, 2 * token_count, list(columns.values())),
        out_shape=jax.ShapeDtypeStruct((token_count, model_width), bf16),
        in_specs=[pl.BlockSpec(memory_space=pltpu.VMEM)] * 5,
        out_specs=pl.BlockSpec(memory_space=pltpu.VMEM),
        compiler_params=pltpu.CompilerParams(vmem_limit_bytes=16 * 1024 * 1024),
    )(rows_at[full - 1], *(moving[side, way] for side in columns for way in ways))

    narrow = hidden_width // dp_count
    if dp_count == 2:
        half = ((ranks, middle + narrow), f32)
        keep, other = simple_call(functools.partial(halves_kernel, plan), totals, [half, half])
        grad_in_all, grad_out_all = simple_call(
            functools.partial(joined_kernel, plan),
            [keep, lax.ppermute(other, "dp", swap)],
            [((local_count, rank, narrow), f32), ((local_count, rank, middle), f32)],
        )
        return (grad_tokens, grad_in_all, grad_out_all)
    grad_in = jnp.stack(
        [
            totals[0][j * rank : (j + 1) * rank, j * hidden_width : (j + 1) * hidden_width]
            for j in range(local_count)
        ]
    )
    both = jnp.concatenate(
        [
            grad_in.reshape(ranks, dp_count, narrow),
            totals[1].reshape(ranks, dp_count, model_width // dp_count),
        ],
        axis=2,
    ).transpose(1, 0, 2)
    summed = lax.psum_scatter(both, "dp", scatter_dimension=0, tiled=False)
    grad_in_all = summed[:, :narrow].reshape(local_count, rank, narrow)
    grad_out_all = summed[:, narrow:].reshape(local_count, rank, model_width // dp_count)
    return (grad_tokens, grad_in_all, grad_out_all)


def solution(mesh):
    snake = mesh.shape["dp"] == 2
    return jax.shard_map(
        functools.partial(per_device, snake),
        mesh=mesh,
        in_specs=(
            P(("group", "expert", "dp"), None),
            P(("group", "expert", "dp"), None),
            P(("group", "expert", "dp"), None),
            P(("group", "expert", "dp"), None),
            P("expert", "dp", None),
            P("expert", "dp", None),
            P("expert", "dp", None),
            P("expert", None, None),
            P("expert", None, None),
        ),
        out_specs=(
            P(("group", "expert", "dp"), None),
            P(("group", "expert"), None, "dp"),
            P(("group", "expert"), None, "dp"),
        ),
        check_vma=False,
    )
```
